32 devices in a mesh: blk: 8 (over z, core), dx: 2 (over y), dy: 2 (over x).
Axes of the slice: x: 2, y: 2, z: 4, core: 2. Of those that a mesh axis runs over, the one named last changes fastest.
Arguments:
- orbitals: bfloat16 [1024, 8, 16, 128], P('blk', 'dx', 'dy'), may hold values from -6 to 6
- coupling: float32 [8, 16, 128], P('dx', 'dy'), may hold values from 0.3 to 3
- pot_grad: float32 [3, 8, 16, 128], P(None, 'dx', 'dy'), may hold values from -6 to 6
Outputs:
- spin_orbit: float32 [3, 5, 1024, 128], P(None, None, ('blk', 'dx', 'dy'))
The draws below stay inside these ranges and needn't reach their ends.
All inputs are finite; a program needn't handle non-finite values.
Results may differ from the reference program's by a relative error of at most 0.0029.
Values may be sent and summed in bfloat16 or wider, within the bound.
No kernel may reach another device: no remote copies, remote signals or barrier semaphores. Data moves between devices by JAX's collectives and lax.ppermute only.
A program may use at most 64 MiB of HBM per device.

```python
import math
import jax
import jax.numpy as jnp
from jax import lax

P_SIZE = 128
HALF = 2
NSTATES = 1024
NX = 8
NY = 16
NZ = 128
N_BLK = 8


def steps_of(rng, dims, pieces, low, largest):
    loudness, own = 1.0, jax.random.fold_in(rng, 6)
    for position, parts in pieces:
        steps = jnp.exp(jax.random.uniform(jax.random.fold_in(own, position), (parts,), jnp.float32, low / len(pieces), largest / len(pieces)))
        loudness = loudness * jnp.repeat(steps, dims[position] // parts).reshape([-1 if axis == position else 1 for axis in range(len(dims))])
    return loudness


def scatter_about(own_key, extent, width, bound, cuts=(), held_as=jnp.bfloat16):
    gain = steps_of(own_key, extent, cuts, -0.22, 0.18) if cuts else 1.0
    drawn = jax.random.normal(own_key, extent, jnp.float32) * width * gain
    return jnp.minimum(jnp.maximum(drawn, -bound), bound).astype(held_as)


def setup_inputs(seed: int = 0) -> dict:
    streams_of = jax.random.split(jax.random.key(seed), 4)
    orbitals = scatter_about(streams_of[0], (NSTATES, NX, NY, NZ), 1.0, 6.0, ((0, 8), (1, 2), (2, 2)))
    coupling = jnp.clip(jnp.exp(math.log(3.0) - 2.3025851 * jax.random.uniform(streams_of[1], (NX, NY, NZ), jnp.float32) ** steps_of(streams_of[1], (NX, NY, NZ), ((0, 2), (1, 2)), -0.2, 0.2)), 0.3, 3.0)
    pot_grad = scatter_about(streams_of[2], (3, NX, NY, NZ), 1.0, 6.0, ((1, 2), (2, 2)), jnp.float32)
    return {"orbitals": orbitals, "coupling": coupling, "pot_grad": pot_grad}


def reference(orbitals, coupling, pot_grad):
    cell_count = NX * NY * NZ
    weight_scale = 1.0 / math.sqrt(cell_count)
    coeff_field = coupling[None] * pot_grad
    coeff_one, coeff_two, coeff_three = (coeff_field[0], coeff_field[1], coeff_field[2])
    flat = orbitals.reshape(N_BLK, P_SIZE, cell_count)

    def one_panel(b):
        panel = lax.dynamic_index_in_dim(flat, b, 0, keepdims=False)
        field_f32 = panel.reshape(P_SIZE, NX, NY, NZ).astype(jnp.float32)
        gradient = [0.5 * (jnp.roll(field_f32, -1, axis=a) - jnp.roll(field_f32, 1, axis=a)) for a in (1, 2, 3)]
        cross_one = coeff_two * gradient[2] - coeff_three * gradient[1]
        cross_two = coeff_three * gradient[0] - coeff_one * gradient[2]
        cross_three = coeff_one * gradient[1] - coeff_two * gradient[0]
        cross_field = jnp.stack([cross_one, cross_two, cross_three]).astype(jnp.bfloat16)
        cross_field = cross_field.reshape(3, P_SIZE, cell_count).astype(jnp.float32)
        tile_list = []
        for t in range(2 * HALF + 1):
            other_index = ((b + t - HALF) % N_BLK).astype(jnp.int32)
            other = lax.dynamic_index_in_dim(flat, other_index, 0, keepdims=False).astype(jnp.float32)
            tile_list.append(jnp.einsum('kjc,ic->kji', cross_field, other))
        return jnp.stack(tile_list, 1) * weight_scale
    every_panel = lax.map(one_panel, jnp.arange(N_BLK, dtype=jnp.int32))
    return every_panel.transpose(1, 2, 0, 3, 4).reshape(3, 2 * HALF + 1, N_BLK * P_SIZE, P_SIZE)
```

```python
import math

import jax
import jax.numpy as jnp
from jax import lax
from jax.sharding import PartitionSpec as P

AXES = ("blk", "dx", "dy")


def shift(block, axis, distance):
    count = lax.axis_size(axis)
    return lax.ppermute(block, axis, [((i + distance) % count, i) for i in range(count)])


def edges(cells, axis, dim):
    count = lax.axis_size(axis)
    size = cells.shape[dim]
    head = lax.slice_in_dim(cells, 0, 1, axis=dim)
    tail = lax.slice_in_dim(cells, size - 1, size, axis=dim)
    if count == 2:
        both = shift(jnp.concatenate([tail, head], axis=dim), axis, 1)
        return lax.slice_in_dim(both, 0, 1, axis=dim), lax.slice_in_dim(both, 1, 2, axis=dim)
    return shift(tail, axis, -1), shift(head, axis, 1)


def neighbours(cells, axis, dim):
    before, after = edges(cells, axis, dim)
    size = cells.shape[dim]
    prev = jnp.concatenate([before, lax.slice_in_dim(cells, 0, size - 1, axis=dim)], axis=dim)
    nxt = jnp.concatenate([lax.slice_in_dim(cells, 1, size, axis=dim), after], axis=dim)
    return prev, nxt


def plane_sum(parts):
    nx, ny = lax.axis_size("dx"), lax.axis_size("dy")
    x, y = lax.axis_index("dx"), lax.axis_index("dy")
    total = lax.dynamic_index_in_dim(parts, x * ny + y, 0, keepdims=False)
    for ox in range(nx):
        for oy in range(ny):
            if ox == 0 and oy == 0:
                continue
            dest = ((x + ox) % nx) * ny + (y + oy) % ny
            piece = lax.dynamic_index_in_dim(parts, dest, 0, keepdims=False)
            route = [
                (i * ny + j, ((i + ox) % nx) * ny + (j + oy) % ny) for i in range(nx) for j in range(ny)
            ]
            total = total + lax.ppermute(piece, ("dx", "dy"), route)
    return total


def on_device(orbitals, coupling, pot_grad):
    states, wx, wy, wz = orbitals.shape
    plane = lax.axis_size("dx") * lax.axis_size("dy")
    rows = states // plane
    scale = 1.0 / math.sqrt(wx * wy * wz * plane)
    psi = orbitals.transpose(1, 2, 0, 3)

    ahead_two = shift(psi, "blk", 2)
    core = lax.axis_index("blk") % 2
    count = lax.axis_size("blk")
    ahead_one = lax.ppermute(
        jnp.where(core == 0, ahead_two, psi), "blk", [(i, i ^ 1) for i in range(count)]
    )

    coeff = coupling[None] * pot_grad
    c = [coeff[k][:, :, None, :] for k in range(3)]
    cx = [a for a in neighbours(coeff, "dx", 1)]
    cy = [a for a in neighbours(coeff, "dy", 2)]
    cz = [jnp.roll(coeff, 1, axis=3), jnp.roll(coeff, -1, axis=3)]
    f32 = jnp.float32
    px = [a.astype(f32) for a in neighbours(psi, "dx", 0)]
    py = [a.astype(f32) for a in neighbours(psi, "dy", 1)]
    field = psi.astype(f32)
    pz = [jnp.roll(field, 1, axis=3), jnp.roll(field, -1, axis=3)]
    gx, gy, gz = [0.5 * (p[1] - p[0]) for p in (px, py, pz)]
    u = jnp.stack(
        [c[1] * gz - c[2] * gy, c[2] * gx - c[0] * gz, c[0] * gy - c[1] * gx]
    ).astype(jnp.bfloat16)

    def grad_of(k, cs, ps):
        a, b = [q[k][:, :, None, :] for q in cs]
        return 0.5 * (b * ps[1] - a * ps[0])

    w = jnp.stack(
        [
            grad_of(2, cy, py) - grad_of(1, cz, pz),
            grad_of(0, cz, pz) - grad_of(2, cx, px),
            grad_of(1, cx, px) - grad_of(0, cy, py),
        ]
    ).astype(jnp.bfloat16)

    def dot(spec, a, b):
        return jnp.einsum(spec, a, b, preferred_element_type=f32) * scale

    own = dot("kxyjz,xyiz->kji", u, psi)
    up_two = dot("kxyjz,xyiz->kji", u, ahead_two)
    up_one = dot("kxyjz,xyiz->kji", u, ahead_one)
    down_two = dot("xyjz,kxyiz->kji", ahead_two, w)
    down_one = dot("xyjz,kxyiz->kji", ahead_one, w)

    def by_dest(tiles):
        stacked = jnp.stack(tiles, 1)
        k, t = stacked.shape[:2]
        return stacked.reshape(k, t, plane, rows, states).transpose(2, 0, 1, 3, 4)

    mine = plane_sum(by_dest([own]))
    rest = plane_sum(by_dest([up_one, up_two, down_one, down_two]))
    one = shift(rest[:, 2], "blk", -1)
    two = shift(rest[:, 3], "blk", -2)
    return jnp.stack([two, one, mine[:, 0], rest[:, 0], rest[:, 1]], 1)


def solution(mesh):
    in_specs = (P("blk", "dx", "dy", None), P("dx", "dy", None), P(None, "dx", "dy", None))
    out_specs = P(None, None, ("blk", "dx", "dy"), None)
    return jax.shard_map(
        on_device, mesh=mesh, in_specs=in_specs, out_specs=out_specs, check_vma=False
    )
```

```python
import functools
import math

import jax
import jax.numpy as jnp
from jax import lax
from jax.experimental import pallas as pl
from jax.experimental.pallas import tpu as pltpu
from jax.sharding import PartitionSpec as P

F32, BF16 = jnp.float32, jnp.bfloat16
VMEM = pl.BlockSpec(memory_space=pltpu.VMEM)
SMEM = pl.BlockSpec(memory_space=pltpu.SMEM)
LIMIT = 24 * 1024 * 1024
NT = (((1,), (1,)), ((), ()))
CHUNK = 16


def shift(block, axis, distance):
    count = lax.axis_size(axis)
    return lax.ppermute(block, axis, [((i + distance) % count, i) for i in range(count)])


def both_sides(tail_head, coeff, axis):
    if lax.axis_size(axis) == 2:
        other = shift(coeff, axis, 1)
        return shift(tail_head, axis, 1), other, other
    tail, head = jnp.split(tail_head, 2, axis=1)
    pair = jnp.concatenate([shift(tail, axis, -1), shift(head, axis, 1)], axis=1)
    return pair, shift(coeff, axis, -1), shift(coeff, axis, 1)


def call(body, outs, operands, scratch=(), flops=0, scalars=0):
    specs = [SMEM] * scalars + [VMEM] * (len(operands) - scalars)
    moved = sum(math.prod(a.shape) * a.dtype.itemsize for a in [*outs, *operands])
    return pl.pallas_call(
        body,
        out_shape=outs,
        in_specs=specs,
        out_specs=[VMEM] * len(outs),
        scratch_shapes=list(scratch),
        compiler_params=pltpu.CompilerParams(vmem_limit_bytes=LIMIT),
        cost_estimate=pl.CostEstimate(flops=flops, bytes_accessed=moved, transcendentals=0),
    )(*operands)


def destinations(me, nx, ny):
    x, y = me // ny, me % ny
    return [((x + ox) % nx) * ny + (y + oy) % ny for ox in range(nx) for oy in range(ny)]


def edges(psi, coupling, pot_grad, hx, hy, c, *, shape):
    wx, wy, wz = shape
    layer = wy * wz
    hx[:, :layer] = psi[:, (wx - 1) * layer :]
    hx[:, layer:] = psi[:, :layer]
    for x in range(wx):
        for side, y in enumerate((wy - 1, 0)):
            to, at = (side * wx + x) * wz, x * layer + y * wz
            hy[:, to : to + wz] = psi[:, at : at + wz]
    c[...] = coupling[...][None] * pot_grad[...]


def operators(
    me_ref, psi, hx, hy, c, cxb, cxa, cyb, cya, u, w, keep, *rest, shape, plane, scale
):
    wx, wy, wz = shape
    sends, (half, back, ahead, acc) = rest[:-4], rest[-4:]
    states = psi.shape[0]
    rows = states // math.prod(plane)
    layer = wy * wz
    half[...] = 0.5 * c[...]
    for k in range(3):
        for x in range(wx):
            back[k, x] = pltpu.roll(half[k, x], 1, 1)
            ahead[k, x] = pltpu.roll(half[k, x], wz - 1, 1)

    def coeff(k, x, y):
        if x < 0:
            return 0.5 * cxb[k, wx - 1, y : y + 1, :]
        if x >= wx:
            return 0.5 * cxa[k, 0, y : y + 1, :]
        if y < 0:
            return 0.5 * cyb[k, x, wy - 1 : wy, :]
        if y >= wy:
            return 0.5 * cya[k, x, 0:1, :]
        return half[k, x, y : y + 1, :]

    def group(step, _):
        r = pl.ds(pl.multiple_of(step * CHUNK, CHUNK), CHUNK)

        def field(x, y):
            if x < 0:
                ref, at = hx, y * wz
            elif x >= wx:
                ref, at = hx, layer + y * wz
            elif y < 0:
                ref, at = hy, x * wz
            elif y >= wy:
                ref, at = hy, (wx + x) * wz
            else:
                ref, at = psi, x * layer + y * wz
            return ref[r, at : at + wz].astype(F32)

        for x in range(wx):
            for y in range(wy):
                here = field(x, y)
                xb, xa = field(x - 1, y), field(x + 1, y)
                yb, ya = field(x, y - 1), field(x, y + 1)
                zb, za = pltpu.roll(here, 1, 1), pltpu.roll(here, wz - 1, 1)
                gx, gy, gz = xa - xb, ya - yb, za - zb
                c1, c2, c3 = [coeff(k, x, y) for k in range(3)]
                at = x * layer + y * wz
                cols = slice(at, at + wz)

                def put(ref, k, value):
                    place = pl.ds(pl.multiple_of(k * states + step * CHUNK, CHUNK), CHUNK)
                    ref[place, cols] = value.astype(BF16)

                put(u, 0, c2 * gz - c3 * gy)
                put(u, 1, c3 * gx - c1 * gz)
                put(u, 2, c1 * gy - c2 * gx)

                def dx(k):
                    return coeff(k, x + 1, y) * xa - coeff(k, x - 1, y) * xb

                def dy(k):
                    return coeff(k, x, y + 1) * ya - coeff(k, x, y - 1) * yb

                def dz(k):
                    return ahead[k, x, y : y + 1, :] * za - back[k, x, y : y + 1, :] * zb

                put(w, 0, dy(2) - dz(1))
                put(w, 1, dz(0) - dx(2))
                put(w, 2, dx(1) - dy(0))
        return 0

    lax.fori_loop(0, states // CHUNK, group, 0)
    acc[...] = lax.dot_general(u[...], psi[...], NT, preferred_element_type=F32) * scale
    for ref, dest in zip((keep, *sends), destinations(me_ref[0], *plane)):
        for k in range(3):
            place = pl.ds(pl.multiple_of(k * states + dest * rows, rows), rows)
            ref[k] = acc[place, :].astype(ref.dtype)


def tiles(me_ref, u, w, one, two, keep, *rest, plane, scale):
    sends, (up, down) = rest[:-2], rest[-2:]
    states = one.shape[0]
    rows = states // math.prod(plane)
    for t, panel in enumerate((one, two)):
        up[t] = lax.dot_general(u[...], panel[...], NT, preferred_element_type=F32) * scale
        down[t] = lax.dot_general(panel[...], w[...], NT, preferred_element_type=F32) * scale
    for ref, dest in zip((keep, *sends), destinations(me_ref[0], *plane)):
        for t in range(2):
            for k in range(3):
                place = pl.ds(pl.multiple_of(k * states + dest * rows, rows), rows)
                ref[t, k] = up[t, place, :].astype(ref.dtype)
                place = pl.ds(pl.multiple_of(dest * rows, rows), rows)
                cols = slice(k * states, (k + 1) * states)
                ref[2 + t, k] = down[t, place, cols].astype(ref.dtype)


def add_down(keep, *rest):
    parts, (one, two) = rest[:-2], rest[-2:]
    for t, ref in enumerate((one, two)):
        total = keep[2 + t]
        for part in parts:
            total = total + part[2 + t].astype(F32)
        ref[...] = total


def assemble(count, *refs):
    keep, parts = refs[0], refs[1:count]
    mine, own_parts = refs[count], refs[count + 1 : 2 * count]
    one, two, out = refs[2 * count :]
    for k in range(3):
        out[k, 0] = two[k]
        out[k, 1] = one[k]
        total = mine[k]
        for part in own_parts:
            total = total + part[k].astype(F32)
        out[k, 2] = total
        for t in range(2):
            total = keep[t, k]
            for part in parts:
                total = total + part[t, k].astype(F32)
            out[k, 3 + t] = total


def exchange(sends):
    nx, ny = lax.axis_size("dx"), lax.axis_size("dy")
    got = []
    for o, piece in enumerate(sends, 1):
        ox, oy = o // ny, o % ny
        route = [
            (i * ny + j, ((i + ox) % nx) * ny + (j + oy) % ny) for i in range(nx) for j in range(ny)
        ]
        got.append(lax.ppermute(piece, ("dx", "dy"), route))
    return got


def on_device(orbitals, coupling, pot_grad):
    states, wx, wy, wz = orbitals.shape
    plane = (lax.axis_size("dx"), lax.axis_size("dy"))
    places = math.prod(plane)
    rows = states // places
    layer = wy * wz
    cells = wx * layer
    scale = 1.0 / math.sqrt(cells * places)
    me = lax.axis_index(("dx", "dy")).astype(jnp.int32).reshape(1)
    psi = lax.optimization_barrier(orbitals.reshape(states, cells))
    two = shift(psi, "blk", 2)

    hx, hy, coeff = call(
        functools.partial(edges, shape=(wx, wy, wz)),
        [
            jax.ShapeDtypeStruct((states, 2 * layer), BF16),
            jax.ShapeDtypeStruct((states, 2 * wx * wz), BF16),
            jax.ShapeDtypeStruct((3, wx, wy, wz), F32),
        ],
        [psi, coupling, pot_grad],
    )
    hx, cxb, cxa = both_sides(hx, coeff, "dx")
    hy, cyb, cya = both_sides(hy, coeff, "dy")

    field = jax.ShapeDtypeStruct((3 * states, cells), BF16)
    small = (3, rows, states)
    u, w, mine, *own_sends = call(
        functools.partial(operators, shape=(wx, wy, wz), plane=plane, scale=scale),
        [field, field, jax.ShapeDtypeStruct(small, F32)]
        + [jax.ShapeDtypeStruct(small, BF16)] * (places - 1),
        [me, psi, hx, hy, coeff, cxb, cxa, cyb, cya],
        scratch=[pltpu.VMEM((3, wx, wy, wz), F32)] * 3 + [pltpu.VMEM((3 * states, states), F32)],
        flops=2 * 3 * states * states * cells,
        scalars=1,
    )
    own_parts = exchange(own_sends)

    two, u, own_parts = lax.optimization_barrier((two, u, own_parts))
    core = lax.axis_index("blk") % 2
    swap = [(i, i ^ 1) for i in range(lax.axis_size("blk"))]
    one = lax.ppermute(jnp.where(core == 0, two, psi), "blk", swap)
    keep, *sends = call(
        functools.partial(tiles, plane=plane, scale=scale),
        [jax.ShapeDtypeStruct((4, *small), F32)]
        + [jax.ShapeDtypeStruct((4, *small), BF16)] * (places - 1),
        [me, u, w, one, two],
        scratch=[pltpu.VMEM((2, 3 * states, states), F32), pltpu.VMEM((2, states, 3 * states), F32)],
        flops=4 * 2 * 3 * states * states * cells,
        scalars=1,
    )
    parts = exchange(sends)
    down = [jax.ShapeDtypeStruct(small, F32)] * 2
    from_one, from_two = call(add_down, down, [keep, *parts])
    from_one = shift(from_one, "blk", -1)
    from_two = shift(from_two, "blk", -2)
    (out,) = call(
        functools.partial(assemble, places),
        [jax.ShapeDtypeStruct((3, 5, rows, states), F32)],
        [keep, *parts, mine, *own_parts, from_one, from_two],
    )
    return out


def solution(mesh):
    in_specs = (P("blk", "dx", "dy", None), P("dx", "dy", None), P(None, "dx", "dy", None))
    out_specs = P(None, None, ("blk", "dx", "dy"), None)
    return jax.shard_map(
        on_device, mesh=mesh, in_specs=in_specs, out_specs=out_specs, check_vma=False
    )
```

```python
import functools
import math

import jax
import jax.numpy as jnp
from jax import lax
from jax.experimental import pallas as pl
from jax.experimental.pallas import tpu as pltpu
from jax.sharding import PartitionSpec as P

F32, BF16 = jnp.float32, jnp.bfloat16
VMEM = pl.BlockSpec(memory_space=pltpu.VMEM)
SMEM = pl.BlockSpec(memory_space=pltpu.SMEM)
LIMIT = 12 * 1024 * 1024
PIECES = 1
NT = (((1,), (1,)), ((), ()))
CHUNK = 16


def shift(block, axis, distance):
    count = lax.axis_size(axis)
    return lax.ppermute(block, axis, [((i + distance) % count, i) for i in range(count)])


def both_sides(pair, axis):
    if lax.axis_size(axis) == 2:
        return shift(pair, axis, 1)
    tail, head = jnp.split(pair, 2, axis=1)
    return jnp.concatenate([shift(tail, axis, -1), shift(head, axis, 1)], axis=1)


def call(body, outs, operands, scratch=(), flops=0, scalars=0):
    specs = [SMEM] * scalars + [VMEM] * (len(operands) - scalars)
    moved = sum(math.prod(a.shape) * a.dtype.itemsize for a in [*outs, *operands])
    return pl.pallas_call(
        body,
        out_shape=outs,
        in_specs=specs,
        out_specs=[VMEM] * len(outs),
        scratch_shapes=list(scratch),
        compiler_params=pltpu.CompilerParams(vmem_limit_bytes=LIMIT),
        cost_estimate=pl.CostEstimate(flops=0, bytes_accessed=0, transcendentals=0),
    )(*operands)


def destinations(me, nx, ny):
    x, y = me // ny, me % ny
    return [((x + ox) % nx) * ny + (y + oy) % ny for ox in range(nx) for oy in range(ny)]


def thirds(value):
    high = value.astype(BF16).astype(F32)
    middle = (value - high).astype(BF16).astype(F32)
    return high, middle, value - high - middle


def edges(*refs, shape):
    pieces, (coupling, pot_grad, hx, hy, c, tmp) = refs[:-6], refs[-6:]
    wx, wy, wz = shape
    layer, line = wy * wz, wx * wz
    c[...] = coupling[...][None] * pot_grad[...]
    for side, (x, y) in enumerate(((wx - 1, wy - 1), (0, 0))):
        to_x, to_y = side * (layer + wz), side * (line + wz)
        end = 0
        for psi in pieces:
            r = slice(end, end + psi.shape[0])
            end = r.stop
            hx[r, to_x : to_x + layer] = psi[:, x * layer : (x + 1) * layer]
            for i in range(wx):
                at = i * layer + y * wz
                hy[r, to_y + i * wz : to_y + (i + 1) * wz] = psi[:, at : at + wz]
        for k in range(3):
            for n, third in enumerate(thirds(c[k, x])):
                tmp[(3 * k + n) * wy : (3 * k + n + 1) * wy] = third
        hx[: tmp.shape[0], to_x + layer : to_x + layer + wz] = tmp[...].astype(BF16)
        for k in range(3):
            for n, third in enumerate(thirds(c[k, :, y])):
                tmp[(3 * k + n) * wx : (3 * k + n + 1) * wx] = third
        hy[: tmp.shape[0], to_y + line : to_y + line + wz] = tmp[...].astype(BF16)


def operators(me_ref, *refs, shape, plane, scale):
    wx, wy, wz = shape
    pieces, (hx, hy, c, u, w, keep, *rest) = refs[:PIECES], refs[PIECES:]
    sends, (half, back, ahead, acc, tmp, ex, ey) = rest[:-7], rest[-7:]
    states = sum(psi.shape[0] for psi in pieces)
    rows = states // math.prod(plane)
    layer, line = wy * wz, wx * wz
    half[...] = 0.5 * c[...]
    for ref, to, length, count in ((hx, ex, layer, wy), (hy, ey, line, wx)):
        for side in range(2):
            at = side * (length + wz) + length
            tmp[...] = ref[: tmp.shape[0], at : at + wz].astype(F32)
            for k in range(3):
                third = [tmp[(3 * k + n) * count : (3 * k + n + 1) * count] for n in range(3)]
                to[side, k] = 0.5 * (third[0] + third[1] + third[2])
    for k in range(3):
        for x in range(wx):
            back[k, x] = pltpu.roll(half[k, x], 1, 1)
            ahead[k, x] = pltpu.roll(half[k, x], wz - 1, 1)

    def coeff(k, x, y):
        if x < 0 or x >= wx:
            return ex[int(x >= wx), k, y : y + 1, :]
        if y < 0 or y >= wy:
            return ey[int(y >= wy), k, x : x + 1, :]
        return half[k, x, y : y + 1, :]

    def group(psi, start, step, _):
        own = pl.ds(pl.multiple_of(step * CHUNK, CHUNK), CHUNK)
        step = step + start // CHUNK
        r = pl.ds(pl.multiple_of(step * CHUNK, CHUNK), CHUNK)

        def field(x, y):
            if x < 0:
                ref, at = hx, y * wz
            elif x >= wx:
                ref, at = hx, layer + wz + y * wz
            elif y < 0:
                ref, at = hy, x * wz
            elif y >= wy:
                ref, at = hy, line + wz + x * wz
            else:
                at = x * layer + y * wz
                return psi[own, at : at + wz].astype(F32)
            return ref[r, at : at + wz].astype(F32)

        for x in range(wx):
            for y in range(wy):
                here = field(x, y)
                xb, xa = field(x - 1, y), field(x + 1, y)
                yb, ya = field(x, y - 1), field(x, y + 1)
                zb, za = pltpu.roll(here, 1, 1), pltpu.roll(here, wz - 1, 1)
                gx, gy, gz = xa - xb, ya - yb, za - zb
                c1, c2, c3 = [coeff(k, x, y) for k in range(3)]
                at = x * layer + y * wz
                cols = slice(at, at + wz)

                def put(ref, k, value):
                    place = pl.ds(pl.multiple_of(k * states + step * CHUNK, CHUNK), CHUNK)
                    ref[place, cols] = value.astype(BF16)

                put(u, 0, c2 * gz - c3 * gy)
                put(u, 1, c3 * gx - c1 * gz)
                put(u, 2, c1 * gy - c2 * gx)

                def dx(k):
                    return coeff(k, x + 1, y) * xa - coeff(k, x - 1, y) * xb

                def dy(k):
                    return coeff(k, x, y + 1) * ya - coeff(k, x, y - 1) * yb

                def dz(k):
                    return ahead[k, x, y : y + 1, :] * za - back[k, x, y : y + 1, :] * zb

                put(w, 0, dy(2) - dz(1))
                put(w, 1, dz(0) - dx(2))
                put(w, 2, dx(1) - dy(0))
        return 0

    end = 0
    for psi in pieces:
        lax.fori_loop(0, psi.shape[0] // CHUNK, functools.partial(group, psi, end), 0)
        end += psi.shape[0]
    whole = jnp.concatenate([psi[...] for psi in pieces], axis=0)
    acc[...] = lax.dot_general(u[...], whole, NT, preferred_element_type=F32) * scale
    for ref, dest in zip((keep, *sends), destinations(me_ref[0], *plane)):
        for k in range(3):
            place = pl.ds(pl.multiple_of(k * states + dest * rows, rows), rows)
            ref[k] = acc[place, :].astype(ref.dtype)


def tiles(me_ref, u, w, *refs, plane, scale):
    panels, (keep, *rest) = refs[: 2 * PIECES], refs[2 * PIECES :]
    sends, (up, down) = rest[:-2], rest[-2:]
    states = sum(panel.shape[0] for panel in panels) // 2
    rows = states // math.prod(plane)
    both = jnp.concatenate([panel[...] for panel in panels], axis=0)
    up[...] = lax.dot_general(u[...], both, NT, preferred_element_type=F32) * scale
    down[...] = lax.dot_general(both, w[...], NT, preferred_element_type=F32) * scale
    for ref, dest in zip((keep, *sends), destinations(me_ref[0], *plane)):
        for t in range(2):
            for k in range(3):
                place = pl.ds(pl.multiple_of(k * states + dest * rows, rows), rows)
                ref[t, k] = up[place, t * states : (t + 1) * states].astype(ref.dtype)
                place = pl.ds(pl.multiple_of(t * states + dest * rows, rows), rows)
                ref[2 + t, k] = down[place, k * states : (k + 1) * states].astype(ref.dtype)


def add_down(keep, *rest):
    parts, (one, two) = rest[:-2], rest[-2:]
    for t, ref in enumerate((one, two)):
        total = keep[2 + t]
        for part in parts:
            total = total + part[2 + t].astype(F32)
        ref[...] = total


def assemble(count, *refs):
    keep, parts = refs[0], refs[1:count]
    mine, own_parts = refs[count], refs[count + 1 : 2 * count]
    one, two, out = refs[2 * count :]
    for k in range(3):
        out[k, 0] = two[k]
        out[k, 1] = one[k]
        total = mine[k]
        for part in own_parts:
            total = total + part[k].astype(F32)
        out[k, 2] = total
        for t in range(2):
            total = keep[t, k]
            for part in parts:
                total = total + part[t, k].astype(F32)
            out[k, 3 + t] = total


def exchange(sends):
    nx, ny = lax.axis_size("dx"), lax.axis_size("dy")
    got = []
    for o, piece in enumerate(sends, 1):
        ox, oy = o // ny, o % ny
        route = [
            (i * ny + j, ((i + ox) % nx) * ny + (j + oy) % ny) for i in range(nx) for j in range(ny)
        ]
        got.append(lax.ppermute(piece, ("dx", "dy"), route))
    return got


def on_device(orbitals, coupling, pot_grad):
    states, wx, wy, wz = orbitals.shape
    plane = (lax.axis_size("dx"), lax.axis_size("dy"))
    places = math.prod(plane)
    rows = states // places
    layer = wy * wz
    cells = wx * layer
    scale = 1.0 / math.sqrt(cells * places)
    me = lax.axis_index(("dx", "dy")).astype(jnp.int32).reshape(1)
    psi = []
    for piece in jnp.split(orbitals, PIECES, axis=0):
        psi.append(lax.optimization_barrier(piece.reshape(piece.shape[0], cells)))
    two = [shift(piece, "blk", 2) for piece in psi]

    spill = -(-9 * max(wx, wy) // 16) * 16
    hx, hy, coeff = call(
        functools.partial(edges, shape=(wx, wy, wz)),
        [
            jax.ShapeDtypeStruct((states, 2 * (layer + wz)), BF16),
            jax.ShapeDtypeStruct((states, 2 * (wx * wz + wz)), BF16),
            jax.ShapeDtypeStruct((3, wx, wy, wz), F32),
        ],
        [*psi, coupling, pot_grad],
        scratch=[pltpu.VMEM((spill, wz), F32)],
    )
    hx, hy = both_sides(hx, "dx"), both_sides(hy, "dy")

    core = lax.axis_index("blk") % 2
    swap = [(i, i ^ 1) for i in range(lax.axis_size("blk"))]

    def swapped(n):
        return lax.ppermute(jnp.where(core == 0, two[n], psi[n]), "blk", swap)

    field = jax.ShapeDtypeStruct((3 * states, cells), BF16)
    small = (3, rows, states)
    u, w, mine, *own_sends = call(
        functools.partial(operators, shape=(wx, wy, wz), plane=plane, scale=scale),
        [field, field, jax.ShapeDtypeStruct(small, F32)]
        + [jax.ShapeDtypeStruct(small, BF16)] * (places - 1),
        [me, *psi, hx, hy, coeff],
        scratch=[pltpu.VMEM((3, wx, wy, wz), F32)] * 3
        + [pltpu.VMEM((3 * states, states), F32), pltpu.VMEM((spill, wz), F32)]
        + [pltpu.VMEM((2, 3, wy, wz), F32), pltpu.VMEM((2, 3, wx, wz), F32)],
        flops=2 * 3 * states * states * cells,
        scalars=1,
    )
    own_parts = exchange(own_sends)

    two, u, own_parts = lax.optimization_barrier((two, u, own_parts))
    one = [swapped(n) for n in range(PIECES)]

    keep, *sends = call(
        functools.partial(tiles, plane=plane, scale=scale),
        [jax.ShapeDtypeStruct((4, *small), F32)]
        + [jax.ShapeDtypeStruct((4, *small), BF16)] * (places - 1),
        [me, u, w, *one, *two],
        scratch=[pltpu.VMEM((3 * states, 2 * states), F32), pltpu.VMEM((2 * states, 3 * states), F32)],
        flops=4 * 2 * 3 * states * states * cells,
        scalars=1,
    )
    parts = exchange(sends)
    down = [jax.ShapeDtypeStruct(small, F32)] * 2
    from_one, from_two = call(add_down, down, [keep, *parts])
    from_one = shift(from_one, "blk", -1)
    from_two = shift(from_two, "blk", -2)
    (out,) = call(
        functools.partial(assemble, places),
        [jax.ShapeDtypeStruct((3, 5, rows, states), F32)],
        [keep, *parts, mine, *own_parts, from_one, from_two],
    )
    return out


def solution(mesh):
    in_specs = (P("blk", "dx", "dy", None), P("dx", "dy", None), P(None, "dx", "dy", None))
    out_specs = P(None, None, ("blk", "dx", "dy"), None)
    return jax.shard_map(
        on_device, mesh=mesh, in_specs=in_specs, out_specs=out_specs, check_vma=False
    )
```

```python
import functools
import math

import jax
import jax.numpy as jnp
from jax import lax
from jax.experimental import pallas as pl
from jax.experimental.pallas import tpu as pltpu
from jax.sharding import PartitionSpec as P

F32, BF16 = jnp.float32, jnp.bfloat16
VMEM = pl.BlockSpec(memory_space=pltpu.VMEM)
SMEM = pl.BlockSpec(memory_space=pltpu.SMEM)
ANY = pl.BlockSpec(memory_space=pl.ANY)
LIMIT = 12 * 1024 * 1024
NT = (((1,), (1,)), ((), ()))
CHUNK = 16


def shape_of(shape, dtype):
    return jax.ShapeDtypeStruct(shape, dtype)


def shift(block, axis, distance):
    count = lax.axis_size(axis)
    return lax.ppermute(block, axis, [((i + distance) % count, i) for i in range(count)])


def both_sides(pair, axis):
    if lax.axis_size(axis) == 2:
        return shift(pair, axis, 1)
    tail, head = jnp.split(pair, 2, axis=1)
    return jnp.concatenate([shift(tail, axis, -1), shift(head, axis, 1)], axis=1)


def exchange(sends):
    nx, ny = lax.axis_size("dx"), lax.axis_size("dy")
    got = []
    for o, piece in enumerate(sends, 1):
        ox, oy = o // ny, o % ny
        route = [
            (i * ny + j, ((i + ox) % nx) * ny + (j + oy) % ny) for i in range(nx) for j in range(ny)
        ]
        got.append(lax.ppermute(piece, ("dx", "dy"), route))
    return got


def call(body, outs, operands, scratch=(), specs=None, us=0):
    run = pl.pallas_call(
        body,
        out_shape=outs,
        in_specs=specs or [VMEM] * len(operands),
        out_specs=[VMEM] * len(outs),
        scratch_shapes=list(scratch),
        compiler_params=pltpu.CompilerParams(vmem_limit_bytes=LIMIT),
        cost_estimate=pl.CostEstimate(
            flops=0, bytes_accessed=int(us * 3e6), transcendentals=0
        ),
    )
    return list(run(*operands))


def destinations(me, nx, ny):
    x, y = me // ny, me % ny
    return [((x + ox) % nx) * ny + (y + oy) % ny for ox in range(nx) for oy in range(ny)]


def thirds(value):
    high = value.astype(BF16).astype(F32)
    middle = (value - high).astype(BF16).astype(F32)
    return high, middle, value - high - middle


def edges(psi, coupling_in, grad_in, hx, hy, c, tmp, coupling, grad, sem, *, shape):
    first = pltpu.make_async_copy(coupling_in, coupling, sem.at[0])
    second = pltpu.make_async_copy(grad_in, grad, sem.at[1])
    first.start()
    second.start()
    wx, wy, wz = shape
    layer, line = wy * wz, wx * wz
    ends = ((wx - 1, wy - 1), (0, 0))
    for side, (x, y) in enumerate(ends):
        to_x, to_y = side * (layer + wz), side * (line + wz)
        hx[:, to_x : to_x + layer] = psi[:, x * layer : (x + 1) * layer]
        for i in range(wx):
            at = i * layer + y * wz
            hy[:, to_y + i * wz : to_y + (i + 1) * wz] = psi[:, at : at + wz]
    first.wait()
    second.wait()
    c[...] = coupling[...][None] * grad[...]
    for side, (x, y) in enumerate(ends):
        to_x, to_y = side * (layer + wz), side * (line + wz)
        for k in range(3):
            for n, third in enumerate(thirds(c[k, x])):
                tmp[(3 * k + n) * wy : (3 * k + n + 1) * wy] = third
        hx[: tmp.shape[0], to_x + layer : to_x + layer + wz] = tmp[...].astype(BF16)
        for k in range(3):
            for n, third in enumerate(thirds(c[k, :, y])):
                tmp[(3 * k + n) * wx : (3 * k + n + 1) * wx] = third
        hy[: tmp.shape[0], to_y + line : to_y + line + wz] = tmp[...].astype(BF16)


def operators(layers, psi, hx, hy, c, u, w, half, back, ahead, tmp, ex, ey, *, shape):
    wx, wy, wz = shape
    layer, line = wy * wz, wx * wz
    states = psi.shape[0]
    half[...] = 0.5 * c[...]
    for ref, to, length, count in ((hx, ex, layer, wy), (hy, ey, line, wx)):
        if ref is None:
            continue
        for side in range(2):
            at = side * (length + wz) + length
            tmp[...] = ref[: tmp.shape[0], at : at + wz].astype(F32)
            for k in range(3):
                third = [tmp[(3 * k + n) * count : (3 * k + n + 1) * count] for n in range(3)]
                to[side, k] = 0.5 * (third[0] + third[1] + third[2])
    for k in range(3):
        for x in layers:
            back[k, x] = pltpu.roll(half[k, x], 1, 1)
            ahead[k, x] = pltpu.roll(half[k, x], wz - 1, 1)

    def coeff(k, x, y):
        if x < 0 or x >= wx:
            return ex[int(x >= wx), k, y : y + 1, :]
        if y < 0 or y >= wy:
            return ey[int(y >= wy), k, x : x + 1, :]
        return half[k, x, y : y + 1, :]

    def group(step, _):
        r = pl.ds(pl.multiple_of(step * CHUNK, CHUNK), CHUNK)

        def field(x, y):
            if x < 0:
                ref, at = hx, y * wz
            elif x >= wx:
                ref, at = hx, layer + wz + y * wz
            elif y < 0:
                ref, at = hy, x * wz
            elif y >= wy:
                ref, at = hy, line + wz + x * wz
            else:
                ref, at = psi, x * layer + y * wz
            return ref[r, at : at + wz].astype(F32)

        for n, x in enumerate(layers):
            for y in range(wy):
                here = field(x, y)
                xb, xa = field(x - 1, y), field(x + 1, y)
                yb, ya = field(x, y - 1), field(x, y + 1)
                zb, za = pltpu.roll(here, 1, 1), pltpu.roll(here, wz - 1, 1)
                gx, gy, gz = xa - xb, ya - yb, za - zb
                c1, c2, c3 = [coeff(k, x, y) for k in range(3)]
                cols = slice(n * layer + y * wz, n * layer + (y + 1) * wz)

                def put(ref, k, value):
                    place = pl.ds(pl.multiple_of(k * states + step * CHUNK, CHUNK), CHUNK)
                    ref[place, cols] = value.astype(BF16)

                put(u, 0, c2 * gz - c3 * gy)
                put(u, 1, c3 * gx - c1 * gz)
                put(u, 2, c1 * gy - c2 * gx)

                def dx(k):
                    return coeff(k, x + 1, y) * xa - coeff(k, x - 1, y) * xb

                def dy(k):
                    return coeff(k, x, y + 1) * ya - coeff(k, x, y - 1) * yb

                def dz(k):
                    return ahead[k, x, y : y + 1, :] * za - back[k, x, y : y + 1, :] * zb

                put(w, 0, dy(2) - dz(1))
                put(w, 1, dz(0) - dx(2))
                put(w, 2, dx(1) - dy(0))
        return 0

    lax.fori_loop(0, states // CHUNK, group, 0)


def inner(psi, hy, c, u, w, half, back, ahead, tmp, ey, *, shape):
    layers = range(1, shape[0] - 1)
    operators(layers, psi, None, hy, c, u, w, half, back, ahead, tmp, None, ey, shape=shape)


def product(a_inner, a_outer, panel, layer, flip):
    cells = panel.shape[1]
    last = a_outer.shape[1] - layer
    pairs = (
        (a_inner[...], panel[:, layer : cells - layer]),
        (a_outer[:, :layer], panel[:, :layer]),
        (a_outer[:, last:], panel[:, cells - layer :]),
    )
    total = 0.0
    for a, b in pairs:
        a, b = (b, a) if flip else (a, b)
        total = total + lax.dot_general(a, b, NT, preferred_element_type=F32)
    return total


def outer(
    me_ref, psi, hx, hy, c, u_inner, u, w, keep, *rest, shape, plane, scale
):
    sends, (half, back, ahead, tmp, ex, ey, acc) = rest[:-7], rest[-7:]
    layers = (0, shape[0] - 1)
    operators(layers, psi, hx, hy, c, u, w, half, back, ahead, tmp, ex, ey, shape=shape)
    states = psi.shape[0]
    rows = states // math.prod(plane)
    acc[...] = product(u_inner, u, psi, shape[1] * shape[2], False) * scale
    for ref, dest in zip((keep, *sends), destinations(me_ref[0], *plane)):
        for k in range(3):
            place = pl.ds(pl.multiple_of(k * states + dest * rows, rows), rows)
            ref[k] = acc[place, :].astype(ref.dtype)


def choose(core_ref, two, psi, out):
    @pl.when(core_ref[0] == 1)
    def _():
        out[...] = two[...]

    @pl.when(core_ref[0] == 0)
    def _():
        out[...] = psi[...]


def tiles(me_ref, u_inner, u_outer, w_inner, w_outer, panel, keep, *rest, layer, plane, scale):
    sends, (here, there) = rest[:-2], rest[-2:]
    states = panel.shape[0]
    rows = states // math.prod(plane)
    here[...] = product(u_inner, u_outer, panel, layer, False) * scale
    there[...] = product(w_inner, w_outer, panel, layer, True) * scale
    for ref, dest in zip((keep, *sends), destinations(me_ref[0], *plane)):
        for k in range(3):
            place = pl.ds(pl.multiple_of(k * states + dest * rows, rows), rows)
            ref[0, k] = here[place, :].astype(ref.dtype)
            place = pl.ds(pl.multiple_of(dest * rows, rows), rows)
            ref[1, k] = there[place, k * states : (k + 1) * states].astype(ref.dtype)


def add_there(keep, *rest):
    parts, total_ref = rest[:-1], rest[-1]
    total = keep[1]
    for part in parts:
        total = total + part[1].astype(F32)
    total_ref[...] = total


def assemble(count, *refs):
    mine, one, two = refs[:count], refs[count : 2 * count], refs[2 * count : 3 * count]
    from_one, from_two, out = refs[3 * count :]
    for k in range(3):
        for t, group in ((0, two), (1, one)):
            total = group[0][0, k]
            for part in group[1:]:
                total = total + part[0, k].astype(F32)
            out[k, t] = total
        total = mine[0][k]
        for part in mine[1:]:
            total = total + part[k].astype(F32)
        out[k, 2] = total
        out[k, 3] = from_one[k]
        out[k, 4] = from_two[k]


def on_device(orbitals, coupling, pot_grad):
    states, wx, wy, wz = orbitals.shape
    shape = (wx, wy, wz)
    plane = (lax.axis_size("dx"), lax.axis_size("dy"))
    places = math.prod(plane)
    rows = states // places
    layer, line = wy * wz, wx * wz
    cells = wx * layer
    scale = 1.0 / math.sqrt(cells * places)
    me = lax.axis_index(("dx", "dy")).astype(jnp.int32).reshape(1)
    core = (lax.axis_index("blk") % 2).astype(jnp.int32).reshape(1)

    psi = lax.optimization_barrier(orbitals.reshape(states, cells))
    two = shift(psi, "blk", -2)

    spill = -(-9 * max(wx, wy) // 16) * 16
    tmp = pltpu.VMEM((spill, wz), F32)
    coeffs = pltpu.VMEM((3, wx, wy, wz), F32)
    hx, hy, coeff = call(
        functools.partial(edges, shape=shape),
        [
            shape_of((states, 2 * (layer + wz)), BF16),
            shape_of((states, 2 * (line + wz)), BF16),
            shape_of((3, wx, wy, wz), F32),
        ],
        [psi, coupling, pot_grad],
        scratch=[tmp, pltpu.VMEM((wx, wy, wz), F32), coeffs, pltpu.SemaphoreType.DMA((2,))],
        specs=[VMEM, ANY, ANY],
    )
    hx, hy = both_sides(hx, "dx"), both_sides(hy, "dy")

    ex, ey = pltpu.VMEM((2, 3, wy, wz), F32), pltpu.VMEM((2, 3, wx, wz), F32)
    small = (3, rows, states)
    field = shape_of((3 * states, cells - 2 * layer), BF16)
    u_inner, w_inner = call(
        functools.partial(inner, shape=shape),
        [field, field],
        [psi, hy, coeff],
        scratch=[coeffs] * 3 + [tmp, ey],
        us=2,
    )
    field = shape_of((3 * states, 2 * layer), BF16)
    u_outer, w_outer, *mine = call(
        functools.partial(outer, shape=shape, plane=plane, scale=scale),
        [field, field, shape_of(small, F32)] + [shape_of(small, BF16)] * (places - 1),
        [me, psi, hx, hy, coeff, u_inner],
        scratch=[coeffs] * 3 + [tmp, ex, ey, pltpu.VMEM((3 * states, states), F32)],
        specs=[SMEM] + [VMEM] * 5,
    )
    mine[1:] = exchange(mine[1:])

    two, mine[1:] = lax.optimization_barrier((two, mine[1:]))
    (mixed,) = call(
        choose, [shape_of((states, cells), BF16)], [core, two, psi], specs=[SMEM, VMEM, VMEM]
    )
    swap = [(i, i ^ 1) for i in range(lax.axis_size("blk"))]
    one = lax.ppermute(mixed, "blk", swap)

    def tiles_with(panel):
        pair = (2, *small)
        return call(
            functools.partial(tiles, layer=layer, plane=plane, scale=scale),
            [shape_of(pair, F32)] + [shape_of(pair, BF16)] * (places - 1),
            [me, u_inner, u_outer, w_inner, w_outer, panel],
            scratch=[
                pltpu.VMEM((3 * states, states), F32),
                pltpu.VMEM((states, 3 * states), F32),
            ],
            specs=[SMEM] + [VMEM] * 5,
            us=1,
        )

    def sent_back(group, distance):
        (total,) = call(add_there, [shape_of(small, F32)], group)
        return shift(total, "blk", distance)

    group_two = tiles_with(two)
    group_two[1:] = exchange(group_two[1:])
    one, group_two[0] = lax.optimization_barrier((one, group_two[0]))
    group_one = tiles_with(one)
    group_one[1:] = exchange(group_one[1:])
    from_two = sent_back(group_two, 2)
    from_one = sent_back(group_one, 1)
    (out,) = call(
        functools.partial(assemble, places),
        [shape_of((3, 5, rows, states), F32)],
        [*mine, *group_one, *group_two, from_one, from_two],
    )
    return out


def solution(mesh):
    in_specs = (P("blk", "dx", "dy", None), P("dx", "dy", None), P(None, "dx", "dy", None))
    out_specs = P(None, None, ("blk", "dx", "dy"), None)
    return jax.shard_map(
        on_device, mesh=mesh, in_specs=in_specs, out_specs=out_specs, check_vma=False
    )
```

```python
import functools
import math

import jax
import jax.numpy as jnp
from jax import lax
from jax.experimental import pallas as pl
from jax.experimental.pallas import tpu as pltpu
from jax.sharding import PartitionSpec as P

F32, BF16 = jnp.float32, jnp.bfloat16
VMEM = pl.BlockSpec(memory_space=pltpu.VMEM)
ANY = pl.BlockSpec(memory_space=pl.ANY)
LIMIT = 12 * 1024 * 1024
NT = (((1,), (1,)), ((), ()))
CHUNK = 16


def shape_of(shape, dtype):
    return jax.ShapeDtypeStruct(shape, dtype)


def shift(block, axis, distance):
    count = lax.axis_size(axis)
    return lax.ppermute(block, axis, [((i + distance) % count, i) for i in range(count)])


def both_sides(pair, axis):
    if lax.axis_size(axis) == 2:
        return shift(pair, axis, 1)
    tail, head = jnp.split(pair, 2, axis=1)
    return jnp.concatenate([shift(tail, axis, -1), shift(head, axis, 1)], axis=1)


def exchange(sends):
    nx, ny = lax.axis_size("dx"), lax.axis_size("dy")
    got = []
    for o, piece in enumerate(sends, 1):
        ox, oy = o // ny, o % ny
        route = [
            (i * ny + j, ((i + ox) % nx) * ny + (j + oy) % ny) for i in range(nx) for j in range(ny)
        ]
        got.append(lax.ppermute(piece, ("dx", "dy"), route))
    return got


def call(body, outs, operands, scratch=(), specs=None, out_specs=None, us=0):
    run = pl.pallas_call(
        body,
        out_shape=outs,
        in_specs=specs or [VMEM] * len(operands),
        out_specs=out_specs or [VMEM] * len(outs),
        scratch_shapes=list(scratch),
        compiler_params=pltpu.CompilerParams(vmem_limit_bytes=LIMIT),
        cost_estimate=pl.CostEstimate(
            flops=0, bytes_accessed=int(us * 3e6), transcendentals=0
        ),
    )
    return list(run(*operands))


def destinations(nx, ny):
    x, y = lax.axis_index("dx"), lax.axis_index("dy")
    return [
        lax.rem(x + ox, nx) * ny + lax.rem(y + oy, ny) for ox in range(nx) for oy in range(ny)
    ]


def thirds(value):
    high = value.astype(BF16).astype(F32)
    middle = (value - high).astype(BF16).astype(F32)
    return high, middle, value - high - middle


def edges(psi, coupling, grad, hx, hy, tmp, *, shape):
    wx, wy, wz = shape
    layer, line = wy * wz, wx * wz
    for side, (x, y) in enumerate(((wx - 1, wy - 1), (0, 0))):
        to_x, to_y = side * (layer + wz), side * (line + wz)
        hx[:, to_x : to_x + layer] = psi[:, x * layer : (x + 1) * layer]
        for i in range(wx):
            at = i * layer + y * wz
            hy[:, to_y + i * wz : to_y + (i + 1) * wz] = psi[:, at : at + wz]
        for k in range(3):
            for n, third in enumerate(thirds(coupling[x] * grad[k, x])):
                tmp[(3 * k + n) * wy : (3 * k + n + 1) * wy] = third
        hx[: tmp.shape[0], to_x + layer : to_x + layer + wz] = tmp[...].astype(BF16)
        for k in range(3):
            for n, third in enumerate(thirds(coupling[:, y] * grad[k, :, y])):
                tmp[(3 * k + n) * wx : (3 * k + n + 1) * wx] = third
        hy[: tmp.shape[0], to_y + line : to_y + line + wz] = tmp[...].astype(BF16)


def operators(layers, psi, hx, hy, coupling, grad, u, w, half, back, ahead, tmp, ex, ey, *, shape):
    wx, wy, wz = shape
    layer, line = wy * wz, wx * wz
    states = psi.shape[0]
    half[...] = 0.5 * (coupling[...][None] * grad[...])
    for ref, to, length, count in ((hx, ex, layer, wy), (hy, ey, line, wx)):
        if ref is None:
            continue
        for side in range(2):
            at = side * (length + wz) + length
            tmp[...] = ref[: tmp.shape[0], at : at + wz].astype(F32)
            for k in range(3):
                third = [tmp[(3 * k + n) * count : (3 * k + n + 1) * count] for n in range(3)]
                to[side, k] = 0.5 * (third[0] + third[1] + third[2])
    for k in range(3):
        for x in layers:
            back[k, x] = pltpu.roll(half[k, x], 1, 1)
            ahead[k, x] = pltpu.roll(half[k, x], wz - 1, 1)

    def coeff(k, x, y):
        if x < 0 or x >= wx:
            return ex[int(x >= wx), k, y : y + 1, :]
        if y < 0 or y >= wy:
            return ey[int(y >= wy), k, x : x + 1, :]
        return half[k, x, y : y + 1, :]

    def group(step, _):
        r = pl.ds(pl.multiple_of(step * CHUNK, CHUNK), CHUNK)

        def field(x, y):
            if x < 0:
                ref, at = hx, y * wz
            elif x >= wx:
                ref, at = hx, layer + wz + y * wz
            elif y < 0:
                ref, at = hy, x * wz
            elif y >= wy:
                ref, at = hy, line + wz + x * wz
            else:
                ref, at = psi, x * layer + y * wz
            return ref[r, at : at + wz].astype(F32)

        for n, x in enumerate(layers):
            for y in range(wy):
                here = field(x, y)
                xb, xa = field(x - 1, y), field(x + 1, y)
                yb, ya = field(x, y - 1), field(x, y + 1)
                zb, za = pltpu.roll(here, 1, 1), pltpu.roll(here, wz - 1, 1)
                gx, gy, gz = xa - xb, ya - yb, za - zb
                c1, c2, c3 = [coeff(k, x, y) for k in range(3)]
                cols = slice(n * layer + y * wz, n * layer + (y + 1) * wz)

                def put(ref, k, value):
                    place = pl.ds(pl.multiple_of(k * states + step * CHUNK, CHUNK), CHUNK)
                    ref[place, cols] = value.astype(BF16)

                put(u, 0, c2 * gz - c3 * gy)
                put(u, 1, c3 * gx - c1 * gz)
                put(u, 2, c1 * gy - c2 * gx)

                def dx(k):
                    return coeff(k, x + 1, y) * xa - coeff(k, x - 1, y) * xb

                def dy(k):
                    return coeff(k, x, y + 1) * ya - coeff(k, x, y - 1) * yb

                def dz(k):
                    return ahead[k, x, y : y + 1, :] * za - back[k, x, y : y + 1, :] * zb

                put(w, 0, dy(2) - dz(1))
                put(w, 1, dz(0) - dx(2))
                put(w, 2, dx(1) - dy(0))
        return 0

    lax.fori_loop(0, states // CHUNK, group, 0)


def inner(psi, hy, coupling, grad, u, w, half, back, ahead, tmp, ey, *, shape):
    layers = range(1, shape[0] - 1)
    operators(
        layers, psi, None, hy, coupling, grad, u, w, half, back, ahead, tmp, None, ey, shape=shape
    )


def outer(psi, hx, hy, coupling, grad, u_inner, w_inner, u, w, *scratch, shape):
    operators((0, shape[0] - 1), psi, hx, hy, coupling, grad, u, w, *scratch, shape=shape)


def product(a_inner, a_outer, panel, layer, flip):
    cells = panel.shape[1]
    last = a_outer.shape[1] - layer
    pairs = (
        (a_inner[...], panel[:, layer : cells - layer]),
        (a_outer[:, :layer], panel[:, :layer]),
        (a_outer[:, last:], panel[:, cells - layer :]),
    )
    total = 0.0
    for a, b in pairs:
        a, b = (b, a) if flip else (a, b)
        total = total + lax.dot_general(a, b, NT, preferred_element_type=F32)
    return total


def own_tiles(u_inner, u_outer, w_inner, w_outer, psi, here, *, layer, scale):
    here[...] = product(u_inner, u_outer, psi, layer, False) * scale


def choose(two, psi, out, sem):
    core = lax.rem(lax.axis_index("blk"), 2)

    @pl.when(core == 1)
    def _():
        copy = pltpu.make_async_copy(two, out, sem)
        copy.start()
        copy.wait()

    @pl.when(core != 1)
    def _():
        copy = pltpu.make_async_copy(psi, out, sem)
        copy.start()
        copy.wait()


def tiles(u_inner, u_outer, w_inner, w_outer, panel, here, there, *, layer, scale):
    here[...] = product(u_inner, u_outer, panel, layer, False) * scale
    there[...] = product(w_inner, w_outer, panel, layer, True) * scale


def tiles_and_pieces(
    u_inner, u_outer, w_inner, w_outer, panel, own, here_two, there_two, *rest,
    layer, plane, scale
):
    outs, (here, there) = rest[:-2], rest[-2:]
    tiles(u_inner, u_outer, w_inner, w_outer, panel, here, there, layer=layer, scale=scale)
    states = panel.shape[0]
    rows = states // math.prod(plane)
    for ref, dest in zip(outs, destinations(*plane)):
        for k in range(3):
            place = pl.ds(pl.multiple_of(k * states + dest * rows, rows), rows)
            for t, tile in enumerate((here_two, here, own)):
                ref[t, k] = tile[place, :].astype(ref.dtype)
            place = pl.ds(pl.multiple_of(dest * rows, rows), rows)
            for t, tile in ((3, there), (4, there_two)):
                ref[t, k] = tile[place, k * states : (k + 1) * states].astype(ref.dtype)


def add(keep, *rest):
    parts, (one, two) = rest[:-2], rest[-2:]
    for t, ref in ((3, one), (4, two)):
        total = keep[t]
        for part in parts:
            total = total + part[t].astype(F32)
        ref[...] = total


def assemble(keep, *rest):
    parts, (from_one, from_two, out) = rest[:-3], rest[-3:]
    for k in range(3):
        for t in range(3):
            total = keep[t, k]
            for part in parts:
                total = total + part[t, k].astype(F32)
            out[k, t] = total
        out[k, 3] = from_one[k]
        out[k, 4] = from_two[k]


def on_device(orbitals, coupling, pot_grad):
    states, wx, wy, wz = orbitals.shape
    shape = (wx, wy, wz)
    plane = (lax.axis_size("dx"), lax.axis_size("dy"))
    places = math.prod(plane)
    rows = states // places
    layer, line = wy * wz, wx * wz
    cells = wx * layer
    scale = 1.0 / math.sqrt(cells * places)

    psi = lax.optimization_barrier(orbitals.reshape(states, cells))
    two = shift(psi, "blk", -2)

    spill = -(-9 * max(wx, wy) // 16) * 16
    tmp = pltpu.VMEM((spill, wz), F32)
    hx, hy = call(
        functools.partial(edges, shape=shape),
        [
            shape_of((states, 2 * (layer + wz)), BF16),
            shape_of((states, 2 * (line + wz)), BF16),
        ],
        [psi, coupling, pot_grad],
        scratch=[tmp],
    )
    hx, hy = both_sides(hx, "dx"), both_sides(hy, "dy")

    coeffs = pltpu.VMEM((3, wx, wy, wz), F32)
    ex, ey = pltpu.VMEM((2, 3, wy, wz), F32), pltpu.VMEM((2, 3, wx, wz), F32)
    field = shape_of((3 * states, cells - 2 * layer), BF16)
    u_inner, w_inner = call(
        functools.partial(inner, shape=shape),
        [field, field],
        [psi, hy, coupling, pot_grad],
        scratch=[coeffs] * 3 + [tmp, ey],
        us=2,
    )
    field = shape_of((3 * states, 2 * layer), BF16)
    u_outer, w_outer = call(
        functools.partial(outer, shape=shape),
        [field, field],
        [psi, hx, hy, coupling, pot_grad, u_inner, w_inner],
        scratch=[coeffs] * 3 + [tmp, ex, ey],
    )
    operands = [u_inner, u_outer, w_inner, w_outer]
    tall, wide = shape_of((3 * states, states), F32), shape_of((states, 3 * states), F32)
    (own,) = call(
        functools.partial(own_tiles, layer=layer, scale=scale), [tall], [*operands, psi]
    )

    two, own = lax.optimization_barrier((two, own))
    (mixed,) = call(
        choose,
        [shape_of((states, cells), BF16)],
        [two, psi],
        scratch=[pltpu.SemaphoreType.DMA],
        specs=[ANY, ANY],
        out_specs=[ANY],
    )
    swap = [(i, i ^ 1) for i in range(lax.axis_size("blk"))]
    one = lax.ppermute(mixed, "blk", swap)
    far = call(
        functools.partial(tiles, layer=layer, scale=scale),
        [tall, wide],
        [*operands, two],
        us=1,
    )
    one, far = lax.optimization_barrier((one, far))
    pieces = (5, 3, rows, states)
    keep, *sends = call(
        functools.partial(tiles_and_pieces, layer=layer, plane=plane, scale=scale),
        [shape_of(pieces, F32)] + [shape_of(pieces, BF16)] * (places - 1),
        [*operands, one, own, *far],
        scratch=[pltpu.VMEM(tall.shape, F32), pltpu.VMEM(wide.shape, F32)],
        us=1,
    )
    parts = exchange(sends)
    from_one, from_two = call(add, [shape_of(pieces[1:], F32)] * 2, [keep, *parts])
    from_one, from_two = shift(from_one, "blk", 1), shift(from_two, "blk", 2)
    (out,) = call(
        assemble,
        [shape_of((3, 5, rows, states), F32)],
        [keep, *parts, from_one, from_two],
    )
    return out


def solution(mesh):
    in_specs = (P("blk", "dx", "dy", None), P("dx", "dy", None), P(None, "dx", "dy", None))
    out_specs = P(None, None, ("blk", "dx", "dy"), None)
    return jax.shard_map(
        on_device, mesh=mesh, in_specs=in_specs, out_specs=out_specs, check_vma=False
    )
```

```python
import functools
import math

import jax
import jax.numpy as jnp
from jax import lax
from jax.experimental import pallas as pl
from jax.experimental.pallas import tpu as pltpu
from jax.sharding import PartitionSpec as P

F32, BF16 = jnp.float32, jnp.bfloat16
VMEM = pl.BlockSpec(memory_space=pltpu.VMEM)
ANY = pl.BlockSpec(memory_space=pl.ANY)
LIMIT = 12 * 1024 * 1024
NT = (((1,), (1,)), ((), ()))
CHUNK = 16


def shape_of(shape, dtype):
    return jax.ShapeDtypeStruct(shape, dtype)


def shift(block, axis, distance):
    count = lax.axis_size(axis)
    return lax.ppermute(block, axis, [((i + distance) % count, i) for i in range(count)])


def both_sides(pair, axis):
    if lax.axis_size(axis) == 2:
        return shift(pair, axis, 1)
    tail, head = jnp.split(pair, 2, axis=1)
    return jnp.concatenate([shift(tail, axis, -1), shift(head, axis, 1)], axis=1)


def call(body, outs, operands, scratch=(), specs=None, out_specs=None, us=0):
    run = pl.pallas_call(
        body,
        out_shape=outs,
        in_specs=specs or [VMEM] * len(operands),
        out_specs=out_specs or [VMEM] * len(outs),
        scratch_shapes=list(scratch),
        compiler_params=pltpu.CompilerParams(vmem_limit_bytes=LIMIT),
        cost_estimate=pl.CostEstimate(
            flops=0, bytes_accessed=int(us * 3e6), transcendentals=0
        ),
    )
    return list(run(*operands))


def thirds(value):
    high = value.astype(BF16).astype(F32)
    middle = (value - high).astype(BF16).astype(F32)
    return high, middle, value - high - middle


def edges(psi, coupling, grad, hx, hy, tmp, *, shape):
    wx, wy, wz = shape
    layer, line = wy * wz, wx * wz
    for side, (x, y) in enumerate(((wx - 1, wy - 1), (0, 0))):
        to_x, to_y = side * (layer + wz), side * (line + wz)
        hx[:, to_x : to_x + layer] = psi[:, x * layer : (x + 1) * layer]
        for i in range(wx):
            at = i * layer + y * wz
            hy[:, to_y + i * wz : to_y + (i + 1) * wz] = psi[:, at : at + wz]
        for k in range(3):
            for n, third in enumerate(thirds(coupling[x] * grad[k, x])):
                tmp[(3 * k + n) * wy : (3 * k + n + 1) * wy] = third
        hx[: tmp.shape[0], to_x + layer : to_x + layer + wz] = tmp[...].astype(BF16)
        for k in range(3):
            for n, third in enumerate(thirds(coupling[:, y] * grad[k, :, y])):
                tmp[(3 * k + n) * wx : (3 * k + n + 1) * wx] = third
        hy[: tmp.shape[0], to_y + line : to_y + line + wz] = tmp[...].astype(BF16)


def operators(layers, psi, hx, hy, coupling, grad, u, w, half, back, ahead, tmp, ex, ey, *, shape):
    wx, wy, wz = shape
    layer, line = wy * wz, wx * wz
    states = psi.shape[0]
    half[...] = 0.5 * (coupling[...][None] * grad[...])
    for ref, to, length, count in ((hx, ex, layer, wy), (hy, ey, line, wx)):
        if ref is None:
            continue
        for side in range(2):
            at = side * (length + wz) + length
            tmp[...] = ref[: tmp.shape[0], at : at + wz].astype(F32)
            for k in range(3):
                third = [tmp[(3 * k + n) * count : (3 * k + n + 1) * count] for n in range(3)]
                to[side, k] = 0.5 * (third[0] + third[1] + third[2])
    for k in range(3):
        for x in layers:
            back[k, x] = pltpu.roll(half[k, x], 1, 1)
            ahead[k, x] = pltpu.roll(half[k, x], wz - 1, 1)

    def coeff(k, x, y):
        if x < 0 or x >= wx:
            return ex[int(x >= wx), k, y : y + 1, :]
        if y < 0 or y >= wy:
            return ey[int(y >= wy), k, x : x + 1, :]
        return half[k, x, y : y + 1, :]

    def group(step, _):
        r = pl.ds(pl.multiple_of(step * CHUNK, CHUNK), CHUNK)

        def field(x, y):
            if x < 0:
                ref, at = hx, y * wz
            elif x >= wx:
                ref, at = hx, layer + wz + y * wz
            elif y < 0:
                ref, at = hy, x * wz
            elif y >= wy:
                ref, at = hy, line + wz + x * wz
            else:
                ref, at = psi, x * layer + y * wz
            return ref[r, at : at + wz].astype(F32)

        for n, x in enumerate(layers):
            for y in range(wy):
                here = field(x, y)
                xb, xa = field(x - 1, y), field(x + 1, y)
                yb, ya = field(x, y - 1), field(x, y + 1)
                zb, za = pltpu.roll(here, 1, 1), pltpu.roll(here, wz - 1, 1)
                gx, gy, gz = xa - xb, ya - yb, za - zb
                c1, c2, c3 = [coeff(k, x, y) for k in range(3)]
                cols = slice(n * layer + y * wz, n * layer + (y + 1) * wz)

                def put(ref, k, value):
                    place = pl.ds(pl.multiple_of(k * states + step * CHUNK, CHUNK), CHUNK)
                    ref[place, cols] = value.astype(BF16)

                put(u, 0, c2 * gz - c3 * gy)
                put(u, 1, c3 * gx - c1 * gz)
                put(u, 2, c1 * gy - c2 * gx)

                def dx(k):
                    return coeff(k, x + 1, y) * xa - coeff(k, x - 1, y) * xb

                def dy(k):
                    return coeff(k, x, y + 1) * ya - coeff(k, x, y - 1) * yb

                def dz(k):
                    return ahead[k, x, y : y + 1, :] * za - back[k, x, y : y + 1, :] * zb

                put(w, 0, dy(2) - dz(1))
                put(w, 1, dz(0) - dx(2))
                put(w, 2, dx(1) - dy(0))
        return 0

    lax.fori_loop(0, states // CHUNK, group, 0)


def inner(psi, hy, coupling, grad, u, w, half, back, ahead, tmp, ey, *, shape):
    layers = range(1, shape[0] - 1)
    operators(
        layers, psi, None, hy, coupling, grad, u, w, half, back, ahead, tmp, None, ey, shape=shape
    )


def outer(psi, hx, hy, coupling, grad, u_inner, w_inner, u, w, *scratch, shape):
    operators((0, shape[0] - 1), psi, hx, hy, coupling, grad, u, w, *scratch, shape=shape)


def product(a_inner, a_outer, panel, layer, flip):
    cells = panel.shape[1]
    last = a_outer.shape[1] - layer
    pairs = (
        (a_inner[...], panel[:, layer : cells - layer]),
        (a_outer[:, :layer], panel[:, :layer]),
        (a_outer[:, last:], panel[:, cells - layer :]),
    )
    total = 0.0
    for a, b in pairs:
        a, b = (b, a) if flip else (a, b)
        total = total + lax.dot_general(a, b, NT, preferred_element_type=F32)
    return total


def own_tiles(u_inner, u_outer, w_inner, w_outer, psi, here, *, layer, scale):
    here[...] = product(u_inner, u_outer, psi, layer, False) * scale


def choose(two, psi, out, sem):
    core = lax.rem(lax.axis_index("blk"), 2)

    @pl.when(core == 1)
    def _():
        copy = pltpu.make_async_copy(two, out, sem)
        copy.start()
        copy.wait()

    @pl.when(core != 1)
    def _():
        copy = pltpu.make_async_copy(psi, out, sem)
        copy.start()
        copy.wait()


def tiles(u_inner, u_outer, w_inner, w_outer, panel, here, there, *, layer, scale):
    here[...] = product(u_inner, u_outer, panel, layer, False) * scale
    there[...] = product(w_inner, w_outer, panel, layer, True) * scale


def tiles_and_pieces(
    u_inner, u_outer, w_inner, w_outer, panel, own, here_two, there_two, *rest,
    layer, plane, scale
):
    keep, sends, here, there = rest
    tiles(u_inner, u_outer, w_inner, w_outer, panel, here, there, layer=layer, scale=scale)
    states = panel.shape[0]
    places = math.prod(plane)
    rows = states // places
    me = lax.axis_index("dx") * plane[1] + lax.axis_index("dy")
    for ref, dest in [(keep, me)] + [(sends.at[d], d) for d in range(places)]:
        for k in range(3):
            place = pl.ds(pl.multiple_of(k * states + dest * rows, rows), rows)
            for t, tile in enumerate((here_two, here, own)):
                ref[t, k] = tile[place, :].astype(ref.dtype)
            place = pl.ds(pl.multiple_of(dest * rows, rows), rows)
            for t, tile in ((3, there), (4, there_two)):
                ref[t, k] = tile[place, k * states : (k + 1) * states].astype(ref.dtype)


def total_of(keep, parts, t, k):
    me = lax.axis_index("dx") * lax.axis_size("dy") + lax.axis_index("dy")
    total = keep[t, k]
    for d in range(parts.shape[0]):
        total = total + jnp.where(d == me, 0.0, parts[d, t, k].astype(F32))
    return total


def add(keep, parts, one, two):
    for k in range(3):
        one[k] = total_of(keep, parts, 3, k)
        two[k] = total_of(keep, parts, 4, k)


def assemble(keep, parts, from_one, from_two, out):
    for k in range(3):
        for t in range(3):
            out[k, t] = total_of(keep, parts, t, k)
        out[k, 3] = from_one[k]
        out[k, 4] = from_two[k]


def on_device(orbitals, coupling, pot_grad):
    states, wx, wy, wz = orbitals.shape
    shape = (wx, wy, wz)
    plane = (lax.axis_size("dx"), lax.axis_size("dy"))
    places = math.prod(plane)
    rows = states // places
    layer, line = wy * wz, wx * wz
    cells = wx * layer
    scale = 1.0 / math.sqrt(cells * places)

    psi = lax.optimization_barrier(orbitals.reshape(states, cells))
    two = shift(psi, "blk", -2)

    spill = -(-9 * max(wx, wy) // 16) * 16
    tmp = pltpu.VMEM((spill, wz), F32)
    hx, hy = call(
        functools.partial(edges, shape=shape),
        [
            shape_of((states, 2 * (layer + wz)), BF16),
            shape_of((states, 2 * (line + wz)), BF16),
        ],
        [psi, coupling, pot_grad],
        scratch=[tmp],
    )
    hx, hy = both_sides(hx, "dx"), both_sides(hy, "dy")

    coeffs = pltpu.VMEM((3, wx, wy, wz), F32)
    ex, ey = pltpu.VMEM((2, 3, wy, wz), F32), pltpu.VMEM((2, 3, wx, wz), F32)
    field = shape_of((3 * states, cells - 2 * layer), BF16)
    u_inner, w_inner = call(
        functools.partial(inner, shape=shape),
        [field, field],
        [psi, hy, coupling, pot_grad],
        scratch=[coeffs] * 3 + [tmp, ey],
        us=2,
    )
    field = shape_of((3 * states, 2 * layer), BF16)
    u_outer, w_outer = call(
        functools.partial(outer, shape=shape),
        [field, field],
        [psi, hx, hy, coupling, pot_grad, u_inner, w_inner],
        scratch=[coeffs] * 3 + [tmp, ex, ey],
    )
    operands = [u_inner, u_outer, w_inner, w_outer]
    tall, wide = shape_of((3 * states, states), F32), shape_of((states, 3 * states), F32)
    (own,) = call(
        functools.partial(own_tiles, layer=layer, scale=scale), [tall], [*operands, psi]
    )

    two, own = lax.optimization_barrier((two, own))
    (mixed,) = call(
        choose,
        [shape_of((states, cells), BF16)],
        [two, psi],
        scratch=[pltpu.SemaphoreType.DMA],
        specs=[ANY, ANY],
        out_specs=[ANY],
    )
    swap = [(i, i ^ 1) for i in range(lax.axis_size("blk"))]
    one = lax.ppermute(mixed, "blk", swap)
    far = call(
        functools.partial(tiles, layer=layer, scale=scale),
        [tall, wide],
        [*operands, two],
        us=1,
    )
    one, far = lax.optimization_barrier((one, far))
    pieces = (5, 3, rows, states)
    keep, sends = call(
        functools.partial(tiles_and_pieces, layer=layer, plane=plane, scale=scale),
        [shape_of(pieces, F32), shape_of((places, *pieces), BF16)],
        [*operands, one, own, *far],
        scratch=[pltpu.VMEM(tall.shape, F32), pltpu.VMEM(wide.shape, F32)],
        us=1,
    )
    parts = lax.all_to_all(sends, ("dx", "dy"), 0, 0)
    from_one, from_two = call(add, [shape_of(pieces[1:], F32)] * 2, [keep, parts])
    from_one, from_two = shift(from_one, "blk", 1), shift(from_two, "blk", 2)
    (out,) = call(
        assemble,
        [shape_of((3, 5, rows, states), F32)],
        [keep, parts, from_one, from_two],
    )
    return out


def solution(mesh):
    in_specs = (P("blk", "dx", "dy", None), P("dx", "dy", None), P(None, "dx", "dy", None))
    out_specs = P(None, None, ("blk", "dx", "dy"), None)
    return jax.shard_map(
        on_device, mesh=mesh, in_specs=in_specs, out_specs=out_specs, check_vma=False
    )
```

```python
import functools
import math

import jax
import jax.numpy as jnp
from jax import lax
from jax.experimental import pallas as pl
from jax.experimental.pallas import tpu as pltpu
from jax.sharding import PartitionSpec as P

F32, BF16 = jnp.float32, jnp.bfloat16
VMEM = pl.BlockSpec(memory_space=pltpu.VMEM)
ANY = pl.BlockSpec(memory_space=pl.ANY)
LIMIT = 12 * 1024 * 1024
NT = (((1,), (1,)), ((), ()))
CHUNK = 16
PIECES = 2


def shape_of(shape, dtype):
    return jax.ShapeDtypeStruct(shape, dtype)


def shift(block, axis, distance):
    count = lax.axis_size(axis)
    return lax.ppermute(block, axis, [((i + distance) % count, i) for i in range(count)])


def both_sides(pair, axis):
    if lax.axis_size(axis) == 2:
        return shift(pair, axis, 1)
    tail, head = jnp.split(pair, 2, axis=1)
    return jnp.concatenate([shift(tail, axis, -1), shift(head, axis, 1)], axis=1)


def exchange(sends):
    nx, ny = lax.axis_size("dx"), lax.axis_size("dy")
    got = []
    for o, piece in enumerate(sends, 1):
        ox, oy = o // ny, o % ny
        route = [
            (i * ny + j, ((i + ox) % nx) * ny + (j + oy) % ny) for i in range(nx) for j in range(ny)
        ]
        got.append(lax.ppermute(piece, ("dx", "dy"), route))
    return got


def call(body, outs, operands, scratch=(), specs=None, out_specs=None, us=0):
    run = pl.pallas_call(
        body,
        out_shape=outs,
        in_specs=specs or [VMEM] * len(operands),
        out_specs=out_specs or [VMEM] * len(outs),
        scratch_shapes=list(scratch),
        compiler_params=pltpu.CompilerParams(vmem_limit_bytes=LIMIT),
        cost_estimate=pl.CostEstimate(
            flops=0, bytes_accessed=int(us * 3e6), transcendentals=0
        ),
    )
    return list(run(*operands))


def destinations(nx, ny):
    x, y = lax.axis_index("dx"), lax.axis_index("dy")
    return [
        lax.rem(x + ox, nx) * ny + lax.rem(y + oy, ny) for ox in range(nx) for oy in range(ny)
    ]


def thirds(value):
    high = value.astype(BF16).astype(F32)
    middle = (value - high).astype(BF16).astype(F32)
    return high, middle, value - high - middle


def edges(*refs, shape):
    pieces, (coupling, grad, tail, head, hy, tmp) = refs[:-6], refs[-6:]
    wx, wy, wz = shape
    layer, line = wy * wz, wx * wz
    for side, (x, y, hx) in enumerate(((wx - 1, wy - 1, tail), (0, 0, head))):
        to_y = side * (line + wz)
        end = 0
        for psi in pieces:
            r = slice(end, end + psi.shape[0])
            end = r.stop
            hx[r, :layer] = psi[:, x * layer : (x + 1) * layer]
            for i in range(wx):
                at = i * layer + y * wz
                hy[r, to_y + i * wz : to_y + (i + 1) * wz] = psi[:, at : at + wz]
        for k in range(3):
            for n, third in enumerate(thirds(coupling[x] * grad[k, x])):
                tmp[(3 * k + n) * wy : (3 * k + n + 1) * wy] = third
        hx[: tmp.shape[0], layer:] = tmp[...].astype(BF16)
        for k in range(3):
            for n, third in enumerate(thirds(coupling[:, y] * grad[k, :, y])):
                tmp[(3 * k + n) * wx : (3 * k + n + 1) * wx] = third
        hy[: tmp.shape[0], to_y + line : to_y + line + wz] = tmp[...].astype(BF16)


def operators(*refs, layers, shape):
    pieces, refs = refs[:PIECES], refs[PIECES:]
    outer = len(refs) == 12
    hx = refs[0] if outer else None
    hy, coupling, grad, u, w, half, back, ahead, tmp, ex, ey = refs[-11:]
    wx, wy, wz = shape
    layer, line = wy * wz, wx * wz
    states = sum(psi.shape[0] for psi in pieces)
    half[...] = 0.5 * (coupling[...][None] * grad[...])

    def unpack(ref, at, to, count):
        tmp[...] = ref[: tmp.shape[0], at : at + wz].astype(F32)
        for k in range(3):
            third = [tmp[(3 * k + n) * count : (3 * k + n + 1) * count] for n in range(3)]
            to[k] = 0.5 * (third[0] + third[1] + third[2])

    if outer:
        unpack(hx, layer, ex, wy)
    for side in range(2):
        unpack(hy, side * (line + wz) + line, ey.at[side], wx)
    for k in range(3):
        for x in layers:
            back[k, x] = pltpu.roll(half[k, x], 1, 1)
            ahead[k, x] = pltpu.roll(half[k, x], wz - 1, 1)

    def coeff(k, x, y):
        if x < 0 or x >= wx:
            return ex[k, y : y + 1, :]
        if y < 0 or y >= wy:
            return ey[int(y >= wy), k, x : x + 1, :]
        return half[k, x, y : y + 1, :]

    def group(psi, start, step, _):
        own = pl.ds(pl.multiple_of(step * CHUNK, CHUNK), CHUNK)
        first = start + step * CHUNK
        r = pl.ds(pl.multiple_of(first, CHUNK), CHUNK)

        def field(x, y):
            if x < 0 or x >= wx:
                return hx[r, y * wz : (y + 1) * wz].astype(F32)
            if y < 0 or y >= wy:
                at = int(y >= wy) * (line + wz) + x * wz
                return hy[r, at : at + wz].astype(F32)
            at = x * layer + y * wz
            return psi[own, at : at + wz].astype(F32)

        for n, x in enumerate(layers):
            for y in range(wy):
                here = field(x, y)
                xb, xa = field(x - 1, y), field(x + 1, y)
                yb, ya = field(x, y - 1), field(x, y + 1)
                zb, za = pltpu.roll(here, 1, 1), pltpu.roll(here, wz - 1, 1)
                gx, gy, gz = xa - xb, ya - yb, za - zb
                c1, c2, c3 = [coeff(k, x, y) for k in range(3)]
                cols = slice(n * layer + y * wz, n * layer + (y + 1) * wz)

                def put(ref, k, value):
                    place = pl.ds(pl.multiple_of(k * states + first, CHUNK), CHUNK)
                    ref[place, cols] = value.astype(BF16)

                put(u, 0, c2 * gz - c3 * gy)
                put(u, 1, c3 * gx - c1 * gz)
                put(u, 2, c1 * gy - c2 * gx)

                def dx(k):
                    return coeff(k, x + 1, y) * xa - coeff(k, x - 1, y) * xb

                def dy(k):
                    return coeff(k, x, y + 1) * ya - coeff(k, x, y - 1) * yb

                def dz(k):
                    return ahead[k, x, y : y + 1, :] * za - back[k, x, y : y + 1, :] * zb

                put(w, 0, dy(2) - dz(1))
                put(w, 1, dz(0) - dx(2))
                put(w, 2, dx(1) - dy(0))
        return 0

    end = 0
    for psi in pieces:
        lax.fori_loop(0, psi.shape[0] // CHUNK, functools.partial(group, psi, end), 0)
        end += psi.shape[0]


def product(fields, panel, layer, flip=False):
    inner, left, right = fields
    cells = inner.shape[1] + 2 * layer
    total = 0.0
    for a, start, stop in (
        (inner, layer, cells - layer), (left, 0, layer), (right, cells - layer, cells)
    ):
        a, b = a[...], panel(slice(start, stop))
        a, b = (b, a) if flip else (a, b)
        total = total + lax.dot_general(a, b, NT, preferred_element_type=F32)
    return total


def stacked(*pieces):
    def rows(cols):
        values = []
        for piece in pieces:
            if isinstance(piece, int):
                piece = jnp.zeros((piece, cols.stop - cols.start), BF16)
            else:
                piece = piece[:, cols]
            if piece.shape[0]:
                values.append(piece)
        return jnp.concatenate(values, axis=0)

    return rows


def own_tiles(*refs, layer, scale):
    fields, pieces, here = refs[:3], refs[3:-1], refs[-1]
    here[...] = product(fields, stacked(*pieces), layer) * scale


def choose(two, psi, out, sem):
    core = lax.rem(lax.axis_index("blk"), 2)

    @pl.when(core == 1)
    def _():
        copy = pltpu.make_async_copy(two, out, sem)
        copy.start()
        copy.wait()

    @pl.when(core != 1)
    def _():
        copy = pltpu.make_async_copy(psi, out, sem)
        copy.start()
        copy.wait()


def tiles(*refs, before, layer, scale):
    u, w, (two, one, here, there) = refs[:3], refs[3:6], refs[6:]
    states = here.shape[0] // 3
    after = states - before - two.shape[0]
    both = stacked(before, two, after, before, one, after)
    here[...] = product(u, both, layer) * scale
    both = product(w, stacked(two, one), layer, True) * scale
    there[0] = both[: two.shape[0]]
    there[1] = both[two.shape[0] :]


def tiles_and_pieces(*refs, before, layer, plane, scale):
    (own, here_first, there_first), rest = refs[8:11], refs[11:]
    outs, (here, there) = rest[:-2], rest[-2:]
    tiles(*refs[:8], here, there.at[:, before:], before=before, layer=layer, scale=scale)
    here[...] += here_first[...]
    there[:, :before] = there_first[...]
    states = here.shape[0] // 3
    rows = states // math.prod(plane)
    for ref, dest in zip(outs, destinations(*plane)):
        for k in range(3):
            place = pl.ds(pl.multiple_of(k * states + dest * rows, rows), rows)
            ref[0, k] = here[place, :states].astype(ref.dtype)
            ref[1, k] = here[place, states:].astype(ref.dtype)
            ref[2, k] = own[place, :].astype(ref.dtype)
            place = pl.ds(pl.multiple_of(dest * rows, rows), rows)
            cols = slice(k * states, (k + 1) * states)
            ref[3, k] = there[1, place, cols].astype(ref.dtype)
            ref[4, k] = there[0, place, cols].astype(ref.dtype)


def add(keep, *rest):
    parts, (one, two) = rest[:-2], rest[-2:]
    for t, ref in ((3, one), (4, two)):
        total = keep[t]
        for part in parts:
            total = total + part[t].astype(F32)
        ref[...] = total


def assemble(keep, *rest):
    parts, (from_one, from_two, out) = rest[:-3], rest[-3:]
    for k in range(3):
        for t in range(3):
            total = keep[t, k]
            for part in parts:
                total = total + part[t, k].astype(F32)
            out[k, t] = total
        out[k, 3] = from_one[k]
        out[k, 4] = from_two[k]


def on_device(orbitals, coupling, pot_grad):
    states, wx, wy, wz = orbitals.shape
    shape = (wx, wy, wz)
    plane = (lax.axis_size("dx"), lax.axis_size("dy"))
    places = math.prod(plane)
    rows = states // places
    layer, line = wy * wz, wx * wz
    cells = wx * layer
    scale = 1.0 / math.sqrt(cells * places)

    before = states * 3 // 8 // CHUNK * CHUNK
    psi = []
    for piece in jnp.split(orbitals, [before], axis=0):
        psi.append(lax.optimization_barrier(piece.reshape(piece.shape[0], cells)))
    two = [shift(piece, "blk", -2) for piece in psi]

    tmp = pltpu.VMEM((-(-9 * max(wx, wy) // 16) * 16, wz), F32)
    tail, head, hy = call(
        functools.partial(edges, shape=shape),
        [shape_of((states, layer + wz), BF16)] * 2 + [shape_of((states, 2 * (line + wz)), BF16)],
        [*psi, coupling, pot_grad],
        scratch=[tmp],
    )
    from_left, from_right = shift(tail, "dx", -1), shift(head, "dx", 1)
    hy = both_sides(hy, "dy")

    coeffs = pltpu.VMEM((3, wx, wy, wz), F32)
    ends = [pltpu.VMEM((3, wy, wz), F32), pltpu.VMEM((2, 3, wx, wz), F32)]
    u, w = [], []
    for layers, hx in (
        (range(1, wx - 1), []), ((0,), [from_left]), ((wx - 1,), [from_right])
    ):
        field = shape_of((3 * states, len(layers) * layer), BF16)
        results = call(
            functools.partial(operators, layers=layers, shape=shape),
            [field, field],
            [*psi, *hx, hy, coupling, pot_grad],
            scratch=[coeffs] * 3 + [tmp, *ends],
        )
        u.append(results[0])
        w.append(results[1])
    tall = shape_of((3 * states, states), F32)
    (own,) = call(
        functools.partial(own_tiles, layer=layer, scale=scale), [tall], [*u, *psi]
    )

    swap = [(i, i ^ 1) for i in range(lax.axis_size("blk"))]

    def swapped(n):
        (mixed,) = call(
            choose,
            [shape_of(psi[n].shape, BF16)],
            [two[n], psi[n]],
            scratch=[pltpu.SemaphoreType.DMA],
            specs=[ANY, ANY],
            out_specs=[ANY],
        )
        return lax.ppermute(mixed, "blk", swap)

    both_here = (3 * states, 2 * states)
    two[0], u = lax.optimization_barrier((two[0], u))
    one = [swapped(0)]
    one[0], own = lax.optimization_barrier((one[0], own))
    first = call(
        functools.partial(tiles, before=0, layer=layer, scale=scale),
        [shape_of(both_here, F32), shape_of((2, before, 3 * states), F32)],
        [*u, *w, two[0], one[0]],
    )
    two[1], first[0] = lax.optimization_barrier((two[1], first[0]))
    one.append(swapped(1))
    pieces = (5, 3, rows, states)
    keep, *sends = call(
        functools.partial(tiles_and_pieces, before=before, layer=layer, plane=plane, scale=scale),
        [shape_of(pieces, F32)] + [shape_of(pieces, BF16)] * (places - 1),
        [*u, *w, two[1], one[1], own, *first],
        scratch=[pltpu.VMEM(both_here, F32), pltpu.VMEM((2, states, 3 * states), F32)],
    )
    parts = exchange(sends)
    from_one, from_two = call(add, [shape_of(pieces[1:], F32)] * 2, [keep, *parts])
    from_one, from_two = shift(from_one, "blk", 1), shift(from_two, "blk", 2)
    (out,) = call(
        assemble,
        [shape_of((3, 5, rows, states), F32)],
        [keep, *parts, from_one, from_two],
    )
    return out


def solution(mesh):
    in_specs = (P("blk", "dx", "dy", None), P("dx", "dy", None), P(None, "dx", "dy", None))
    out_specs = P(None, None, ("blk", "dx", "dy"), None)
    return jax.shard_map(
        on_device, mesh=mesh, in_specs=in_specs, out_specs=out_specs, check_vma=False
    )
```

```python
import functools
import math

import jax
import jax.numpy as jnp
from jax import lax
from jax.experimental import pallas as pl
from jax.experimental.pallas import tpu as pltpu
from jax.sharding import PartitionSpec as P

F32, BF16 = jnp.float32, jnp.bfloat16
VMEM = pl.BlockSpec(memory_space=pltpu.VMEM)
ANY = pl.BlockSpec(memory_space=pl.ANY)
LIMIT = 12 * 1024 * 1024
NT = (((1,), (1,)), ((), ()))
CHUNK = 16
PIECES = 2


def shape_of(shape, dtype):
    return jax.ShapeDtypeStruct(shape, dtype)


def shift(block, axis, distance):
    count = lax.axis_size(axis)
    return lax.ppermute(block, axis, [((i + distance) % count, i) for i in range(count)])


def both_sides(pair, axis):
    if lax.axis_size(axis) == 2:
        return shift(pair, axis, 1)
    tail, head = jnp.split(pair, 2, axis=1)
    return jnp.concatenate([shift(tail, axis, -1), shift(head, axis, 1)], axis=1)


def exchange(sends):
    nx, ny = lax.axis_size("dx"), lax.axis_size("dy")
    got = []
    for o, piece in enumerate(sends, 1):
        ox, oy = o // ny, o % ny
        route = [
            (i * ny + j, ((i + ox) % nx) * ny + (j + oy) % ny) for i in range(nx) for j in range(ny)
        ]
        got.append(lax.ppermute(piece, ("dx", "dy"), route))
    return got


def call(body, outs, operands, scratch=(), specs=None, out_specs=None, us=0):
    run = pl.pallas_call(
        body,
        out_shape=outs,
        in_specs=specs or [VMEM] * len(operands),
        out_specs=out_specs or [VMEM] * len(outs),
        scratch_shapes=list(scratch),
        compiler_params=pltpu.CompilerParams(vmem_limit_bytes=LIMIT),
        cost_estimate=pl.CostEstimate(
            flops=0, bytes_accessed=int(us * 3e6), transcendentals=0
        ),
    )
    return list(run(*operands))


def destinations(nx, ny):
    x, y = lax.axis_index("dx"), lax.axis_index("dy")
    return [
        lax.rem(x + ox, nx) * ny + lax.rem(y + oy, ny) for ox in range(nx) for oy in range(ny)
    ]


def thirds(value):
    high = value.astype(BF16).astype(F32)
    middle = (value - high).astype(BF16).astype(F32)
    return high, middle, value - high - middle


def edges(*refs, shape):
    pieces, (coupling, grad, tail, head, hy, tmp) = refs[:-6], refs[-6:]
    wx, wy, wz = shape
    layer, line = wy * wz, wx * wz
    for side, (x, y, hx) in enumerate(((wx - 1, wy - 1, tail), (0, 0, head))):
        to_y = side * (line + wz)
        end = 0
        for psi in pieces:
            r = slice(end, end + psi.shape[0])
            end = r.stop
            hx[r, :layer] = psi[:, x * layer : (x + 1) * layer]
            for i in range(wx):
                at = i * layer + y * wz
                hy[r, to_y + i * wz : to_y + (i + 1) * wz] = psi[:, at : at + wz]
        for k in range(3):
            for n, third in enumerate(thirds(coupling[x] * grad[k, x])):
                tmp[(3 * k + n) * wy : (3 * k + n + 1) * wy] = third
        hx[: tmp.shape[0], layer:] = tmp[...].astype(BF16)
        for k in range(3):
            for n, third in enumerate(thirds(coupling[:, y] * grad[k, :, y])):
                tmp[(3 * k + n) * wx : (3 * k + n + 1) * wx] = third
        hy[: tmp.shape[0], to_y + line : to_y + line + wz] = tmp[...].astype(BF16)


def operators(*refs, layers, shape):
    pieces, refs = refs[:PIECES], refs[PIECES:]
    outer = len(refs) == 12
    hx = refs[0] if outer else None
    hy, coupling, grad, u, w, half, back, ahead, tmp, ex, ey = refs[-11:]
    wx, wy, wz = shape
    layer, line = wy * wz, wx * wz
    states = sum(psi.shape[0] for psi in pieces)
    half[...] = 0.5 * (coupling[...][None] * grad[...])

    def unpack(ref, at, to, count):
        tmp[...] = ref[: tmp.shape[0], at : at + wz].astype(F32)
        for k in range(3):
            third = [tmp[(3 * k + n) * count : (3 * k + n + 1) * count] for n in range(3)]
            to[k] = 0.5 * (third[0] + third[1] + third[2])

    if outer:
        unpack(hx, layer, ex, wy)
    for side in range(2):
        unpack(hy, side * (line + wz) + line, ey.at[side], wx)
    for k in range(3):
        for x in layers:
            back[k, x] = pltpu.roll(half[k, x], 1, 1)
            ahead[k, x] = pltpu.roll(half[k, x], wz - 1, 1)

    def coeff(k, x, y):
        if x < 0 or x >= wx:
            return ex[k, y : y + 1, :]
        if y < 0 or y >= wy:
            return ey[int(y >= wy), k, x : x + 1, :]
        return half[k, x, y : y + 1, :]

    def group(psi, start, step, _):
        own = pl.ds(pl.multiple_of(step * CHUNK, CHUNK), CHUNK)
        first = start + step * CHUNK
        r = pl.ds(pl.multiple_of(first, CHUNK), CHUNK)

        def field(x, y):
            if x < 0 or x >= wx:
                return hx[r, y * wz : (y + 1) * wz].astype(F32)
            if y < 0 or y >= wy:
                at = int(y >= wy) * (line + wz) + x * wz
                return hy[r, at : at + wz].astype(F32)
            at = x * layer + y * wz
            return psi[own, at : at + wz].astype(F32)

        for n, x in enumerate(layers):
            for y in range(wy):
                here = field(x, y)
                xb, xa = field(x - 1, y), field(x + 1, y)
                yb, ya = field(x, y - 1), field(x, y + 1)
                zb, za = pltpu.roll(here, 1, 1), pltpu.roll(here, wz - 1, 1)
                gx, gy, gz = xa - xb, ya - yb, za - zb
                c1, c2, c3 = [coeff(k, x, y) for k in range(3)]
                cols = slice(n * layer + y * wz, n * layer + (y + 1) * wz)

                def put(ref, k, value):
                    place = pl.ds(pl.multiple_of(k * states + first, CHUNK), CHUNK)
                    ref[place, cols] = value.astype(BF16)

                put(u, 0, c2 * gz - c3 * gy)
                put(u, 1, c3 * gx - c1 * gz)
                put(u, 2, c1 * gy - c2 * gx)

                def dx(k):
                    return coeff(k, x + 1, y) * xa - coeff(k, x - 1, y) * xb

                def dy(k):
                    return coeff(k, x, y + 1) * ya - coeff(k, x, y - 1) * yb

                def dz(k):
                    return ahead[k, x, y : y + 1, :] * za - back[k, x, y : y + 1, :] * zb

                put(w, 0, dy(2) - dz(1))
                put(w, 1, dz(0) - dx(2))
                put(w, 2, dx(1) - dy(0))
        return 0

    end = 0
    for psi in pieces:
        lax.fori_loop(0, psi.shape[0] // CHUNK, functools.partial(group, psi, end), 0)
        end += psi.shape[0]


def product(fields, panel, layer, flip=False):
    inner, left, right = fields
    cells = inner.shape[1] + 2 * layer
    total = 0.0
    for a, start, stop in (
        (inner, layer, cells - layer), (left, 0, layer), (right, cells - layer, cells)
    ):
        a, b = a[...], panel(slice(start, stop))
        a, b = (b, a) if flip else (a, b)
        total = total + lax.dot_general(a, b, NT, preferred_element_type=F32)
    return total


def stacked(*pieces):
    def rows(cols):
        values = []
        for piece in pieces:
            if isinstance(piece, int):
                piece = jnp.zeros((piece, cols.stop - cols.start), BF16)
            else:
                piece = piece[:, cols]
            if piece.shape[0]:
                values.append(piece)
        return jnp.concatenate(values, axis=0)

    return rows


def own_tiles(*refs, layer, scale):
    fields, pieces, here = refs[:3], refs[3:-1], refs[-1]
    here[...] = product(fields, stacked(*pieces), layer) * scale


def choose(two, psi, out, sem):
    core = lax.rem(lax.axis_index("blk"), 2)

    @pl.when(core == 1)
    def _():
        copy = pltpu.make_async_copy(two, out, sem)
        copy.start()
        copy.wait()

    @pl.when(core != 1)
    def _():
        copy = pltpu.make_async_copy(psi, out, sem)
        copy.start()
        copy.wait()


def tiles(*refs, before, layer, scale):
    u, w, (panel, here, there) = refs[:3], refs[3:6], refs[6:]
    states = here.shape[0] // 3
    after = states - before - panel.shape[0]
    here[...] = product(u, stacked(before, panel, after), layer) * scale
    there[...] = product(w, stacked(panel), layer, True) * scale


def both_tiles(*refs, before, layer, scale):
    fields, (two, one), outs = refs[:6], refs[6:8], refs[8:]
    here_two, there_two, here_one, there_one = outs
    states = here_two.shape[0] // 3
    height = two.shape[0]
    after = states - before - height
    both = stacked(before, two, after, before, one, after)
    here = product(fields[:3], both, layer) * scale
    here_two[...], here_one[...] = here[:, :states], here[:, states:]
    there = product(fields[3:], stacked(two, one), layer, True) * scale
    there_two[...], there_one[...] = there[:height], there[height:]


def tiles_and_pieces(*refs, before, layer, plane, scale, with_own):
    here_first, there_first, *rest = refs[7:]
    own = [rest.pop(0)] if with_own else []
    outs, (here, there) = rest[:-2], rest[-2:]
    tiles(*refs[:7], here, there.at[before:], before=before, layer=layer, scale=scale)
    here[...] += here_first[...]
    there[:before] = there_first[...]
    states = here.shape[0] // 3
    rows = states // math.prod(plane)
    for ref, dest in zip(outs, destinations(*plane)):
        for k in range(3):
            place = pl.ds(pl.multiple_of(k * states + dest * rows, rows), rows)
            for t, tile in enumerate((here, *own)):
                ref[t, k] = tile[place, :].astype(ref.dtype)
            place = pl.ds(pl.multiple_of(dest * rows, rows), rows)
            cols = slice(k * states, (k + 1) * states)
            ref[len(own) + 1, k] = there[place, cols].astype(ref.dtype)


def add(keep, *rest):
    parts, out = rest[:-1], rest[-1]
    total = keep[keep.shape[0] - 1]
    for part in parts:
        total = total + part[keep.shape[0] - 1].astype(F32)
    out[...] = total


def assemble(*refs):
    from_one, from_two, out = refs[-3:]
    size = (len(refs) - 3) // 2
    for k in range(3):
        for t, group, n in ((0, refs[:size], 0), (1, refs[size:-3], 0), (2, refs[:size], 1)):
            total = group[0][n, k]
            for part in group[1:]:
                total = total + part[n, k].astype(F32)
            out[k, t] = total
        out[k, 3] = from_one[k]
        out[k, 4] = from_two[k]


def fetch(whole, piece, sem):
    copy = pltpu.make_async_copy(whole.at[pl.ds(0, piece.shape[0])], piece, sem)
    copy.start()
    copy.wait()


def on_device(orbitals, coupling, pot_grad):
    states, wx, wy, wz = orbitals.shape
    shape = (wx, wy, wz)
    plane = (lax.axis_size("dx"), lax.axis_size("dy"))
    places = math.prod(plane)
    rows = states // places
    layer, line = wy * wz, wx * wz
    cells = wx * layer
    scale = 1.0 / math.sqrt(cells * places)

    before = states * 3 // 8 // CHUNK * CHUNK
    (first,) = call(
        fetch,
        [shape_of((before, wx, wy, wz), BF16)],
        [orbitals],
        scratch=[pltpu.SemaphoreType.DMA],
        specs=[pl.BlockSpec(memory_space=pltpu.HBM)],
    )
    psi = []
    for piece in (first, orbitals[before:]):
        psi.append(lax.optimization_barrier(piece.reshape(piece.shape[0], cells)))
    two = [shift(piece, "blk", -2) for piece in psi]

    tmp = pltpu.VMEM((-(-9 * max(wx, wy) // 16) * 16, wz), F32)
    tail, head, hy = call(
        functools.partial(edges, shape=shape),
        [shape_of((states, layer + wz), BF16)] * 2 + [shape_of((states, 2 * (line + wz)), BF16)],
        [*psi, coupling, pot_grad],
        scratch=[tmp],
    )
    from_left, from_right = shift(tail, "dx", -1), shift(head, "dx", 1)
    hy = both_sides(hy, "dy")

    coeffs = pltpu.VMEM((3, wx, wy, wz), F32)
    ends = [pltpu.VMEM((3, wy, wz), F32), pltpu.VMEM((2, 3, wx, wz), F32)]
    u, w = [], []
    for layers, hx in (
        (range(1, wx - 1), []), ((0,), [from_left]), ((wx - 1,), [from_right])
    ):
        field = shape_of((3 * states, len(layers) * layer), BF16)
        results = call(
            functools.partial(operators, layers=layers, shape=shape),
            [field, field],
            [*psi, *hx, hy, coupling, pot_grad],
            scratch=[coeffs] * 3 + [tmp, *ends],
        )
        u.append(results[0])
        w.append(results[1])
    tall = shape_of((3 * states, states), F32)
    (own,) = call(
        functools.partial(own_tiles, layer=layer, scale=scale), [tall], [*u, *psi]
    )

    swap = [(i, i ^ 1) for i in range(lax.axis_size("blk"))]

    def swapped(n):
        (mixed,) = call(
            choose,
            [shape_of(psi[n].shape, BF16)],
            [two[n], psi[n]],
            scratch=[pltpu.SemaphoreType.DMA],
            specs=[ANY, ANY],
            out_specs=[ANY],
        )
        return lax.ppermute(mixed, "blk", swap)

    wide = shape_of((before, 3 * states), F32)
    two[0], u = lax.optimization_barrier((two[0], u))
    one = [swapped(0)]
    one[0], own = lax.optimization_barrier((one[0], own))
    first = call(
        functools.partial(both_tiles, before=0, layer=layer, scale=scale),
        [tall, wide, tall, wide],
        [*u, *w, two[0], one[0]],
    )
    two[1], first[0] = lax.optimization_barrier((two[1], first[0]))
    one.append(swapped(1))

    def summed(panel, earlier, with_own):
        pieces = (2 + with_own, 3, rows, states)
        keep, *sends = call(
            functools.partial(
                tiles_and_pieces,
                before=before,
                layer=layer,
                plane=plane,
                scale=scale,
                with_own=with_own,
            ),
            [shape_of(pieces, F32)] + [shape_of(pieces, BF16)] * (places - 1),
            [*u, *w, panel, *earlier] + [own] * with_own,
            scratch=[pltpu.VMEM(tall.shape, F32), pltpu.VMEM((states, 3 * states), F32)],
            us=1,
        )
        return [keep, *exchange(sends)]

    def sent_back(group, distance):
        (total,) = call(add, [shape_of((3, rows, states), F32)], group)
        return shift(total, "blk", distance)

    group_two = summed(two[1], first[:2], True)
    one[1], group_two[0] = lax.optimization_barrier((one[1], group_two[0]))
    group_one = summed(one[1], first[2:], False)
    from_two = sent_back(group_two, 2)
    from_one = sent_back(group_one, 1)
    (out,) = call(
        assemble,
        [shape_of((3, 5, rows, states), F32)],
        [*group_two, *group_one, from_one, from_two],
    )
    return out


def solution(mesh):
    in_specs = (P("blk", "dx", "dy", None), P("dx", "dy", None), P(None, "dx", "dy", None))
    out_specs = P(None, None, ("blk", "dx", "dy"), None)
    return jax.shard_map(
        on_device, mesh=mesh, in_specs=in_specs, out_specs=out_specs, check_vma=False
    )
```

```python
import functools
import math

import jax
import jax.numpy as jnp
from jax import lax
from jax.experimental import pallas as pl
from jax.experimental.pallas import tpu as pltpu
from jax.sharding import PartitionSpec as P

F32, BF16 = jnp.float32, jnp.bfloat16
VMEM = pl.BlockSpec(memory_space=pltpu.VMEM)
ANY = pl.BlockSpec(memory_space=pl.ANY)
LIMIT = 12 * 1024 * 1024
NT = (((1,), (1,)), ((), ()))
CHUNK = 16


def shape_of(shape, dtype):
    return jax.ShapeDtypeStruct(shape, dtype)


def shift(block, axis, distance):
    count = lax.axis_size(axis)
    return lax.ppermute(block, axis, [((i + distance) % count, i) for i in range(count)])


def both_sides(pair, axis):
    if lax.axis_size(axis) == 2:
        return shift(pair, axis, 1)
    tail, head = jnp.split(pair, 2, axis=1)
    return jnp.concatenate([shift(tail, axis, -1), shift(head, axis, 1)], axis=1)


def exchange(sends):
    nx, ny = lax.axis_size("dx"), lax.axis_size("dy")
    got = []
    for o, piece in enumerate(sends, 1):
        ox, oy = o // ny, o % ny
        route = [
            (i * ny + j, ((i + ox) % nx) * ny + (j + oy) % ny) for i in range(nx) for j in range(ny)
        ]
        got.append(lax.ppermute(piece, ("dx", "dy"), route))
    return got


def call(body, outs, operands, scratch=(), specs=None, out_specs=None, us=0):
    run = pl.pallas_call(
        body,
        out_shape=outs,
        in_specs=specs or [VMEM] * len(operands),
        out_specs=out_specs or [VMEM] * len(outs),
        scratch_shapes=list(scratch),
        compiler_params=pltpu.CompilerParams(vmem_limit_bytes=LIMIT),
        cost_estimate=pl.CostEstimate(
            flops=0, bytes_accessed=int(us * 3e6), transcendentals=0
        ),
    )
    return list(run(*operands))


def destinations(nx, ny):
    x, y = lax.axis_index("dx"), lax.axis_index("dy")
    return [
        lax.rem(x + ox, nx) * ny + lax.rem(y + oy, ny) for ox in range(nx) for oy in range(ny)
    ]


def thirds(value):
    high = value.astype(BF16).astype(F32)
    middle = (value - high).astype(BF16).astype(F32)
    return high, middle, value - high - middle


def edges(psi, coupling, grad, tail, head, hy, tmp, *, shape):
    wx, wy, wz = shape
    layer, line = wy * wz, wx * wz
    for side, (x, y, hx) in enumerate(((wx - 1, wy - 1, tail), (0, 0, head))):
        to_y = side * (line + wz)
        hx[:, :layer] = psi[:, x * layer : (x + 1) * layer]
        for i in range(wx):
            at = i * layer + y * wz
            hy[:, to_y + i * wz : to_y + (i + 1) * wz] = psi[:, at : at + wz]
        for k in range(3):
            for n, third in enumerate(thirds(coupling[x] * grad[k, x])):
                tmp[(3 * k + n) * wy : (3 * k + n + 1) * wy] = third
        hx[: tmp.shape[0], layer:] = tmp[...].astype(BF16)
        for k in range(3):
            for n, third in enumerate(thirds(coupling[:, y] * grad[k, :, y])):
                tmp[(3 * k + n) * wx : (3 * k + n + 1) * wx] = third
        hy[: tmp.shape[0], to_y + line : to_y + line + wz] = tmp[...].astype(BF16)


def operators(*refs, layers, shape):
    psi, *refs = refs
    outer = len(refs) == 13
    hx = refs[:2]
    hy, coupling, grad, u, w, half, back, ahead, tmp, ex, ey = refs[-11:]
    wx, wy, wz = shape
    layer, line = wy * wz, wx * wz
    states = psi.shape[0]
    half[...] = 0.5 * (coupling[...][None] * grad[...])

    def unpack(ref, at, to, count):
        tmp[...] = ref[: tmp.shape[0], at : at + wz].astype(F32)
        for k in range(3):
            third = [tmp[(3 * k + n) * count : (3 * k + n + 1) * count] for n in range(3)]
            to[k] = 0.5 * (third[0] + third[1] + third[2])

    for side in range(2):
        if outer:
            unpack(hx[side], layer, ex.at[side], wy)
        unpack(hy, side * (line + wz) + line, ey.at[side], wx)
    for k in range(3):
        for x in layers:
            back[k, x] = pltpu.roll(half[k, x], 1, 1)
            ahead[k, x] = pltpu.roll(half[k, x], wz - 1, 1)

    def coeff(k, x, y):
        if x < 0 or x >= wx:
            return ex[int(x >= wx), k, y : y + 1, :]
        if y < 0 or y >= wy:
            return ey[int(y >= wy), k, x : x + 1, :]
        return half[k, x, y : y + 1, :]

    def group(step, _):
        r = pl.ds(pl.multiple_of(step * CHUNK, CHUNK), CHUNK)

        def field(x, y):
            if x < 0 or x >= wx:
                return hx[int(x >= wx)][r, y * wz : (y + 1) * wz].astype(F32)
            if y < 0 or y >= wy:
                at = int(y >= wy) * (line + wz) + x * wz
                return hy[r, at : at + wz].astype(F32)
            at = x * layer + y * wz
            return psi[r, at : at + wz].astype(F32)

        for n, x in enumerate(layers):
            for y in range(wy):
                here = field(x, y)
                xb, xa = field(x - 1, y), field(x + 1, y)
                yb, ya = field(x, y - 1), field(x, y + 1)
                zb, za = pltpu.roll(here, 1, 1), pltpu.roll(here, wz - 1, 1)
                gx, gy, gz = xa - xb, ya - yb, za - zb
                c1, c2, c3 = [coeff(k, x, y) for k in range(3)]
                cols = slice(n * layer + y * wz, n * layer + (y + 1) * wz)

                def put(ref, k, value):
                    place = pl.ds(pl.multiple_of(k * states + step * CHUNK, CHUNK), CHUNK)
                    ref[place, cols] = value.astype(BF16)

                put(u, 0, c2 * gz - c3 * gy)
                put(u, 1, c3 * gx - c1 * gz)
                put(u, 2, c1 * gy - c2 * gx)

                def dx(k):
                    return coeff(k, x + 1, y) * xa - coeff(k, x - 1, y) * xb

                def dy(k):
                    return coeff(k, x, y + 1) * ya - coeff(k, x, y - 1) * yb

                def dz(k):
                    return ahead[k, x, y : y + 1, :] * za - back[k, x, y : y + 1, :] * zb

                put(w, 0, dy(2) - dz(1))
                put(w, 1, dz(0) - dx(2))
                put(w, 2, dx(1) - dy(0))
        return 0

    lax.fori_loop(0, states // CHUNK, group, 0)


def product(fields, panel, layer, flip=False):
    inner, outer = fields
    cells = inner.shape[1] + outer.shape[1]
    total = 0.0
    for a, start, stop in (
        (inner[...], layer, cells - layer),
        (outer[:, :layer], 0, layer),
        (outer[:, layer:], cells - layer, cells),
    ):
        b = panel(slice(start, stop))
        a, b = (b, a) if flip else (a, b)
        total = total + lax.dot_general(a, b, NT, preferred_element_type=F32)
    return total


def stacked(*panels):
    return lambda cols: jnp.concatenate([panel[:, cols] for panel in panels], axis=0)


def own_tiles(*refs, layer, scale):
    u, (psi, own) = refs[:2], refs[2:]
    own[...] = product(u, stacked(psi), layer) * scale


def duplicate(source, target, sem):
    copy = pltpu.make_async_copy(source, target, sem)
    copy.start()
    copy.wait()


def cut(outs, slots, plane, states):
    rows = states // math.prod(plane)
    for ref, dest in zip(outs, destinations(*plane)):
        for n, slot in enumerate(slots):
            for k in range(3):
                ref[n, k] = slot(k, dest * rows, rows).astype(ref.dtype)


def tall_rows(tile):
    states = tile.shape[0] // 3

    def rows_of(k, start, rows):
        return tile[pl.ds(pl.multiple_of(k * states + start, rows), rows), :]

    return rows_of


def wide_rows(tile):
    states = tile.shape[0]

    def rows_of(k, start, rows):
        cols = slice(k * states, (k + 1) * states)
        return tile[pl.ds(pl.multiple_of(start, rows), rows), cols]

    return rows_of


def either(first, second):
    core = lax.rem(lax.axis_index("blk"), 2)
    return lambda *place: jnp.where(core == 0, first(*place), second(*place))


def there_tiles(*refs, layer, plane, scale):
    w, w_mate, (two, psi, own), refs = refs[:2], refs[2:4], refs[4:7], refs[7:]
    mate, outs, (there, there_mate) = refs[0], refs[1:-2], refs[-2:]
    states = two.shape[0]
    there[...] = product(w, stacked(two), layer, True) * scale
    both = product(w_mate, stacked(two, psi), layer, True) * scale
    there_mate[...], mate[...] = both[:states], both[states:]
    slots = (wide_rows(there), either(tall_rows(own), wide_rows(there_mate)))
    cut(outs, slots, plane, states)


def here_tiles(*refs, layer, plane, scale):
    u, (two, one, own, mate), refs = refs[:2], refs[2:6], refs[6:]
    outs, (here_two, here_one) = refs[:-2], refs[-2:]
    states = two.shape[0]
    both = product(u, stacked(two, one), layer) * scale
    here_two[...], here_one[...] = both[:, :states], both[:, states:]
    slots = (
        tall_rows(here_two), wide_rows(mate), either(tall_rows(here_one), tall_rows(own))
    )
    cut(outs, slots, plane, states)


def total_of(group, n, k):
    total = group[0][n, k]
    for part in group[1:]:
        total = total + part[n, k].astype(F32)
    return total


def add(*refs):
    group, out = refs[:-1], refs[-1]
    for n in range(out.shape[0]):
        for k in range(3):
            out[n, k] = total_of(group, n, k)


def assemble(*refs):
    group, (there, back, out) = refs[:-3], refs[-3:]
    core = lax.rem(lax.axis_index("blk"), 2)
    for k in range(3):
        mate, third = total_of(group, 1, k), total_of(group, 2, k)
        out[k, 0] = total_of(group, 0, k)
        out[k, 1] = jnp.where(core == 0, third, mate)
        out[k, 2] = jnp.where(core == 0, there[1, k], third)
        out[k, 3] = jnp.where(core == 0, mate, back[1, k])
        out[k, 4] = back[0, k]


def on_device(orbitals, coupling, pot_grad):
    states, wx, wy, wz = orbitals.shape
    shape = (wx, wy, wz)
    plane = (lax.axis_size("dx"), lax.axis_size("dy"))
    places = math.prod(plane)
    rows = states // places
    layer, line = wy * wz, wx * wz
    cells = wx * layer
    scale = 1.0 / math.sqrt(cells * places)

    swap = [(i, i ^ 1) for i in range(lax.axis_size("blk"))]
    psi = lax.optimization_barrier(orbitals.reshape(states, cells))
    two = shift(psi, "blk", -2)

    tmp = pltpu.VMEM((-(-9 * max(wx, wy) // 16) * 16, wz), F32)
    tail, head, hy = call(
        functools.partial(edges, shape=shape),
        [shape_of((states, layer + wz), BF16)] * 2 + [shape_of((states, 2 * (line + wz)), BF16)],
        [psi, coupling, pot_grad],
        scratch=[tmp],
    )
    hx = [shift(tail, "dx", -1), shift(head, "dx", 1)]
    hy = both_sides(hy, "dy")

    coeffs = pltpu.VMEM((3, wx, wy, wz), F32)
    ends = [pltpu.VMEM((2, 3, wy, wz), F32), pltpu.VMEM((2, 3, wx, wz), F32)]
    u, w, w_mate = [], [], []
    for layers, sides in ((range(1, wx - 1), []), ((0, wx - 1), hx)):
        if sides:
            sides, u[0] = lax.optimization_barrier((sides, u[0]))
        field = shape_of((3 * states, len(layers) * layer), BF16)
        results = call(
            functools.partial(operators, layers=layers, shape=shape),
            [field, field],
            [psi, *sides, hy, coupling, pot_grad],
            scratch=[coeffs] * 3 + [tmp, *ends],
        )
        u.append(results[0])
        w.append(results[1])
        w_mate.append(lax.ppermute(w[-1], "blk", swap))
    tall, wide = shape_of((3 * states, states), F32), shape_of((states, 3 * states), F32)
    (own,) = call(
        functools.partial(own_tiles, layer=layer, scale=scale), [tall], [*u, psi]
    )

    def cut_shapes(slots):
        shape = (slots, 3, rows, states)
        return [shape_of(shape, F32)] + [shape_of(shape, BF16)] * (places - 1)

    given = dict(layer=layer, plane=plane, scale=scale)
    two, own = lax.optimization_barrier((two, own))
    one = lax.ppermute(two, "blk", swap)
    (two,) = call(
        duplicate,
        [shape_of((states, cells), BF16)],
        [two],
        scratch=[pltpu.SemaphoreType.DMA],
        specs=[ANY],
        out_specs=[ANY],
        us=60,
    )
    mate, kept_there, *sends = call(
        functools.partial(there_tiles, **given),
        [wide, *cut_shapes(2)],
        [*w, *w_mate, two, psi, own],
        scratch=[pltpu.VMEM(wide.shape, F32)] * 2,
        us=1,
    )
    first = exchange(sends)
    one, mate = lax.optimization_barrier((one, mate))
    kept, *sends = call(
        functools.partial(here_tiles, **given),
        cut_shapes(3),
        [*u, two, one, own, mate],
        scratch=[pltpu.VMEM(tall.shape, F32)] * 2,
        us=1,
    )
    second = exchange(sends)
    first, kept = lax.optimization_barrier((first, kept))
    (there,) = call(add, [shape_of((2, 3, rows, states), F32)], [kept_there, *first])
    back = shift(there, "blk", 2)
    (out,) = call(
        assemble, [shape_of((3, 5, rows, states), F32)], [kept, *second, there, back]
    )
    return out


def solution(mesh):
    in_specs = (P("blk", "dx", "dy", None), P("dx", "dy", None), P(None, "dx", "dy", None))
    out_specs = P(None, None, ("blk", "dx", "dy"), None)
    return jax.shard_map(
        on_device, mesh=mesh, in_specs=in_specs, out_specs=out_specs, check_vma=False
    )
```

```python
import functools
import math

import jax
import jax.numpy as jnp
from jax import lax
from jax.experimental import pallas as pl
from jax.experimental.pallas import tpu as pltpu
from jax.sharding import PartitionSpec as P

F32, BF16 = jnp.float32, jnp.bfloat16
VMEM = pl.BlockSpec(memory_space=pltpu.VMEM)
LIMIT = 12 * 1024 * 1024
NT = (((1,), (1,)), ((), ()))
CHUNK = 16


def shape_of(shape, dtype):
    return jax.ShapeDtypeStruct(shape, dtype)


def shift(block, axis, distance):
    count = lax.axis_size(axis)
    return lax.ppermute(block, axis, [((i + distance) % count, i) for i in range(count)])


def both_sides(pair, axis):
    if lax.axis_size(axis) == 2:
        return shift(pair, axis, 1)
    tail, head = jnp.split(pair, 2, axis=1)
    return jnp.concatenate([shift(tail, axis, -1), shift(head, axis, 1)], axis=1)


def exchange(sends):
    nx, ny = lax.axis_size("dx"), lax.axis_size("dy")
    got = []
    for o, piece in enumerate(sends, 1):
        ox, oy = o // ny, o % ny
        route = [
            (i * ny + j, ((i + ox) % nx) * ny + (j + oy) % ny) for i in range(nx) for j in range(ny)
        ]
        got.append(lax.ppermute(piece, ("dx", "dy"), route))
    return got


def call(body, outs, operands, scratch=(), specs=None, out_specs=None, us=0):
    run = pl.pallas_call(
        body,
        out_shape=outs,
        in_specs=specs or [VMEM] * len(operands),
        out_specs=out_specs or [VMEM] * len(outs),
        scratch_shapes=list(scratch),
        compiler_params=pltpu.CompilerParams(vmem_limit_bytes=LIMIT),
        cost_estimate=pl.CostEstimate(
            flops=0, bytes_accessed=int(us * 3e6), transcendentals=0
        ),
    )
    return list(run(*operands))


def destinations(nx, ny):
    x, y = lax.axis_index("dx"), lax.axis_index("dy")
    return [
        lax.rem(x + ox, nx) * ny + lax.rem(y + oy, ny) for ox in range(nx) for oy in range(ny)
    ]


def thirds(value):
    high = value.astype(BF16).astype(F32)
    middle = (value - high).astype(BF16).astype(F32)
    return high, middle, value - high - middle


def edges(psi, coupling, grad, tail, head, hy, tmp, *, shape):
    wx, wy, wz = shape
    layer, line = wy * wz, wx * wz
    for side, (x, y, hx) in enumerate(((wx - 1, wy - 1, tail), (0, 0, head))):
        to_y = side * (line + wz)
        hx[:, :layer] = psi[:, x * layer : (x + 1) * layer]
        for i in range(wx):
            at = i * layer + y * wz
            hy[:, to_y + i * wz : to_y + (i + 1) * wz] = psi[:, at : at + wz]
        for k in range(3):
            for n, third in enumerate(thirds(coupling[x] * grad[k, x])):
                tmp[(3 * k + n) * wy : (3 * k + n + 1) * wy] = third
        hx[: tmp.shape[0], layer:] = tmp[...].astype(BF16)
        for k in range(3):
            for n, third in enumerate(thirds(coupling[:, y] * grad[k, :, y])):
                tmp[(3 * k + n) * wx : (3 * k + n + 1) * wx] = third
        hy[: tmp.shape[0], to_y + line : to_y + line + wz] = tmp[...].astype(BF16)


def operators(*refs, layers, shape):
    psi, *refs = refs
    outer = len(refs) == 13
    hx = refs[:2]
    hy, coupling, grad, u, w, half, back, ahead, tmp, ex, ey = refs[-11:]
    wx, wy, wz = shape
    layer, line = wy * wz, wx * wz
    states = psi.shape[0]
    half[...] = 0.5 * (coupling[...][None] * grad[...])

    def unpack(ref, at, to, count):
        tmp[...] = ref[: tmp.shape[0], at : at + wz].astype(F32)
        for k in range(3):
            third = [tmp[(3 * k + n) * count : (3 * k + n + 1) * count] for n in range(3)]
            to[k] = 0.5 * (third[0] + third[1] + third[2])

    for side in range(2):
        if outer:
            unpack(hx[side], layer, ex.at[side], wy)
        unpack(hy, side * (line + wz) + line, ey.at[side], wx)
    for k in range(3):
        for x in layers:
            back[k, x] = pltpu.roll(half[k, x], 1, 1)
            ahead[k, x] = pltpu.roll(half[k, x], wz - 1, 1)

    def coeff(k, x, y):
        if x < 0 or x >= wx:
            return ex[int(x >= wx), k, y : y + 1, :]
        if y < 0 or y >= wy:
            return ey[int(y >= wy), k, x : x + 1, :]
        return half[k, x, y : y + 1, :]

    def group(step, _):
        r = pl.ds(pl.multiple_of(step * CHUNK, CHUNK), CHUNK)

        def field(x, y):
            if x < 0 or x >= wx:
                return hx[int(x >= wx)][r, y * wz : (y + 1) * wz].astype(F32)
            if y < 0 or y >= wy:
                at = int(y >= wy) * (line + wz) + x * wz
                return hy[r, at : at + wz].astype(F32)
            at = x * layer + y * wz
            return psi[r, at : at + wz].astype(F32)

        for n, x in enumerate(layers):
            for y in range(wy):
                here = field(x, y)
                xb, xa = field(x - 1, y), field(x + 1, y)
                yb, ya = field(x, y - 1), field(x, y + 1)
                zb, za = pltpu.roll(here, 1, 1), pltpu.roll(here, wz - 1, 1)
                gx, gy, gz = xa - xb, ya - yb, za - zb
                c1, c2, c3 = [coeff(k, x, y) for k in range(3)]
                cols = slice(n * layer + y * wz, n * layer + (y + 1) * wz)

                def put(ref, k, value):
                    place = pl.ds(pl.multiple_of(k * states + step * CHUNK, CHUNK), CHUNK)
                    ref[place, cols] = value.astype(BF16)

                put(u, 0, c2 * gz - c3 * gy)
                put(u, 1, c3 * gx - c1 * gz)
                put(u, 2, c1 * gy - c2 * gx)

                def dx(k):
                    return coeff(k, x + 1, y) * xa - coeff(k, x - 1, y) * xb

                def dy(k):
                    return coeff(k, x, y + 1) * ya - coeff(k, x, y - 1) * yb

                def dz(k):
                    return ahead[k, x, y : y + 1, :] * za - back[k, x, y : y + 1, :] * zb

                put(w, 0, dy(2) - dz(1))
                put(w, 1, dz(0) - dx(2))
                put(w, 2, dx(1) - dy(0))
        return 0

    lax.fori_loop(0, states // CHUNK, group, 0)


def product(fields, panel, layer, flip=False):
    inner, outer = fields
    cells = inner.shape[1] + outer.shape[1]
    total = 0.0
    for a, start, stop in (
        (inner[...], layer, cells - layer),
        (outer[:, :layer], 0, layer),
        (outer[:, layer:], cells - layer, cells),
    ):
        b = panel(slice(start, stop))
        a, b = (b, a) if flip else (a, b)
        total = total + lax.dot_general(a, b, NT, preferred_element_type=F32)
    return total


def stacked(*panels):
    return lambda cols: jnp.concatenate([panel[:, cols] for panel in panels], axis=0)


def own_tiles(*refs, layer, scale):
    u, (psi, own) = refs[:2], refs[2:]
    own[...] = product(u, stacked(psi), layer) * scale


def cut(outs, slots, plane, states):
    rows = states // math.prod(plane)
    for ref, dest in zip(outs, destinations(*plane)):
        for n, slot in enumerate(slots):
            for k in range(3):
                ref[n, k] = slot(k, dest * rows, rows).astype(ref.dtype)


def tall_rows(tile):
    states = tile.shape[0] // 3

    def rows_of(k, start, rows):
        return tile[pl.ds(pl.multiple_of(k * states + start, rows), rows), :]

    return rows_of


def wide_rows(tile):
    states = tile.shape[0]

    def rows_of(k, start, rows):
        cols = slice(k * states, (k + 1) * states)
        return tile[pl.ds(pl.multiple_of(start, rows), rows), cols]

    return rows_of


def either(first, second):
    core = lax.rem(lax.axis_index("blk"), 2)
    return lambda *place: jnp.where(core == 0, first(*place), second(*place))


def there_tiles(*refs, layer, plane, scale):
    w, w_mate, (two, psi, own), refs = refs[:2], refs[2:4], refs[4:7], refs[7:]
    mate, outs, (there, there_mate) = refs[0], refs[1:-2], refs[-2:]
    states = two.shape[0]
    there[...] = product(w, stacked(two), layer, True) * scale
    both = product(w_mate, stacked(two, psi), layer, True) * scale
    there_mate[...], mate[...] = both[:states], both[states:]
    slots = (wide_rows(there), either(tall_rows(own), wide_rows(there_mate)))
    cut(outs, slots, plane, states)


def here_tiles(*refs, layer, plane, scale):
    u, (two, one, own, mate), refs = refs[:2], refs[2:6], refs[6:]
    outs, (here_two, here_one) = refs[:-2], refs[-2:]
    states = two.shape[0]
    both = product(u, stacked(two, one), layer) * scale
    here_two[...], here_one[...] = both[:, :states], both[:, states:]
    slots = (
        tall_rows(here_two), wide_rows(mate), either(tall_rows(here_one), tall_rows(own))
    )
    cut(outs, slots, plane, states)


def total_of(group, n, k):
    total = group[0][n, k]
    for part in group[1:]:
        total = total + part[n, k].astype(F32)
    return total


def add(*refs):
    group, outs = refs[:-2], refs[-2:]
    for n, out in enumerate(outs):
        for k in range(3):
            out[k] = total_of(group, n, k)


def assemble(*refs):
    group, (ours, back_two, back_one, out) = refs[:-4], refs[-4:]
    core = lax.rem(lax.axis_index("blk"), 2)
    for k in range(3):
        mate, third = total_of(group, 1, k), total_of(group, 2, k)
        out[k, 0] = total_of(group, 0, k)
        out[k, 1] = jnp.where(core == 0, third, mate)
        out[k, 2] = jnp.where(core == 0, ours[k], third)
        out[k, 3] = jnp.where(core == 0, mate, back_one[k])
        out[k, 4] = back_two[k]


def on_device(orbitals, coupling, pot_grad):
    states, wx, wy, wz = orbitals.shape
    shape = (wx, wy, wz)
    plane = (lax.axis_size("dx"), lax.axis_size("dy"))
    places = math.prod(plane)
    rows = states // places
    layer, line = wy * wz, wx * wz
    cells = wx * layer
    scale = 1.0 / math.sqrt(cells * places)

    swap = [(i, i ^ 1) for i in range(lax.axis_size("blk"))]
    psi = lax.optimization_barrier(orbitals.reshape(states, cells))
    two = shift(psi, "blk", -2)

    tmp = pltpu.VMEM((-(-9 * max(wx, wy) // 16) * 16, wz), F32)
    tail, head, hy = call(
        functools.partial(edges, shape=shape),
        [shape_of((states, layer + wz), BF16)] * 2 + [shape_of((states, 2 * (line + wz)), BF16)],
        [psi, coupling, pot_grad],
        scratch=[tmp],
    )
    hx = [shift(tail, "dx", -1), shift(head, "dx", 1)]
    hy = both_sides(hy, "dy")

    coeffs = pltpu.VMEM((3, wx, wy, wz), F32)
    ends = [pltpu.VMEM((2, 3, wy, wz), F32), pltpu.VMEM((2, 3, wx, wz), F32)]
    u, w, w_mate = [], [], []
    for layers, sides in ((range(1, wx - 1), []), ((0, wx - 1), hx)):
        if sides:
            sides, u[0] = lax.optimization_barrier((sides, u[0]))
        field = shape_of((3 * states, len(layers) * layer), BF16)
        results = call(
            functools.partial(operators, layers=layers, shape=shape),
            [field, field],
            [psi, *sides, hy, coupling, pot_grad],
            scratch=[coeffs] * 3 + [tmp, *ends],
        )
        u.append(results[0])
        w.append(results[1])
        w_mate.append(lax.ppermute(w[-1], "blk", swap))
    tall, wide = shape_of((3 * states, states), F32), shape_of((states, 3 * states), F32)
    (own,) = call(
        functools.partial(own_tiles, layer=layer, scale=scale), [tall], [*u, psi]
    )

    def cut_shapes(slots):
        shape = (slots, 3, rows, states)
        return [shape_of(shape, F32)] + [shape_of(shape, BF16)] * (places - 1)

    given = dict(layer=layer, plane=plane, scale=scale)
    two, own = lax.optimization_barrier((two, own))
    one = lax.ppermute(two, "blk", swap)
    mate, kept_there, *sends = call(
        functools.partial(there_tiles, **given),
        [wide, *cut_shapes(2)],
        [*w, *w_mate, two, psi, own],
        scratch=[pltpu.VMEM(wide.shape, F32)] * 2,
        us=1,
    )
    first = exchange(sends)
    one, mate = lax.optimization_barrier((one, mate))
    kept, *sends = call(
        functools.partial(here_tiles, **given),
        cut_shapes(3),
        [*u, two, one, own, mate],
        scratch=[pltpu.VMEM(tall.shape, F32)] * 2,
        us=1,
    )
    second = exchange(sends)
    first, kept = lax.optimization_barrier((first, kept))
    small = shape_of((3, rows, states), F32)
    there, ours = call(add, [small, small], [kept_there, *first])
    count = lax.axis_size("blk")
    back_two = shift(there, "blk", 2)
    odd = [((i + 2) % count, i) for i in range(1, count, 2)]
    back_one = lax.ppermute(ours, "blk", odd)
    (out,) = call(
        assemble,
        [shape_of((3, 5, rows, states), F32)],
        [kept, *second, ours, back_two, back_one],
    )
    return out


def solution(mesh):
    in_specs = (P("blk", "dx", "dy", None), P("dx", "dy", None), P(None, "dx", "dy", None))
    out_specs = P(None, None, ("blk", "dx", "dy"), None)
    return jax.shard_map(
        on_device, mesh=mesh, in_specs=in_specs, out_specs=out_specs, check_vma=False
    )
```

```python
import functools
import math

import jax
import jax.numpy as jnp
from jax import lax
from jax.experimental import pallas as pl
from jax.experimental.pallas import tpu as pltpu
from jax.sharding import PartitionSpec as P

F32, BF16 = jnp.float32, jnp.bfloat16
VMEM = pl.BlockSpec(memory_space=pltpu.VMEM)
ANY = pl.BlockSpec(memory_space=pl.ANY)
LIMIT = 12 * 1024 * 1024
NT = (((1,), (1,)), ((), ()))
CHUNK = 16
FETCHES = 8
MOST = 53248 * 1024


def shape_of(shape, dtype):
    return jax.ShapeDtypeStruct(shape, dtype)


def shift(block, axis, distance):
    count = lax.axis_size(axis)
    return lax.ppermute(block, axis, [((i + distance) % count, i) for i in range(count)])


def both_sides(pair, axis):
    if lax.axis_size(axis) == 2:
        return shift(pair, axis, 1)
    tail, head = jnp.split(pair, 2, axis=1)
    return jnp.concatenate([shift(tail, axis, -1), shift(head, axis, 1)], axis=1)


def exchange(sends):
    nx, ny = lax.axis_size("dx"), lax.axis_size("dy")
    got = []
    for o, piece in enumerate(sends, 1):
        ox, oy = o // ny, o % ny
        route = [
            (i * ny + j, ((i + ox) % nx) * ny + (j + oy) % ny) for i in range(nx) for j in range(ny)
        ]
        got.append(lax.ppermute(piece, ("dx", "dy"), route))
    return got


def call(body, outs, operands, scratch=(), specs=None, out_specs=None, us=0, limit=LIMIT):
    run = pl.pallas_call(
        body,
        out_shape=outs,
        in_specs=specs or [VMEM] * len(operands),
        out_specs=out_specs or [VMEM] * len(outs),
        scratch_shapes=list(scratch),
        compiler_params=pltpu.CompilerParams(vmem_limit_bytes=limit),
        cost_estimate=pl.CostEstimate(
            flops=0, bytes_accessed=int(us * 3e6), transcendentals=0
        ),
    )
    return list(run(*operands))


def destinations(nx, ny):
    x, y = lax.axis_index("dx"), lax.axis_index("dy")
    return [
        lax.rem(x + ox, nx) * ny + lax.rem(y + oy, ny) for ox in range(nx) for oy in range(ny)
    ]


def thirds(value):
    high = value.astype(BF16).astype(F32)
    middle = (value - high).astype(BF16).astype(F32)
    return high, middle, value - high - middle


def fetch(source, target, sems):
    size = source.shape[0] // FETCHES
    copies = []
    for n in range(FETCHES):
        part = pl.ds(n * size, size)
        copies.append(pltpu.make_async_copy(source.at[part], target.at[part], sems.at[n]))
        copies[n].start()
    for copy in copies:
        copy.wait()


def edges(psi, coupling, grad, tail, head, hy, tmp, *, shape):
    wx, wy, wz = shape
    layer, line = wy * wz, wx * wz
    for side, (x, y, hx) in enumerate(((wx - 1, wy - 1, tail), (0, 0, head))):
        to_y = side * (line + wz)
        hx[:, :layer] = psi[:, x * layer : (x + 1) * layer]
        for i in range(wx):
            at = i * layer + y * wz
            hy[:, to_y + i * wz : to_y + (i + 1) * wz] = psi[:, at : at + wz]
        for k in range(3):
            for n, third in enumerate(thirds(coupling[x] * grad[k, x])):
                tmp[(3 * k + n) * wy : (3 * k + n + 1) * wy] = third
        hx[: tmp.shape[0], layer:] = tmp[...].astype(BF16)
        for k in range(3):
            for n, third in enumerate(thirds(coupling[:, y] * grad[k, :, y])):
                tmp[(3 * k + n) * wx : (3 * k + n + 1) * wx] = third
        hy[: tmp.shape[0], to_y + line : to_y + line + wz] = tmp[...].astype(BF16)


def operators(*refs, layers, shape):
    psi, *refs = refs
    outer = len(refs) == 13
    hx = refs[:2]
    hy, coupling, grad, u, w, half, back, ahead, tmp, ex, ey = refs[-11:]
    wx, wy, wz = shape
    layer, line = wy * wz, wx * wz
    states = psi.shape[0]
    half[...] = 0.5 * (coupling[...][None] * grad[...])

    def unpack(ref, at, to, count):
        tmp[...] = ref[: tmp.shape[0], at : at + wz].astype(F32)
        for k in range(3):
            third = [tmp[(3 * k + n) * count : (3 * k + n + 1) * count] for n in range(3)]
            to[k] = 0.5 * (third[0] + third[1] + third[2])

    for side in range(2):
        if outer:
            unpack(hx[side], layer, ex.at[side], wy)
        unpack(hy, side * (line + wz) + line, ey.at[side], wx)
    for k in range(3):
        for x in layers:
            back[k, x] = pltpu.roll(half[k, x], 1, 1)
            ahead[k, x] = pltpu.roll(half[k, x], wz - 1, 1)

    def coeff(k, x, y):
        if x < 0 or x >= wx:
            return ex[int(x >= wx), k, y : y + 1, :]
        if y < 0 or y >= wy:
            return ey[int(y >= wy), k, x : x + 1, :]
        return half[k, x, y : y + 1, :]

    def group(step, _):
        r = pl.ds(pl.multiple_of(step * CHUNK, CHUNK), CHUNK)

        def field(x, y):
            if x < 0 or x >= wx:
                return hx[int(x >= wx)][r, y * wz : (y + 1) * wz].astype(F32)
            if y < 0 or y >= wy:
                at = int(y >= wy) * (line + wz) + x * wz
                return hy[r, at : at + wz].astype(F32)
            at = x * layer + y * wz
            return psi[r, at : at + wz].astype(F32)

        for n, x in enumerate(layers):
            for y in range(wy):
                here = field(x, y)
                xb, xa = field(x - 1, y), field(x + 1, y)
                yb, ya = field(x, y - 1), field(x, y + 1)
                zb, za = pltpu.roll(here, 1, 1), pltpu.roll(here, wz - 1, 1)
                gx, gy, gz = xa - xb, ya - yb, za - zb
                c1, c2, c3 = [coeff(k, x, y) for k in range(3)]
                cols = slice(n * layer + y * wz, n * layer + (y + 1) * wz)

                def put(ref, k, value):
                    place = pl.ds(pl.multiple_of(k * states + step * CHUNK, CHUNK), CHUNK)
                    ref[place, cols] = value.astype(BF16)

                put(u, 0, c2 * gz - c3 * gy)
                put(u, 1, c3 * gx - c1 * gz)
                put(u, 2, c1 * gy - c2 * gx)

                def dx(k):
                    return coeff(k, x + 1, y) * xa - coeff(k, x - 1, y) * xb

                def dy(k):
                    return coeff(k, x, y + 1) * ya - coeff(k, x, y - 1) * yb

                def dz(k):
                    return ahead[k, x, y : y + 1, :] * za - back[k, x, y : y + 1, :] * zb

                put(w, 0, dy(2) - dz(1))
                put(w, 1, dz(0) - dx(2))
                put(w, 2, dx(1) - dy(0))
        return 0

    lax.fori_loop(0, states // CHUNK, group, 0)


def product(fields, panel, layer, flip=False):
    inner, outer = fields
    cells = inner.shape[1] + outer.shape[1]
    total = 0.0
    for a, start, stop in (
        (inner[...], layer, cells - layer),
        (outer[:, :layer], 0, layer),
        (outer[:, layer:], cells - layer, cells),
    ):
        b = panel(slice(start, stop))
        a, b = (b, a) if flip else (a, b)
        total = total + lax.dot_general(a, b, NT, preferred_element_type=F32)
    return total


def stacked(*panels):
    return lambda cols: jnp.concatenate([panel[:, cols] for panel in panels], axis=0)


def own_tiles(*refs, layer, scale):
    u, (psi, own) = refs[:2], refs[2:]
    own[...] = product(u, stacked(psi), layer) * scale


def cut(outs, slots, plane, states):
    rows = states // math.prod(plane)
    for ref, dest in zip(outs, destinations(*plane)):
        for n, slot in enumerate(slots):
            for k in range(3):
                ref[n, k] = slot(k, dest * rows, rows).astype(ref.dtype)


def tall_rows(tile):
    states = tile.shape[0] // 3

    def rows_of(k, start, rows):
        return tile[pl.ds(pl.multiple_of(k * states + start, rows), rows), :]

    return rows_of


def wide_rows(tile):
    states = tile.shape[0]

    def rows_of(k, start, rows):
        cols = slice(k * states, (k + 1) * states)
        return tile[pl.ds(pl.multiple_of(start, rows), rows), cols]

    return rows_of


def either(first, second):
    core = lax.rem(lax.axis_index("blk"), 2)
    return lambda *place: jnp.where(core == 0, first(*place), second(*place))


def there_tiles(*refs, layer, plane, scale):
    w, w_mate, (two, psi, own), refs = refs[:2], refs[2:4], refs[4:7], refs[7:]
    mate, outs, (there, there_mate) = refs[0], refs[1:-2], refs[-2:]
    states = two.shape[0]
    there[...] = product(w, stacked(two), layer, True) * scale
    both = product(w_mate, stacked(two, psi), layer, True) * scale
    there_mate[...], mate[...] = both[:states], both[states:]
    slots = (wide_rows(there), either(tall_rows(own), wide_rows(there_mate)))
    cut(outs, slots, plane, states)


def here_tiles(*refs, layer, plane, scale):
    u, (two, one, own, mate), refs = refs[:2], refs[2:6], refs[6:]
    outs, (here_two, here_one) = refs[:-2], refs[-2:]
    states = two.shape[0]
    both = product(u, stacked(two, one), layer) * scale
    here_two[...], here_one[...] = both[:, :states], both[:, states:]
    slots = (
        tall_rows(here_two), wide_rows(mate), either(tall_rows(here_one), tall_rows(own))
    )
    cut(outs, slots, plane, states)


def total_of(group, n, k):
    total = group[0][n, k]
    for part in group[1:]:
        total = total + part[n, k].astype(F32)
    return total


def add(*refs):
    group, outs = refs[:-2], refs[-2:]
    for n, out in enumerate(outs):
        for k in range(3):
            out[k] = total_of(group, n, k)


def assemble(*refs):
    group, (ours, back_two, back_one, out) = refs[:-4], refs[-4:]
    core = lax.rem(lax.axis_index("blk"), 2)
    for k in range(3):
        mate, third = total_of(group, 1, k), total_of(group, 2, k)
        out[k, 0] = total_of(group, 0, k)
        out[k, 1] = jnp.where(core == 0, third, mate)
        out[k, 2] = jnp.where(core == 0, ours[k], third)
        out[k, 3] = jnp.where(core == 0, mate, back_one[k])
        out[k, 4] = back_two[k]


def on_device(orbitals, coupling, pot_grad):
    states, wx, wy, wz = orbitals.shape
    shape = (wx, wy, wz)
    plane = (lax.axis_size("dx"), lax.axis_size("dy"))
    places = math.prod(plane)
    rows = states // places
    layer, line = wy * wz, wx * wz
    cells = wx * layer
    scale = 1.0 / math.sqrt(cells * places)

    swap = [(i, i ^ 1) for i in range(lax.axis_size("blk"))]
    (raw,) = call(
        fetch,
        [shape_of(orbitals.shape, BF16)],
        [orbitals],
        scratch=[pltpu.SemaphoreType.DMA((FETCHES,))],
        specs=[ANY],
        limit=MOST,
    )
    psi = lax.optimization_barrier(raw.reshape(states, cells))
    two = shift(psi, "blk", -2)

    tmp = pltpu.VMEM((-(-9 * max(wx, wy) // 16) * 16, wz), F32)
    tail, head, hy = call(
        functools.partial(edges, shape=shape),
        [shape_of((states, layer + wz), BF16)] * 2 + [shape_of((states, 2 * (line + wz)), BF16)],
        [psi, coupling, pot_grad],
        scratch=[tmp],
    )
    hx = [shift(tail, "dx", -1), shift(head, "dx", 1)]
    hy = both_sides(hy, "dy")

    coeffs = pltpu.VMEM((3, wx, wy, wz), F32)
    ends = [pltpu.VMEM((2, 3, wy, wz), F32), pltpu.VMEM((2, 3, wx, wz), F32)]
    u, w, w_mate = [], [], []
    for layers, sides in ((range(1, wx - 1), []), ((0, wx - 1), hx)):
        if sides:
            sides, u[0] = lax.optimization_barrier((sides, u[0]))
        field = shape_of((3 * states, len(layers) * layer), BF16)
        results = call(
            functools.partial(operators, layers=layers, shape=shape),
            [field, field],
            [psi, *sides, hy, coupling, pot_grad],
            scratch=[coeffs] * 3 + [tmp, *ends],
        )
        u.append(results[0])
        w.append(results[1])
        w_mate.append(lax.ppermute(w[-1], "blk", swap))
    tall, wide = shape_of((3 * states, states), F32), shape_of((states, 3 * states), F32)
    (own,) = call(
        functools.partial(own_tiles, layer=layer, scale=scale), [tall], [*u, psi]
    )

    def cut_shapes(slots):
        shape = (slots, 3, rows, states)
        return [shape_of(shape, F32)] + [shape_of(shape, BF16)] * (places - 1)

    given = dict(layer=layer, plane=plane, scale=scale)
    two, own = lax.optimization_barrier((two, own))
    one = lax.ppermute(two, "blk", swap)
    mate, kept_there, *sends = call(
        functools.partial(there_tiles, **given),
        [wide, *cut_shapes(2)],
        [*w, *w_mate, two, psi, own],
        scratch=[pltpu.VMEM(wide.shape, F32)] * 2,
        us=1,
    )
    first = exchange(sends)
    one, mate = lax.optimization_barrier((one, mate))
    kept, *sends = call(
        functools.partial(here_tiles, **given),
        cut_shapes(3),
        [*u, two, one, own, mate],
        scratch=[pltpu.VMEM(tall.shape, F32)] * 2,
        us=1,
    )
    second = exchange(sends)
    first, kept = lax.optimization_barrier((first, kept))
    small = shape_of((3, rows, states), F32)
    there, ours = call(add, [small, small], [kept_there, *first])
    count = lax.axis_size("blk")
    back_two = shift(there, "blk", 2)
    odd = [((i + 2) % count, i) for i in range(1, count, 2)]
    back_one = lax.ppermute(ours, "blk", odd)
    (out,) = call(
        assemble,
        [shape_of((3, 5, rows, states), F32)],
        [kept, *second, ours, back_two, back_one],
    )
    return out


def solution(mesh):
    in_specs = (P("blk", "dx", "dy", None), P("dx", "dy", None), P(None, "dx", "dy", None))
    out_specs = P(None, None, ("blk", "dx", "dy"), None)
    return jax.shard_map(
        on_device, mesh=mesh, in_specs=in_specs, out_specs=out_specs, check_vma=False
    )
```

```python
import functools
import math

import jax
import jax.numpy as jnp
from jax import lax
from jax.experimental import pallas as pl
from jax.experimental.pallas import tpu as pltpu
from jax.sharding import PartitionSpec as P

F32, BF16 = jnp.float32, jnp.bfloat16
VMEM = pl.BlockSpec(memory_space=pltpu.VMEM)
LIMIT = 12 * 1024 * 1024
NT = (((1,), (1,)), ((), ()))
CHUNK = 16


def shape_of(shape, dtype):
    return jax.ShapeDtypeStruct(shape, dtype)


def shift(block, axis, distance):
    count = lax.axis_size(axis)
    return lax.ppermute(block, axis, [((i + distance) % count, i) for i in range(count)])


def both_sides(pair, axis):
    if lax.axis_size(axis) == 2:
        return shift(pair, axis, 1)
    tail, head = jnp.split(pair, 2, axis=1)
    return jnp.concatenate([shift(tail, axis, -1), shift(head, axis, 1)], axis=1)


def exchange(sends):
    nx, ny = lax.axis_size("dx"), lax.axis_size("dy")
    got = []
    for o, piece in enumerate(sends, 1):
        ox, oy = o // ny, o % ny
        route = [
            (i * ny + j, ((i + ox) % nx) * ny + (j + oy) % ny) for i in range(nx) for j in range(ny)
        ]
        got.append(lax.ppermute(piece, ("dx", "dy"), route))
    return got


def call(body, outs, operands, scratch=(), specs=None, out_specs=None, us=0):
    run = pl.pallas_call(
        body,
        out_shape=outs,
        in_specs=specs or [VMEM] * len(operands),
        out_specs=out_specs or [VMEM] * len(outs),
        scratch_shapes=list(scratch),
        compiler_params=pltpu.CompilerParams(vmem_limit_bytes=LIMIT),
        cost_estimate=pl.CostEstimate(
            flops=0, bytes_accessed=int(us * 3e6), transcendentals=0
        ),
    )
    return list(run(*operands))


def destinations(nx, ny):
    x, y = lax.axis_index("dx"), lax.axis_index("dy")
    return [
        lax.rem(x + ox, nx) * ny + lax.rem(y + oy, ny) for ox in range(nx) for oy in range(ny)
    ]


def thirds(value):
    high = value.astype(BF16).astype(F32)
    middle = (value - high).astype(BF16).astype(F32)
    return high, middle, value - high - middle


def edges(psi, coupling, grad, tail, head, hy, tmp, *, shape):
    wx, wy, wz = shape
    layer, line = wy * wz, wx * wz
    for side, (x, y, hx) in enumerate(((wx - 1, wy - 1, tail), (0, 0, head))):
        to_y = side * (line + wz)
        hx[:, :layer] = psi[:, x * layer : (x + 1) * layer]
        for i in range(wx):
            at = i * layer + y * wz
            hy[:, to_y + i * wz : to_y + (i + 1) * wz] = psi[:, at : at + wz]
        for k in range(3):
            for n, third in enumerate(thirds(coupling[x] * grad[k, x])):
                tmp[(3 * k + n) * wy : (3 * k + n + 1) * wy] = third
        hx[: tmp.shape[0], layer:] = tmp[...].astype(BF16)
        for k in range(3):
            for n, third in enumerate(thirds(coupling[:, y] * grad[k, :, y])):
                tmp[(3 * k + n) * wx : (3 * k + n + 1) * wx] = third
        hy[: tmp.shape[0], to_y + line : to_y + line + wz] = tmp[...].astype(BF16)


def operators(*refs, layers, shape):
    psi, *refs = refs
    outer = len(refs) == 13
    hx = refs[:2]
    hy, coupling, grad, u, w, half, back, ahead, tmp, ex, ey = refs[-11:]
    wx, wy, wz = shape
    layer, line = wy * wz, wx * wz
    states = psi.shape[0]
    half[...] = 0.5 * (coupling[...][None] * grad[...])

    def unpack(ref, at, to, count):
        tmp[...] = ref[: tmp.shape[0], at : at + wz].astype(F32)
        for k in range(3):
            third = [tmp[(3 * k + n) * count : (3 * k + n + 1) * count] for n in range(3)]
            to[k] = 0.5 * (third[0] + third[1] + third[2])

    for side in range(2):
        if outer:
            unpack(hx[side], layer, ex.at[side], wy)
        unpack(hy, side * (line + wz) + line, ey.at[side], wx)
    for k in range(3):
        for x in layers:
            back[k, x] = pltpu.roll(half[k, x], 1, 1)
            ahead[k, x] = pltpu.roll(half[k, x], wz - 1, 1)

    def coeff(k, x, y):
        if x < 0 or x >= wx:
            return ex[int(x >= wx), k, y : y + 1, :]
        if y < 0 or y >= wy:
            return ey[int(y >= wy), k, x : x + 1, :]
        return half[k, x, y : y + 1, :]

    def group(step, _):
        r = pl.ds(pl.multiple_of(step * CHUNK, CHUNK), CHUNK)

        def field(x, y):
            if x < 0 or x >= wx:
                return hx[int(x >= wx)][r, y * wz : (y + 1) * wz].astype(F32)
            if y < 0 or y >= wy:
                at = int(y >= wy) * (line + wz) + x * wz
                return hy[r, at : at + wz].astype(F32)
            at = x * layer + y * wz
            return psi[r, at : at + wz].astype(F32)

        for n, x in enumerate(layers):
            for y in range(wy):
                here = field(x, y)
                xb, xa = field(x - 1, y), field(x + 1, y)
                yb, ya = field(x, y - 1), field(x, y + 1)
                zb, za = pltpu.roll(here, 1, 1), pltpu.roll(here, wz - 1, 1)
                gx, gy, gz = xa - xb, ya - yb, za - zb
                c1, c2, c3 = [coeff(k, x, y) for k in range(3)]
                cols = slice(n * layer + y * wz, n * layer + (y + 1) * wz)

                def put(ref, k, value):
                    place = pl.ds(pl.multiple_of(k * states + step * CHUNK, CHUNK), CHUNK)
                    ref[place, cols] = value.astype(BF16)

                put(u, 0, c2 * gz - c3 * gy)
                put(u, 1, c3 * gx - c1 * gz)
                put(u, 2, c1 * gy - c2 * gx)

                def dx(k):
                    return coeff(k, x + 1, y) * xa - coeff(k, x - 1, y) * xb

                def dy(k):
                    return coeff(k, x, y + 1) * ya - coeff(k, x, y - 1) * yb

                def dz(k):
                    return ahead[k, x, y : y + 1, :] * za - back[k, x, y : y + 1, :] * zb

                put(w, 0, dy(2) - dz(1))
                put(w, 1, dz(0) - dx(2))
                put(w, 2, dx(1) - dy(0))
        return 0

    lax.fori_loop(0, states // CHUNK, group, 0)


def product(fields, panel, layer, flip=False):
    inner, outer = fields
    cells = inner.shape[1] + outer.shape[1]
    total = 0.0
    for a, start, stop in (
        (inner[...], layer, cells - layer),
        (outer[:, :layer], 0, layer),
        (outer[:, layer:], cells - layer, cells),
    ):
        b = panel(slice(start, stop))
        a, b = (b, a) if flip else (a, b)
        total = total + lax.dot_general(a, b, NT, preferred_element_type=F32)
    return total


def stacked(*panels):
    return lambda cols: jnp.concatenate([panel[:, cols] for panel in panels], axis=0)


def own_tiles(*refs, layer, scale):
    u, (psi, own) = refs[:2], refs[2:]
    own[...] = product(u, stacked(psi), layer) * scale


def cut(outs, slots, plane, states):
    rows = states // math.prod(plane)
    for ref, dest in zip(outs, destinations(*plane)):
        for n, slot in enumerate(slots):
            for k in range(3):
                ref[n, k] = slot(k, dest * rows, rows).astype(ref.dtype)


def tall_rows(tile):
    states = tile.shape[0] // 3

    def rows_of(k, start, rows):
        return tile[pl.ds(pl.multiple_of(k * states + start, rows), rows), :]

    return rows_of


def wide_rows(tile):
    states = tile.shape[0]

    def rows_of(k, start, rows):
        cols = slice(k * states, (k + 1) * states)
        return tile[pl.ds(pl.multiple_of(start, rows), rows), cols]

    return rows_of


def either(first, second):
    core = lax.rem(lax.axis_index("blk"), 2)
    return lambda *place: jnp.where(core == 0, first(*place), second(*place))


def there_tiles(*refs, layer, plane, scale):
    w, w_mate, (two, psi, own), refs = refs[:2], refs[2:4], refs[4:7], refs[7:]
    mate, outs, (there, there_mate) = refs[0], refs[1:-2], refs[-2:]
    states = two.shape[0]
    there[...] = product(w, stacked(two), layer, True) * scale
    both = product(w_mate, stacked(two, psi), layer, True) * scale
    there_mate[...], mate[...] = both[:states], both[states:]
    slots = (wide_rows(there), either(tall_rows(own), wide_rows(there_mate)))
    cut(outs, slots, plane, states)


def here_tiles(*refs, layer, plane, scale):
    u, (two, one, own, mate), refs = refs[:2], refs[2:6], refs[6:]
    outs, (here_two, here_one) = refs[:-2], refs[-2:]
    states = two.shape[0]
    both = product(u, stacked(two, one), layer) * scale
    here_two[...], here_one[...] = both[:, :states], both[:, states:]
    slots = (
        tall_rows(here_two), wide_rows(mate), either(tall_rows(here_one), tall_rows(own))
    )
    cut(outs, slots, plane, states)


def total_of(group, n, k):
    total = group[0][n, k]
    for part in group[1:]:
        total = total + part[n, k].astype(F32)
    return total


def add(*refs):
    group, outs = refs[:-2], refs[-2:]
    for n, out in enumerate(outs):
        for k in range(3):
            out[k] = total_of(group, n, k)


def assemble(*refs):
    group, (ours, back_two, back_one, out) = refs[:-4], refs[-4:]
    core = lax.rem(lax.axis_index("blk"), 2)
    for k in range(3):
        mate, third = total_of(group, 1, k), total_of(group, 2, k)
        out[k, 0] = total_of(group, 0, k)
        out[k, 1] = jnp.where(core == 0, third, mate)
        out[k, 2] = jnp.where(core == 0, ours[k], third)
        out[k, 3] = jnp.where(core == 0, mate, back_one[k])
        out[k, 4] = back_two[k]


def on_device(orbitals, coupling, pot_grad):
    states, wx, wy, wz = orbitals.shape
    shape = (wx, wy, wz)
    plane = (lax.axis_size("dx"), lax.axis_size("dy"))
    places = math.prod(plane)
    rows = states // places
    layer, line = wy * wz, wx * wz
    cells = wx * layer
    scale = 1.0 / math.sqrt(cells * places)

    swap = [(i, i ^ 1) for i in range(lax.axis_size("blk"))]
    two = shift(orbitals, "blk", -2)
    psi = lax.optimization_barrier(orbitals.reshape(states, cells))

    tmp = pltpu.VMEM((-(-9 * max(wx, wy) // 16) * 16, wz), F32)
    tail, head, hy = call(
        functools.partial(edges, shape=shape),
        [shape_of((states, layer + wz), BF16)] * 2 + [shape_of((states, 2 * (line + wz)), BF16)],
        [psi, coupling, pot_grad],
        scratch=[tmp],
    )
    hx = [shift(tail, "dx", -1), shift(head, "dx", 1)]
    hy = both_sides(hy, "dy")

    coeffs = pltpu.VMEM((3, wx, wy, wz), F32)
    ends = [pltpu.VMEM((2, 3, wy, wz), F32), pltpu.VMEM((2, 3, wx, wz), F32)]
    u, w, w_mate = [], [], []
    for layers, sides in ((range(1, wx - 1), []), ((0, wx - 1), hx)):
        if sides:
            sides, u[0] = lax.optimization_barrier((sides, u[0]))
        field = shape_of((3 * states, len(layers) * layer), BF16)
        results = call(
            functools.partial(operators, layers=layers, shape=shape),
            [field, field],
            [psi, *sides, hy, coupling, pot_grad],
            scratch=[coeffs] * 3 + [tmp, *ends],
        )
        u.append(results[0])
        w.append(results[1])
        w_mate.append(lax.ppermute(w[-1], "blk", swap))
    tall, wide = shape_of((3 * states, states), F32), shape_of((states, 3 * states), F32)
    (own,) = call(
        functools.partial(own_tiles, layer=layer, scale=scale), [tall], [*u, psi]
    )

    def cut_shapes(slots):
        shape = (slots, 3, rows, states)
        return [shape_of(shape, F32)] + [shape_of(shape, BF16)] * (places - 1)

    given = dict(layer=layer, plane=plane, scale=scale)
    two, own = lax.optimization_barrier((two, own))
    two = lax.optimization_barrier(two.reshape(states, cells))
    one = lax.ppermute(two, "blk", swap)
    mate, kept_there, *sends = call(
        functools.partial(there_tiles, **given),
        [wide, *cut_shapes(2)],
        [*w, *w_mate, two, psi, own],
        scratch=[pltpu.VMEM(wide.shape, F32)] * 2,
        us=1,
    )
    first = exchange(sends)
    one, mate = lax.optimization_barrier((one, mate))
    kept, *sends = call(
        functools.partial(here_tiles, **given),
        cut_shapes(3),
        [*u, two, one, own, mate],
        scratch=[pltpu.VMEM(tall.shape, F32)] * 2,
        us=1,
    )
    second = exchange(sends)
    first, kept = lax.optimization_barrier((first, kept))
    small = shape_of((3, rows, states), F32)
    there, ours = call(add, [small, small], [kept_there, *first])
    count = lax.axis_size("blk")
    back_two = shift(there, "blk", 2)
    odd = [((i + 2) % count, i) for i in range(1, count, 2)]
    back_one = lax.ppermute(ours, "blk", odd)
    (out,) = call(
        assemble,
        [shape_of((3, 5, rows, states), F32)],
        [kept, *second, ours, back_two, back_one],
    )
    return out


def solution(mesh):
    in_specs = (P("blk", "dx", "dy", None), P("dx", "dy", None), P(None, "dx", "dy", None))
    out_specs = P(None, None, ("blk", "dx", "dy"), None)
    return jax.shard_map(
        on_device, mesh=mesh, in_specs=in_specs, out_specs=out_specs, check_vma=False
    )
```

```python
import functools
import math

import jax
import jax.numpy as jnp
from jax import lax
from jax.experimental import pallas as pl
from jax.experimental.pallas import tpu as pltpu
from jax.sharding import PartitionSpec as P

F32, BF16 = jnp.float32, jnp.bfloat16
VMEM = pl.BlockSpec(memory_space=pltpu.VMEM)
LIMIT = 12 * 1024 * 1024
NT = (((1,), (1,)), ((), ()))
CHUNK = 16


def shape_of(shape, dtype):
    return jax.ShapeDtypeStruct(shape, dtype)


def shift(block, axis, distance):
    count = lax.axis_size(axis)
    return lax.ppermute(block, axis, [((i + distance) % count, i) for i in range(count)])


def both_sides(pair, axis):
    if lax.axis_size(axis) == 2:
        return shift(pair, axis, 1)
    tail, head = jnp.split(pair, 2, axis=1)
    return jnp.concatenate([shift(tail, axis, -1), shift(head, axis, 1)], axis=1)


def exchange(sends):
    nx, ny = lax.axis_size("dx"), lax.axis_size("dy")
    got = []
    for o, piece in enumerate(sends, 1):
        ox, oy = o // ny, o % ny
        route = [
            (i * ny + j, ((i + ox) % nx) * ny + (j + oy) % ny) for i in range(nx) for j in range(ny)
        ]
        got.append(lax.ppermute(piece, ("dx", "dy"), route))
    return got


def call(body, outs, operands, scratch=(), specs=None, out_specs=None, us=0):
    run = pl.pallas_call(
        body,
        out_shape=outs,
        in_specs=specs or [VMEM] * len(operands),
        out_specs=out_specs or [VMEM] * len(outs),
        scratch_shapes=list(scratch),
        compiler_params=pltpu.CompilerParams(vmem_limit_bytes=LIMIT),
        cost_estimate=pl.CostEstimate(
            flops=0, bytes_accessed=int(us * 3e6), transcendentals=0
        ),
    )
    return list(run(*operands))


def destinations(nx, ny):
    x, y = lax.axis_index("dx"), lax.axis_index("dy")
    return [
        lax.rem(x + ox, nx) * ny + lax.rem(y + oy, ny) for ox in range(nx) for oy in range(ny)
    ]


def thirds(value):
    high = value.astype(BF16).astype(F32)
    middle = (value - high).astype(BF16).astype(F32)
    return high, middle, value - high - middle


def edges(psi, coupling, grad, tail, head, hy, tmp, *, shape):
    wx, wy, wz = shape
    layer, line = wy * wz, wx * wz
    for side, (x, y, hx) in enumerate(((wx - 1, wy - 1, tail), (0, 0, head))):
        to_y = side * (line + wz)
        hx[:, :layer] = psi[:, x * layer : (x + 1) * layer]
        for i in range(wx):
            at = i * layer + y * wz
            hy[:, to_y + i * wz : to_y + (i + 1) * wz] = psi[:, at : at + wz]
        for k in range(3):
            for n, third in enumerate(thirds(coupling[x] * grad[k, x])):
                tmp[(3 * k + n) * wy : (3 * k + n + 1) * wy] = third
        hx[: tmp.shape[0], layer:] = tmp[...].astype(BF16)
        for k in range(3):
            for n, third in enumerate(thirds(coupling[:, y] * grad[k, :, y])):
                tmp[(3 * k + n) * wx : (3 * k + n + 1) * wx] = third
        hy[: tmp.shape[0], to_y + line : to_y + line + wz] = tmp[...].astype(BF16)


def operators(*refs, layers, shape):
    psi, *refs = refs
    outer = len(refs) == 13
    hx = refs[:2]
    hy, coupling, grad, u, w, half, back, ahead, tmp, ex, ey = refs[-11:]
    wx, wy, wz = shape
    layer, line = wy * wz, wx * wz
    states = psi.shape[0]
    half[...] = 0.5 * (coupling[...][None] * grad[...])

    def unpack(ref, at, to, count):
        tmp[...] = ref[: tmp.shape[0], at : at + wz].astype(F32)
        for k in range(3):
            third = [tmp[(3 * k + n) * count : (3 * k + n + 1) * count] for n in range(3)]
            to[k] = 0.5 * (third[0] + third[1] + third[2])

    for side in range(2):
        if outer:
            unpack(hx[side], layer, ex.at[side], wy)
        unpack(hy, side * (line + wz) + line, ey.at[side], wx)
    for k in range(3):
        for x in layers:
            back[k, x] = pltpu.roll(half[k, x], 1, 1)
            ahead[k, x] = pltpu.roll(half[k, x], wz - 1, 1)

    def coeff(k, x, y):
        if x < 0 or x >= wx:
            return ex[int(x >= wx), k, y : y + 1, :]
        if y < 0 or y >= wy:
            return ey[int(y >= wy), k, x : x + 1, :]
        return half[k, x, y : y + 1, :]

    def group(step, _):
        r = pl.ds(pl.multiple_of(step * CHUNK, CHUNK), CHUNK)

        def field(x, y):
            if x < 0 or x >= wx:
                return hx[int(x >= wx)][r, y * wz : (y + 1) * wz].astype(F32)
            if y < 0 or y >= wy:
                at = int(y >= wy) * (line + wz) + x * wz
                return hy[r, at : at + wz].astype(F32)
            at = x * layer + y * wz
            return psi[r, at : at + wz].astype(F32)

        for n, x in enumerate(layers):
            for y in range(wy):
                here = field(x, y)
                xb, xa = field(x - 1, y), field(x + 1, y)
                yb, ya = field(x, y - 1), field(x, y + 1)
                zb, za = pltpu.roll(here, 1, 1), pltpu.roll(here, wz - 1, 1)
                gx, gy, gz = xa - xb, ya - yb, za - zb
                c1, c2, c3 = [coeff(k, x, y) for k in range(3)]
                cols = slice(n * layer + y * wz, n * layer + (y + 1) * wz)

                def put(ref, k, value):
                    place = pl.ds(pl.multiple_of(k * states + step * CHUNK, CHUNK), CHUNK)
                    ref[place, cols] = value.astype(BF16)

                put(u, 0, c2 * gz - c3 * gy)
                put(u, 1, c3 * gx - c1 * gz)
                put(u, 2, c1 * gy - c2 * gx)

                def dx(k):
                    return coeff(k, x + 1, y) * xa - coeff(k, x - 1, y) * xb

                def dy(k):
                    return coeff(k, x, y + 1) * ya - coeff(k, x, y - 1) * yb

                def dz(k):
                    return ahead[k, x, y : y + 1, :] * za - back[k, x, y : y + 1, :] * zb

                put(w, 0, dy(2) - dz(1))
                put(w, 1, dz(0) - dx(2))
                put(w, 2, dx(1) - dy(0))
        return 0

    lax.fori_loop(0, states // CHUNK, group, 0)


def product(fields, panel, layer, flip=False):
    inner, outer = fields
    cells = inner.shape[1] + outer.shape[1]
    total = 0.0
    for a, start, stop in (
        (inner[...], layer, cells - layer),
        (outer[:, :layer], 0, layer),
        (outer[:, layer:], cells - layer, cells),
    ):
        b = panel(slice(start, stop))
        a, b = (b, a) if flip else (a, b)
        total = total + lax.dot_general(a, b, NT, preferred_element_type=F32)
    return total


def stacked(*panels):
    return lambda cols: jnp.concatenate([panel[:, cols] for panel in panels], axis=0)


def own_tiles(*refs, layer, scale):
    u, (psi, own) = refs[:2], refs[2:]
    own[...] = product(u, stacked(psi), layer) * scale


def cut(outs, slots, plane, states):
    rows = states // math.prod(plane)
    for ref, dest in zip(outs, destinations(*plane)):
        for n, slot in enumerate(slots):
            for k in range(3):
                ref[n, k] = slot(k, dest * rows, rows).astype(ref.dtype)


def tall_rows(tile):
    states = tile.shape[0] // 3

    def rows_of(k, start, rows):
        return tile[pl.ds(pl.multiple_of(k * states + start, rows), rows), :]

    return rows_of


def wide_rows(tile):
    states = tile.shape[0]

    def rows_of(k, start, rows):
        cols = slice(k * states, (k + 1) * states)
        return tile[pl.ds(pl.multiple_of(start, rows), rows), cols]

    return rows_of


def either(first, second):
    core = lax.rem(lax.axis_index("blk"), 2)
    return lambda *place: jnp.where(core == 0, first(*place), second(*place))


def there_tiles(*refs, layer, plane, scale):
    w, w_mate, (two, psi, own), refs = refs[:2], refs[2:4], refs[4:7], refs[7:]
    mate, outs, (there, there_mate) = refs[0], refs[1:-2], refs[-2:]
    states = two.shape[0]
    there[...] = product(w, stacked(two), layer, True) * scale
    both = product(w_mate, stacked(two, psi), layer, True) * scale
    there_mate[...], mate[...] = both[:states], both[states:]
    slots = (wide_rows(there), either(tall_rows(own), wide_rows(there_mate)))
    cut(outs, slots, plane, states)


def here_tiles(*refs, layer, plane, scale):
    u, (two, one, own, mate), refs = refs[:2], refs[2:6], refs[6:]
    outs, (here_two, here_one) = refs[:-2], refs[-2:]
    states = two.shape[0]
    both = product(u, stacked(two, one), layer) * scale
    here_two[...], here_one[...] = both[:, :states], both[:, states:]
    slots = (
        tall_rows(here_two), wide_rows(mate), either(tall_rows(here_one), tall_rows(own))
    )
    cut(outs, slots, plane, states)


def total_of(group, n, k):
    total = group[0][n, k]
    for part in group[1:]:
        total = total + part[n, k].astype(F32)
    return total


def add(*refs):
    group, outs = refs[:-2], refs[-2:]
    for n, out in enumerate(outs):
        for k in range(3):
            out[k] = total_of(group, n, k)


def assemble(*refs):
    group, (ours, back_two, back_one, out) = refs[:-4], refs[-4:]
    core = lax.rem(lax.axis_index("blk"), 2)
    for k in range(3):
        mate, third = total_of(group, 1, k), total_of(group, 2, k)
        out[k, 0] = total_of(group, 0, k)
        out[k, 1] = jnp.where(core == 0, third, mate)
        out[k, 2] = jnp.where(core == 0, ours[k], third)
        out[k, 3] = jnp.where(core == 0, mate, back_one[k])
        out[k, 4] = back_two[k]


def on_device(orbitals, coupling, pot_grad):
    states, wx, wy, wz = orbitals.shape
    shape = (wx, wy, wz)
    plane = (lax.axis_size("dx"), lax.axis_size("dy"))
    places = math.prod(plane)
    rows = states // places
    layer, line = wy * wz, wx * wz
    cells = wx * layer
    scale = 1.0 / math.sqrt(cells * places)

    swap = [(i, i ^ 1) for i in range(lax.axis_size("blk"))]
    two = shift(orbitals, "blk", -2)
    psi = lax.optimization_barrier(orbitals.reshape(states, cells))

    tmp = pltpu.VMEM((-(-9 * max(wx, wy) // 16) * 16, wz), F32)
    tail, head, hy = call(
        functools.partial(edges, shape=shape),
        [shape_of((states, layer + wz), BF16)] * 2 + [shape_of((states, 2 * (line + wz)), BF16)],
        [psi, coupling, pot_grad],
        scratch=[tmp],
    )
    hx = [shift(tail, "dx", -1), shift(head, "dx", 1)]
    hy = both_sides(hy, "dy")

    coeffs = pltpu.VMEM((3, wx, wy, wz), F32)
    ends = [pltpu.VMEM((2, 3, wy, wz), F32), pltpu.VMEM((2, 3, wx, wz), F32)]
    u, w, w_mate = [], [], []
    for layers, sides in ((range(1, wx - 1), []), ((0, wx - 1), hx)):
        if sides:
            sides, u[0] = lax.optimization_barrier((sides, u[0]))
        field = shape_of((3 * states, len(layers) * layer), BF16)
        results = call(
            functools.partial(operators, layers=layers, shape=shape),
            [field, field],
            [psi, *sides, hy, coupling, pot_grad],
            scratch=[coeffs] * 3 + [tmp, *ends],
        )
        u.append(results[0])
        w.append(results[1])
        w_mate.append(lax.ppermute(w[-1], "blk", swap))
    tall, wide = shape_of((3 * states, states), F32), shape_of((states, 3 * states), F32)
    (own,) = call(
        functools.partial(own_tiles, layer=layer, scale=scale), [tall], [*u, psi]
    )

    def cut_shapes(slots):
        shape = (slots, 3, rows, states)
        return [shape_of(shape, F32)] + [shape_of(shape, BF16)] * (places - 1)

    given = dict(layer=layer, plane=plane, scale=scale)
    two, own = lax.optimization_barrier((two, own))
    two = lax.optimization_barrier(two.reshape(states, cells))
    one = lax.ppermute(two, "blk", swap)
    mate, kept_there, *sends = call(
        functools.partial(there_tiles, **given),
        [wide, *cut_shapes(2)],
        [*w, *w_mate, two, psi, own],
        scratch=[pltpu.VMEM(wide.shape, F32)] * 2,
        us=1,
    )
    first = exchange(sends)
    one, mate = lax.optimization_barrier((one, mate))
    kept, *sends = call(
        functools.partial(here_tiles, **given),
        cut_shapes(3),
        [*u, two, one, own, mate],
        scratch=[pltpu.VMEM(tall.shape, F32)] * 2,
        us=1,
    )
    second = exchange(sends)
    first, kept = lax.optimization_barrier((first, kept))
    small = shape_of((3, rows, states), F32)
    there, ours = call(add, [small, small], [kept_there, *first])
    back_two, back_one = shift(there, "blk", 2), shift(ours, "blk", 2)
    (out,) = call(
        assemble,
        [shape_of((3, 5, rows, states), F32)],
        [kept, *second, ours, back_two, back_one],
    )
    return out


def solution(mesh):
    in_specs = (P("blk", "dx", "dy", None), P("dx", "dy", None), P(None, "dx", "dy", None))
    out_specs = P(None, None, ("blk", "dx", "dy"), None)
    return jax.shard_map(
        on_device, mesh=mesh, in_specs=in_specs, out_specs=out_specs, check_vma=False
    )
```

```python
import functools
import math

import jax
import jax.numpy as jnp
from jax import lax
from jax.experimental import pallas as pl
from jax.experimental.pallas import tpu as pltpu
from jax.sharding import PartitionSpec as P

F32, BF16 = jnp.float32, jnp.bfloat16
VMEM = pl.BlockSpec(memory_space=pltpu.VMEM)
LIMIT = 12 * 1024 * 1024
NT = (((1,), (1,)), ((), ()))
CHUNK = 16


def shape_of(shape, dtype):
    return jax.ShapeDtypeStruct(shape, dtype)


def shift(block, axis, distance):
    count = lax.axis_size(axis)
    return lax.ppermute(block, axis, [((i + distance) % count, i) for i in range(count)])


def both_sides(pair, axis):
    if lax.axis_size(axis) == 2:
        return shift(pair, axis, 1)
    tail, head = jnp.split(pair, 2, axis=1)
    return jnp.concatenate([shift(tail, axis, -1), shift(head, axis, 1)], axis=1)


def both_sides_in_two(first, second, axis):
    if lax.axis_size(axis) == 2:
        return [shift(first, axis, 1), shift(second, axis, 1)]
    pair = both_sides(jnp.concatenate([first, second], axis=1), axis)
    return jnp.split(pair, [first.shape[1]], axis=1)


def exchange(sends):
    nx, ny = lax.axis_size("dx"), lax.axis_size("dy")
    got = []
    for o, piece in enumerate(sends, 1):
        ox, oy = o // ny, o % ny
        route = [
            (i * ny + j, ((i + ox) % nx) * ny + (j + oy) % ny) for i in range(nx) for j in range(ny)
        ]
        got.append(lax.ppermute(piece, ("dx", "dy"), route))
    return got


def call(body, outs, operands, scratch=(), specs=None, out_specs=None, us=0):
    run = pl.pallas_call(
        body,
        out_shape=outs,
        in_specs=specs or [VMEM] * len(operands),
        out_specs=out_specs or [VMEM] * len(outs),
        scratch_shapes=list(scratch),
        compiler_params=pltpu.CompilerParams(vmem_limit_bytes=LIMIT),
        cost_estimate=pl.CostEstimate(
            flops=0, bytes_accessed=int(us * 3e6), transcendentals=0
        ),
    )
    return list(run(*operands))


def destinations(nx, ny):
    x, y = lax.axis_index("dx"), lax.axis_index("dy")
    return [
        lax.rem(x + ox, nx) * ny + lax.rem(y + oy, ny) for ox in range(nx) for oy in range(ny)
    ]


def thirds(value):
    high = value.astype(BF16).astype(F32)
    middle = (value - high).astype(BF16).astype(F32)
    return high, middle, value - high - middle


def parted(parts, at):
    first = parts[0].shape[1]
    return (parts[0], at) if at < first else (parts[1], at - first)


def edges(psi, coupling, grad, first, second, hy, tmp, *, shape):
    wx, wy, wz = shape
    layer, line = wy * wz, wx * wz
    for side, (x, y) in enumerate(((wx - 1, wy - 1), (0, 0))):
        to_x, to_y = side * (layer + wz), side * (line + wz)
        for i in range(wy):
            ref, to = parted((first, second), to_x + i * wz)
            at = x * layer + i * wz
            ref[:, to : to + wz] = psi[:, at : at + wz]
        for i in range(wx):
            at = i * layer + y * wz
            hy[:, to_y + i * wz : to_y + (i + 1) * wz] = psi[:, at : at + wz]
        for k in range(3):
            for n, third in enumerate(thirds(coupling[x] * grad[k, x])):
                tmp[(3 * k + n) * wy : (3 * k + n + 1) * wy] = third
        ref, to = parted((first, second), to_x + layer)
        ref[: tmp.shape[0], to : to + wz] = tmp[...].astype(BF16)
        for k in range(3):
            for n, third in enumerate(thirds(coupling[:, y] * grad[k, :, y])):
                tmp[(3 * k + n) * wx : (3 * k + n + 1) * wx] = third
        hy[: tmp.shape[0], to_y + line : to_y + line + wz] = tmp[...].astype(BF16)


def operators(*refs, layers, shape):
    psi, *refs = refs
    outer = len(refs) == 13
    hx = refs[:2]
    hy, coupling, grad, u, w, half, back, ahead, tmp, ex, ey = refs[-11:]
    wx, wy, wz = shape
    layer, line = wy * wz, wx * wz
    states = psi.shape[0]
    half[...] = 0.5 * (coupling[...][None] * grad[...])

    def unpack(ref, at, to, count):
        tmp[...] = ref[: tmp.shape[0], at : at + wz].astype(F32)
        for k in range(3):
            third = [tmp[(3 * k + n) * count : (3 * k + n + 1) * count] for n in range(3)]
            to[k] = 0.5 * (third[0] + third[1] + third[2])

    for side in range(2):
        if outer:
            unpack(*parted(hx, side * (layer + wz) + layer), ex.at[side], wy)
        unpack(hy, side * (line + wz) + line, ey.at[side], wx)
    for k in range(3):
        for x in layers:
            back[k, x] = pltpu.roll(half[k, x], 1, 1)
            ahead[k, x] = pltpu.roll(half[k, x], wz - 1, 1)

    def coeff(k, x, y):
        if x < 0 or x >= wx:
            return ex[int(x >= wx), k, y : y + 1, :]
        if y < 0 or y >= wy:
            return ey[int(y >= wy), k, x : x + 1, :]
        return half[k, x, y : y + 1, :]

    def group(step, _):
        r = pl.ds(pl.multiple_of(step * CHUNK, CHUNK), CHUNK)

        def field(x, y):
            if x < 0 or x >= wx:
                ref, at = parted(hx, int(x >= wx) * (layer + wz) + y * wz)
                return ref[r, at : at + wz].astype(F32)
            if y < 0 or y >= wy:
                at = int(y >= wy) * (line + wz) + x * wz
                return hy[r, at : at + wz].astype(F32)
            at = x * layer + y * wz
            return psi[r, at : at + wz].astype(F32)

        for n, x in enumerate(layers):
            for y in range(wy):
                here = field(x, y)
                xb, xa = field(x - 1, y), field(x + 1, y)
                yb, ya = field(x, y - 1), field(x, y + 1)
                zb, za = pltpu.roll(here, 1, 1), pltpu.roll(here, wz - 1, 1)
                gx, gy, gz = xa - xb, ya - yb, za - zb
                c1, c2, c3 = [coeff(k, x, y) for k in range(3)]
                cols = slice(n * layer + y * wz, n * layer + (y + 1) * wz)

                def put(ref, k, value):
                    place = pl.ds(pl.multiple_of(k * states + step * CHUNK, CHUNK), CHUNK)
                    ref[place, cols] = value.astype(BF16)

                put(u, 0, c2 * gz - c3 * gy)
                put(u, 1, c3 * gx - c1 * gz)
                put(u, 2, c1 * gy - c2 * gx)

                def dx(k):
                    return coeff(k, x + 1, y) * xa - coeff(k, x - 1, y) * xb

                def dy(k):
                    return coeff(k, x, y + 1) * ya - coeff(k, x, y - 1) * yb

                def dz(k):
                    return ahead[k, x, y : y + 1, :] * za - back[k, x, y : y + 1, :] * zb

                put(w, 0, dy(2) - dz(1))
                put(w, 1, dz(0) - dx(2))
                put(w, 2, dx(1) - dy(0))
        return 0

    lax.fori_loop(0, states // CHUNK, group, 0)


def product(fields, panel, layer, flip=False):
    inner, outer = fields
    cells = inner.shape[1] + outer.shape[1]
    total = 0.0
    for a, start, stop in (
        (inner[...], layer, cells - layer),
        (outer[:, :layer], 0, layer),
        (outer[:, layer:], cells - layer, cells),
    ):
        b = panel(slice(start, stop))
        a, b = (b, a) if flip else (a, b)
        total = total + lax.dot_general(a, b, NT, preferred_element_type=F32)
    return total


def stacked(*panels):
    return lambda cols: jnp.concatenate([panel[:, cols] for panel in panels], axis=0)


def cut(outs, slots, plane, states):
    rows = states // math.prod(plane)
    for ref, dest in zip(outs, destinations(*plane)):
        for n, slot in enumerate(slots):
            for k in range(3):
                ref[n, k] = slot(k, dest * rows, rows).astype(ref.dtype)


def tall_rows(tile):
    states = tile.shape[0] // 3

    def rows_of(k, start, rows):
        return tile[pl.ds(pl.multiple_of(k * states + start, rows), rows), :]

    return rows_of


def wide_rows(tile):
    states = tile.shape[0]

    def rows_of(k, start, rows):
        cols = slice(k * states, (k + 1) * states)
        return tile[pl.ds(pl.multiple_of(start, rows), rows), cols]

    return rows_of


def either(first, second):
    core = lax.rem(lax.axis_index("blk"), 2)
    return lambda *place: jnp.where(core == 0, first(*place), second(*place))


def near_tiles(*refs, layer, plane, scale):
    u, panels, outs, (here, here_mate) = refs[:2], refs[2:5], refs[5:-2], refs[-2:]
    states = panels[0].shape[0]
    both = product(u, stacked(*panels), layer) * scale
    here[...], here_mate[...] = both[:, :states], both[:, states:]
    cut(outs, (tall_rows(here), tall_rows(here_mate)), plane, states)


def there_tiles(*refs, layer, scale):
    w, w_mate, (two, there, there_mate) = refs[:2], refs[2:4], refs[4:]
    there[...] = product(w, stacked(two), layer, True) * scale
    there_mate[...] = product(w_mate, stacked(two), layer, True) * scale


def here_tiles(*refs, layer, plane, scale):
    u, (two, one, there, there_mate), refs = refs[:2], refs[2:6], refs[6:]
    outs, (here_two, here_one) = refs[:-2], refs[-2:]
    states = two.shape[0]
    both = product(u, stacked(two, one), layer) * scale
    here_two[...], here_one[...] = both[:, :states], both[:, states:]
    third = either(tall_rows(here_one), wide_rows(there_mate))
    cut(outs, (tall_rows(here_two), wide_rows(there), third), plane, states)


def total_of(group, n, k):
    total = group[0][n, k]
    for part in group[1:]:
        total = total + part[n, k].astype(F32)
    return total


def add(*refs):
    group, back = refs[:-1], refs[-1]
    for k in range(3):
        total = total_of(group, 1, k)
        back[0, k] = total.astype(BF16)
        back[1, k] = (total - back[0, k].astype(F32)).astype(BF16)
        back[2, k] = total_of(group, 2, k).astype(BF16)


def assemble(*refs):
    size = (len(refs) - 2) // 2
    early, late, (back, out) = refs[:size], refs[size:-2], refs[-2:]
    core = lax.rem(lax.axis_index("blk"), 2)
    for k in range(3):
        mate = total_of(early, 1, k)
        out[k, 0] = total_of(late, 0, k)
        out[k, 1] = jnp.where(core == 0, total_of(late, 2, k), mate)
        out[k, 2] = total_of(early, 0, k)
        out[k, 3] = jnp.where(core == 0, mate, back[2, k].astype(F32))
        out[k, 4] = back[0, k].astype(F32) + back[1, k].astype(F32)


def on_device(orbitals, coupling, pot_grad):
    states, wx, wy, wz = orbitals.shape
    shape = (wx, wy, wz)
    plane = (lax.axis_size("dx"), lax.axis_size("dy"))
    places = math.prod(plane)
    rows = states // places
    layer, line = wy * wz, wx * wz
    cells = wx * layer
    scale = 1.0 / math.sqrt(cells * places)

    swap = [(i, i ^ 1) for i in range(lax.axis_size("blk"))]
    two = shift(orbitals, "blk", -2)
    psi = lax.optimization_barrier(orbitals.reshape(states, cells))
    mate = [lax.ppermute(half, "blk", swap) for half in jnp.split(psi, 2, axis=0)]

    tmp = pltpu.VMEM((-(-9 * max(wx, wy) // 16) * 16, wz), F32)
    widths = (layer + wz + layer // 4, layer + wz - layer // 4, 2 * (line + wz))
    *hx, hy = call(
        functools.partial(edges, shape=shape),
        [shape_of((states, width), BF16) for width in widths],
        [psi, coupling, pot_grad],
        scratch=[tmp],
    )
    hx = both_sides_in_two(*hx, "dx")
    hy = both_sides(hy, "dy")

    coeffs = pltpu.VMEM((3, wx, wy, wz), F32)
    ends = [pltpu.VMEM((2, 3, wy, wz), F32), pltpu.VMEM((2, 3, wx, wz), F32)]
    u, w, w_mate = [], [], []
    for layers, sides in ((range(1, wx - 1), []), ((0, wx - 1), hx)):
        if sides:
            sides, u[0] = lax.optimization_barrier((sides, u[0]))
        field = shape_of((3 * states, len(layers) * layer), BF16)
        results = call(
            functools.partial(operators, layers=layers, shape=shape),
            [field, field],
            [psi, *sides, hy, coupling, pot_grad],
            scratch=[coeffs] * 3 + [tmp, *ends],
        )
        u.append(results[0])
        w.append(results[1])
        w_mate.append(lax.ppermute(w[-1], "blk", swap))
    tall, wide = shape_of((3 * states, states), F32), shape_of((states, 3 * states), F32)
    given = dict(layer=layer, scale=scale)

    def summed(body, slots, operands):
        shape = (slots, 3, rows, states)
        kept, *sends = call(
            functools.partial(body, plane=plane, **given),
            [shape_of(shape, F32)] + [shape_of(shape, BF16)] * (places - 1),
            operands,
            scratch=[pltpu.VMEM(tall.shape, F32)] * 2,
        )
        return [kept, *exchange(sends)]

    early = summed(near_tiles, 2, [*u, psi, *mate])
    two, early = lax.optimization_barrier((two, early))
    two = lax.optimization_barrier(two.reshape(states, cells))
    one = lax.ppermute(two, "blk", swap)
    there = call(
        functools.partial(there_tiles, **given), [wide, wide], [*w, *w_mate, two]
    )
    one, there = lax.optimization_barrier((one, there))
    late = summed(here_tiles, 3, [*u, two, one, *there])
    (back,) = call(add, [shape_of((3, 3, rows, states), BF16)], late)
    back = shift(back, "blk", 2)
    (out,) = call(assemble, [shape_of((3, 5, rows, states), F32)], [*early, *late, back])
    return out


def solution(mesh):
    in_specs = (P("blk", "dx", "dy", None), P("dx", "dy", None), P(None, "dx", "dy", None))
    out_specs = P(None, None, ("blk", "dx", "dy"), None)
    return jax.shard_map(
        on_device, mesh=mesh, in_specs=in_specs, out_specs=out_specs, check_vma=False
    )
```

```python
import functools
import math

import jax
import jax.numpy as jnp
from jax import lax
from jax.experimental import pallas as pl
from jax.experimental.pallas import tpu as pltpu
from jax.sharding import PartitionSpec as P

F32, BF16 = jnp.float32, jnp.bfloat16
VMEM = pl.BlockSpec(memory_space=pltpu.VMEM)
LIMIT = 12 * 1024 * 1024
NT = (((1,), (1,)), ((), ()))
CHUNK = 16


def shape_of(shape, dtype):
    return jax.ShapeDtypeStruct(shape, dtype)


def shift(block, axis, distance):
    count = lax.axis_size(axis)
    return lax.ppermute(block, axis, [((i + distance) % count, i) for i in range(count)])


def both_sides(pair, axis):
    if lax.axis_size(axis) == 2:
        return shift(pair, axis, 1)
    tail, head = jnp.split(pair, 2, axis=1)
    return jnp.concatenate([shift(tail, axis, -1), shift(head, axis, 1)], axis=1)


def exchange(sends):
    nx, ny = lax.axis_size("dx"), lax.axis_size("dy")
    got = []
    for o, piece in enumerate(sends, 1):
        ox, oy = o // ny, o % ny
        route = [
            (i * ny + j, ((i + ox) % nx) * ny + (j + oy) % ny) for i in range(nx) for j in range(ny)
        ]
        got.append(lax.ppermute(piece, ("dx", "dy"), route))
    return got


def call(body, outs, operands, scratch=(), specs=None, out_specs=None, us=0):
    run = pl.pallas_call(
        body,
        out_shape=outs,
        in_specs=specs or [VMEM] * len(operands),
        out_specs=out_specs or [VMEM] * len(outs),
        scratch_shapes=list(scratch),
        compiler_params=pltpu.CompilerParams(vmem_limit_bytes=LIMIT),
        cost_estimate=pl.CostEstimate(
            flops=0, bytes_accessed=int(us * 3e6), transcendentals=0
        ),
    )
    return list(run(*operands))


def destinations(nx, ny):
    x, y = lax.axis_index("dx"), lax.axis_index("dy")
    return [
        lax.rem(x + ox, nx) * ny + lax.rem(y + oy, ny) for ox in range(nx) for oy in range(ny)
    ]


def thirds(value):
    high = value.astype(BF16).astype(F32)
    middle = (value - high).astype(BF16).astype(F32)
    return high, middle, value - high - middle


def edges(psi, coupling, grad, tail, head, hy, tmp, *, shape):
    wx, wy, wz = shape
    layer, line = wy * wz, wx * wz
    for side, (x, y, hx) in enumerate(((wx - 1, wy - 1, tail), (0, 0, head))):
        to_y = side * (line + wz)
        hx[:, :layer] = psi[:, x * layer : (x + 1) * layer]
        for i in range(wx):
            at = i * layer + y * wz
            hy[:, to_y + i * wz : to_y + (i + 1) * wz] = psi[:, at : at + wz]
        for k in range(3):
            for n, third in enumerate(thirds(coupling[x] * grad[k, x])):
                tmp[(3 * k + n) * wy : (3 * k + n + 1) * wy] = third
        hx[: tmp.shape[0], layer:] = tmp[...].astype(BF16)
        for k in range(3):
            for n, third in enumerate(thirds(coupling[:, y] * grad[k, :, y])):
                tmp[(3 * k + n) * wx : (3 * k + n + 1) * wx] = third
        hy[: tmp.shape[0], to_y + line : to_y + line + wz] = tmp[...].astype(BF16)


def operators(*refs, layers, shape):
    psi, *refs = refs
    outer = len(refs) == 13
    hx = refs[:2]
    hy, coupling, grad, u, w, half, back, ahead, tmp, ex, ey = refs[-11:]
    wx, wy, wz = shape
    layer, line = wy * wz, wx * wz
    states = psi.shape[0]
    half[...] = 0.5 * (coupling[...][None] * grad[...])

    def unpack(ref, at, to, count):
        tmp[...] = ref[: tmp.shape[0], at : at + wz].astype(F32)
        for k in range(3):
            third = [tmp[(3 * k + n) * count : (3 * k + n + 1) * count] for n in range(3)]
            to[k] = 0.5 * (third[0] + third[1] + third[2])

    for side in range(2):
        if outer:
            unpack(hx[side], layer, ex.at[side], wy)
        unpack(hy, side * (line + wz) + line, ey.at[side], wx)
    for k in range(3):
        for x in layers:
            back[k, x] = pltpu.roll(half[k, x], 1, 1)
            ahead[k, x] = pltpu.roll(half[k, x], wz - 1, 1)

    def coeff(k, x, y):
        if x < 0 or x >= wx:
            return ex[int(x >= wx), k, y : y + 1, :]
        if y < 0 or y >= wy:
            return ey[int(y >= wy), k, x : x + 1, :]
        return half[k, x, y : y + 1, :]

    def group(step, _):
        r = pl.ds(pl.multiple_of(step * CHUNK, CHUNK), CHUNK)

        def field(x, y):
            if x < 0 or x >= wx:
                return hx[int(x >= wx)][r, y * wz : (y + 1) * wz].astype(F32)
            if y < 0 or y >= wy:
                at = int(y >= wy) * (line + wz) + x * wz
                return hy[r, at : at + wz].astype(F32)
            at = x * layer + y * wz
            return psi[r, at : at + wz].astype(F32)

        for n, x in enumerate(layers):
            for y in range(wy):
                here = field(x, y)
                xb, xa = field(x - 1, y), field(x + 1, y)
                yb, ya = field(x, y - 1), field(x, y + 1)
                zb, za = pltpu.roll(here, 1, 1), pltpu.roll(here, wz - 1, 1)
                gx, gy, gz = xa - xb, ya - yb, za - zb
                c1, c2, c3 = [coeff(k, x, y) for k in range(3)]
                cols = slice(n * layer + y * wz, n * layer + (y + 1) * wz)

                def put(ref, k, value):
                    place = pl.ds(pl.multiple_of(k * states + step * CHUNK, CHUNK), CHUNK)
                    ref[place, cols] = value.astype(BF16)

                put(u, 0, c2 * gz - c3 * gy)
                put(u, 1, c3 * gx - c1 * gz)
                put(u, 2, c1 * gy - c2 * gx)

                def dx(k):
                    return coeff(k, x + 1, y) * xa - coeff(k, x - 1, y) * xb

                def dy(k):
                    return coeff(k, x, y + 1) * ya - coeff(k, x, y - 1) * yb

                def dz(k):
                    return ahead[k, x, y : y + 1, :] * za - back[k, x, y : y + 1, :] * zb

                put(w, 0, dy(2) - dz(1))
                put(w, 1, dz(0) - dx(2))
                put(w, 2, dx(1) - dy(0))
        return 0

    lax.fori_loop(0, states // CHUNK, group, 0)


def product(fields, panel, layer, flip=False):
    inner, outer = fields
    cells = inner.shape[1] + outer.shape[1]
    total = 0.0
    for a, start, stop in (
        (inner[...], layer, cells - layer),
        (outer[:, :layer], 0, layer),
        (outer[:, layer:], cells - layer, cells),
    ):
        b = panel(slice(start, stop))
        a, b = (b, a) if flip else (a, b)
        total = total + lax.dot_general(a, b, NT, preferred_element_type=F32)
    return total


def stacked(*panels):
    return lambda cols: jnp.concatenate([panel[:, cols] for panel in panels], axis=0)


def own_tiles(*refs, layer, scale):
    u, (psi, own) = refs[:2], refs[2:]
    own[...] = product(u, stacked(psi), layer) * scale


def cut(outs, slots, plane, states):
    rows = states // math.prod(plane)
    for ref, dest in zip(outs, destinations(*plane)):
        for n, slot in enumerate(slots):
            for k in range(3):
                ref[n, k] = slot(k, dest * rows, rows).astype(ref.dtype)


def tall_rows(tile):
    states = tile.shape[0] // 3

    def rows_of(k, start, rows):
        return tile[pl.ds(pl.multiple_of(k * states + start, rows), rows), :]

    return rows_of


def wide_rows(tile):
    states = tile.shape[0]

    def rows_of(k, start, rows):
        cols = slice(k * states, (k + 1) * states)
        return tile[pl.ds(pl.multiple_of(start, rows), rows), cols]

    return rows_of


def either(first, second):
    core = lax.rem(lax.axis_index("blk"), 2)
    return lambda *place: jnp.where(core == 0, first(*place), second(*place))


def there_tiles(*refs, layer, plane, scale):
    w, w_mate, (two, psi, own), refs = refs[:2], refs[2:4], refs[4:7], refs[7:]
    mate, outs, (there, there_mate) = refs[0], refs[1:-2], refs[-2:]
    states = two.shape[0]
    there[...] = product(w, stacked(two), layer, True) * scale
    both = product(w_mate, stacked(two, psi), layer, True) * scale
    there_mate[...], mate[...] = both[:states], both[states:]
    slots = (wide_rows(there), either(tall_rows(own), wide_rows(there_mate)))
    cut(outs, slots, plane, states)


def here_tiles(*refs, layer, plane, scale):
    u, (two, one, own, mate), refs = refs[:2], refs[2:6], refs[6:]
    outs, (here_two, here_one) = refs[:-2], refs[-2:]
    states = two.shape[0]
    both = product(u, stacked(two, one), layer) * scale
    here_two[...], here_one[...] = both[:, :states], both[:, states:]
    slots = (
        tall_rows(here_two), wide_rows(mate), either(tall_rows(here_one), tall_rows(own))
    )
    cut(outs, slots, plane, states)


def total_of(group, n, k):
    total = group[0][n, k]
    for part in group[1:]:
        total = total + part[n, k].astype(F32)
    return total


def add(*refs):
    group, (ours, back) = refs[:-2], refs[-2:]
    for k in range(3):
        total = total_of(group, 1, k)
        ours[k], back[1, k] = total, total.astype(BF16)
        back[0, k] = total_of(group, 0, k).astype(BF16)


def assemble(*refs):
    group, (ours, back, out) = refs[:-3], refs[-3:]
    core = lax.rem(lax.axis_index("blk"), 2)
    for k in range(3):
        mate, third = total_of(group, 1, k), total_of(group, 2, k)
        out[k, 0] = total_of(group, 0, k)
        out[k, 1] = jnp.where(core == 0, third, mate)
        out[k, 2] = jnp.where(core == 0, ours[k], third)
        out[k, 3] = jnp.where(core == 0, mate, back[1, k].astype(F32))
        out[k, 4] = back[0, k].astype(F32)


def on_device(orbitals, coupling, pot_grad):
    states, wx, wy, wz = orbitals.shape
    shape = (wx, wy, wz)
    plane = (lax.axis_size("dx"), lax.axis_size("dy"))
    places = math.prod(plane)
    rows = states // places
    layer, line = wy * wz, wx * wz
    cells = wx * layer
    scale = 1.0 / math.sqrt(cells * places)

    swap = [(i, i ^ 1) for i in range(lax.axis_size("blk"))]
    two = shift(orbitals, "blk", -2)
    psi = lax.optimization_barrier(orbitals.reshape(states, cells))

    tmp = pltpu.VMEM((-(-9 * max(wx, wy) // 16) * 16, wz), F32)
    tail, head, hy = call(
        functools.partial(edges, shape=shape),
        [shape_of((states, layer + wz), BF16)] * 2 + [shape_of((states, 2 * (line + wz)), BF16)],
        [psi, coupling, pot_grad],
        scratch=[tmp],
    )
    hx = [shift(tail, "dx", -1), shift(head, "dx", 1)]
    hy = both_sides(hy, "dy")

    coeffs = pltpu.VMEM((3, wx, wy, wz), F32)
    ends = [pltpu.VMEM((2, 3, wy, wz), F32), pltpu.VMEM((2, 3, wx, wz), F32)]
    u, w, w_mate = [], [], []
    for layers, sides in ((range(1, wx - 1), []), ((0, wx - 1), hx)):
        if sides:
            sides, u[0] = lax.optimization_barrier((sides, u[0]))
        field = shape_of((3 * states, len(layers) * layer), BF16)
        results = call(
            functools.partial(operators, layers=layers, shape=shape),
            [field, field],
            [psi, *sides, hy, coupling, pot_grad],
            scratch=[coeffs] * 3 + [tmp, *ends],
        )
        u.append(results[0])
        w.append(results[1])
        w_mate.append(lax.ppermute(w[-1], "blk", swap))
    tall, wide = shape_of((3 * states, states), F32), shape_of((states, 3 * states), F32)
    (own,) = call(
        functools.partial(own_tiles, layer=layer, scale=scale), [tall], [*u, psi]
    )

    def cut_shapes(slots):
        shape = (slots, 3, rows, states)
        return [shape_of(shape, F32)] + [shape_of(shape, BF16)] * (places - 1)

    given = dict(layer=layer, plane=plane, scale=scale)
    two, own = lax.optimization_barrier((two, own))
    two = lax.optimization_barrier(two.reshape(states, cells))
    one = lax.ppermute(two, "blk", swap)
    mate, kept_there, *sends = call(
        functools.partial(there_tiles, **given),
        [wide, *cut_shapes(2)],
        [*w, *w_mate, two, psi, own],
        scratch=[pltpu.VMEM(wide.shape, F32)] * 2,
        us=1,
    )
    first = exchange(sends)
    one, mate = lax.optimization_barrier((one, mate))
    kept, *sends = call(
        functools.partial(here_tiles, **given),
        cut_shapes(3),
        [*u, two, one, own, mate],
        scratch=[pltpu.VMEM(tall.shape, F32)] * 2,
        us=1,
    )
    second = exchange(sends)
    first, kept = lax.optimization_barrier((first, kept))
    small = (3, rows, states)
    ours, back = call(
        add, [shape_of(small, F32), shape_of((2, *small), BF16)], [kept_there, *first]
    )
    back = shift(back, "blk", 2)
    (out,) = call(
        assemble, [shape_of((3, 5, rows, states), F32)], [kept, *second, ours, back]
    )
    return out


def solution(mesh):
    in_specs = (P("blk", "dx", "dy", None), P("dx", "dy", None), P(None, "dx", "dy", None))
    out_specs = P(None, None, ("blk", "dx", "dy"), None)
    return jax.shard_map(
        on_device, mesh=mesh, in_specs=in_specs, out_specs=out_specs, check_vma=False
    )
```

```python
import functools
import math

import jax
import jax.numpy as jnp
from jax import lax
from jax.experimental import pallas as pl
from jax.experimental.pallas import tpu as pltpu
from jax.sharding import PartitionSpec as P

F32, BF16 = jnp.float32, jnp.bfloat16
VMEM = pl.BlockSpec(memory_space=pltpu.VMEM)
LIMIT = 12 * 1024 * 1024
NT = (((1,), (1,)), ((), ()))
CHUNK = 16


def shape_of(shape, dtype):
    return jax.ShapeDtypeStruct(shape, dtype)


def shift(block, axis, distance):
    count = lax.axis_size(axis)
    return lax.ppermute(block, axis, [((i + distance) % count, i) for i in range(count)])


def both_sides(pair, axis):
    if lax.axis_size(axis) == 2:
        return shift(pair, axis, 1)
    tail, head = jnp.split(pair, 2, axis=1)
    return jnp.concatenate([shift(tail, axis, -1), shift(head, axis, 1)], axis=1)


def exchange(sends):
    nx, ny = lax.axis_size("dx"), lax.axis_size("dy")
    got = []
    for o, piece in reversed(list(enumerate(sends, 1))):
        ox, oy = o // ny, o % ny
        route = [
            (i * ny + j, ((i + ox) % nx) * ny + (j + oy) % ny) for i in range(nx) for j in range(ny)
        ]
        got.append(lax.ppermute(piece, ("dx", "dy"), route))
    return got


def call(body, outs, operands, scratch=(), specs=None, out_specs=None, us=0):
    run = pl.pallas_call(
        body,
        out_shape=outs,
        in_specs=specs or [VMEM] * len(operands),
        out_specs=out_specs or [VMEM] * len(outs),
        scratch_shapes=list(scratch),
        compiler_params=pltpu.CompilerParams(vmem_limit_bytes=LIMIT),
        cost_estimate=pl.CostEstimate(
            flops=0, bytes_accessed=int(us * 3e6), transcendentals=0
        ),
    )
    return list(run(*operands))


def destinations(nx, ny):
    x, y = lax.axis_index("dx"), lax.axis_index("dy")
    return [
        lax.rem(x + ox, nx) * ny + lax.rem(y + oy, ny) for ox in range(nx) for oy in range(ny)
    ]


def thirds(value):
    high = value.astype(BF16).astype(F32)
    middle = (value - high).astype(BF16).astype(F32)
    return high, middle, value - high - middle


def edges(psi, coupling, grad, tail, head, hy, tmp, *, shape):
    wx, wy, wz = shape
    layer, line = wy * wz, wx * wz
    for side, (x, y, hx) in enumerate(((wx - 1, wy - 1, tail), (0, 0, head))):
        to_y = side * (line + wz)
        hx[:, :layer] = psi[:, x * layer : (x + 1) * layer]
        for i in range(wx):
            at = i * layer + y * wz
            hy[:, to_y + i * wz : to_y + (i + 1) * wz] = psi[:, at : at + wz]
        for k in range(3):
            for n, third in enumerate(thirds(coupling[x] * grad[k, x])):
                tmp[(3 * k + n) * wy : (3 * k + n + 1) * wy] = third
        hx[: tmp.shape[0], layer:] = tmp[...].astype(BF16)
        for k in range(3):
            for n, third in enumerate(thirds(coupling[:, y] * grad[k, :, y])):
                tmp[(3 * k + n) * wx : (3 * k + n + 1) * wx] = third
        hy[: tmp.shape[0], to_y + line : to_y + line + wz] = tmp[...].astype(BF16)


def operators(*refs, layers, shape):
    psi, *refs = refs
    outer = len(refs) == 13
    hx = refs[:2]
    hy, coupling, grad, u, w, half, back, ahead, tmp, ex, ey = refs[-11:]
    wx, wy, wz = shape
    layer, line = wy * wz, wx * wz
    states = psi.shape[0]
    half[...] = 0.5 * (coupling[...][None] * grad[...])

    def unpack(ref, at, to, count):
        tmp[...] = ref[: tmp.shape[0], at : at + wz].astype(F32)
        for k in range(3):
            third = [tmp[(3 * k + n) * count : (3 * k + n + 1) * count] for n in range(3)]
            to[k] = 0.5 * (third[0] + third[1] + third[2])

    for side in range(2):
        if outer:
            unpack(hx[side], layer, ex.at[side], wy)
        unpack(hy, side * (line + wz) + line, ey.at[side], wx)
    for k in range(3):
        for x in layers:
            back[k, x] = pltpu.roll(half[k, x], 1, 1)
            ahead[k, x] = pltpu.roll(half[k, x], wz - 1, 1)

    def coeff(k, x, y):
        if x < 0 or x >= wx:
            return ex[int(x >= wx), k, y : y + 1, :]
        if y < 0 or y >= wy:
            return ey[int(y >= wy), k, x : x + 1, :]
        return half[k, x, y : y + 1, :]

    def group(step, _):
        r = pl.ds(pl.multiple_of(step * CHUNK, CHUNK), CHUNK)

        def field(x, y):
            if x < 0 or x >= wx:
                return hx[int(x >= wx)][r, y * wz : (y + 1) * wz].astype(F32)
            if y < 0 or y >= wy:
                at = int(y >= wy) * (line + wz) + x * wz
                return hy[r, at : at + wz].astype(F32)
            at = x * layer + y * wz
            return psi[r, at : at + wz].astype(F32)

        for n, x in enumerate(layers):
            for y in range(wy):
                here = field(x, y)
                xb, xa = field(x - 1, y), field(x + 1, y)
                yb, ya = field(x, y - 1), field(x, y + 1)
                zb, za = pltpu.roll(here, 1, 1), pltpu.roll(here, wz - 1, 1)
                gx, gy, gz = xa - xb, ya - yb, za - zb
                c1, c2, c3 = [coeff(k, x, y) for k in range(3)]
                cols = slice(n * layer + y * wz, n * layer + (y + 1) * wz)

                def put(ref, k, value):
                    place = pl.ds(pl.multiple_of(k * states + step * CHUNK, CHUNK), CHUNK)
                    ref[place, cols] = value.astype(BF16)

                put(u, 0, c2 * gz - c3 * gy)
                put(u, 1, c3 * gx - c1 * gz)
                put(u, 2, c1 * gy - c2 * gx)

                def dx(k):
                    return coeff(k, x + 1, y) * xa - coeff(k, x - 1, y) * xb

                def dy(k):
                    return coeff(k, x, y + 1) * ya - coeff(k, x, y - 1) * yb

                def dz(k):
                    return ahead[k, x, y : y + 1, :] * za - back[k, x, y : y + 1, :] * zb

                put(w, 0, dy(2) - dz(1))
                put(w, 1, dz(0) - dx(2))
                put(w, 2, dx(1) - dy(0))
        return 0

    lax.fori_loop(0, states // CHUNK, group, 0)


def product(fields, panel, layer, flip=False):
    inner, outer = fields
    cells = inner.shape[1] + outer.shape[1]
    total = 0.0
    for a, start, stop in (
        (inner[...], layer, cells - layer),
        (outer[:, :layer], 0, layer),
        (outer[:, layer:], cells - layer, cells),
    ):
        b = panel(slice(start, stop))
        a, b = (b, a) if flip else (a, b)
        total = total + lax.dot_general(a, b, NT, preferred_element_type=F32)
    return total


def stacked(*panels):
    return lambda cols: jnp.concatenate([panel[:, cols] for panel in panels], axis=0)


def own_tiles(*refs, layer, scale):
    u, (psi, own) = refs[:2], refs[2:]
    own[...] = product(u, stacked(psi), layer) * scale


def cut(outs, slots, plane, states):
    rows = states // math.prod(plane)
    for ref, dest in zip(outs, destinations(*plane)):
        for n, slot in enumerate(slots):
            for k in range(3):
                ref[n, k] = slot(k, dest * rows, rows).astype(ref.dtype)


def tall_rows(tile):
    states = tile.shape[0] // 3

    def rows_of(k, start, rows):
        return tile[pl.ds(pl.multiple_of(k * states + start, rows), rows), :]

    return rows_of


def wide_rows(tile):
    states = tile.shape[0]

    def rows_of(k, start, rows):
        cols = slice(k * states, (k + 1) * states)
        return tile[pl.ds(pl.multiple_of(start, rows), rows), cols]

    return rows_of


def either(first, second):
    core = lax.rem(lax.axis_index("blk"), 2)
    return lambda *place: jnp.where(core == 0, first(*place), second(*place))


def there_tiles(*refs, layer, plane, scale):
    w, w_mate, (two, psi, own), refs = refs[:2], refs[2:4], refs[4:7], refs[7:]
    mate, outs, (there, there_mate) = refs[0], refs[1:-2], refs[-2:]
    states = two.shape[0]
    there[...] = product(w, stacked(two), layer, True) * scale
    both = product(w_mate, stacked(two, psi), layer, True) * scale
    there_mate[...], mate[...] = both[:states], both[states:]
    slots = (wide_rows(there), either(tall_rows(own), wide_rows(there_mate)))
    cut(outs, slots, plane, states)


def here_tiles(*refs, layer, plane, scale):
    u, (two, one, own, mate), refs = refs[:2], refs[2:6], refs[6:]
    outs, (here_two, here_one) = refs[:-2], refs[-2:]
    states = two.shape[0]
    both = product(u, stacked(two, one), layer) * scale
    here_two[...], here_one[...] = both[:, :states], both[:, states:]
    slots = (
        tall_rows(here_two), wide_rows(mate), either(tall_rows(here_one), tall_rows(own))
    )
    cut(outs, slots, plane, states)


def total_of(group, n, k):
    total = group[0][n, k]
    for part in group[1:]:
        total = total + part[n, k].astype(F32)
    return total


def add(*refs):
    group, outs = refs[:-2], refs[-2:]
    for n, out in enumerate(outs):
        for k in range(3):
            out[k] = total_of(group, n, k)


def assemble(*refs):
    group, (ours, back_two, back_one, out) = refs[:-4], refs[-4:]
    core = lax.rem(lax.axis_index("blk"), 2)
    for k in range(3):
        mate, third = total_of(group, 1, k), total_of(group, 2, k)
        out[k, 0] = total_of(group, 0, k)
        out[k, 1] = jnp.where(core == 0, third, mate)
        out[k, 2] = jnp.where(core == 0, ours[k], third)
        out[k, 3] = jnp.where(core == 0, mate, back_one[k])
        out[k, 4] = back_two[k]


def on_device(orbitals, coupling, pot_grad):
    states, wx, wy, wz = orbitals.shape
    shape = (wx, wy, wz)
    plane = (lax.axis_size("dx"), lax.axis_size("dy"))
    places = math.prod(plane)
    rows = states // places
    layer, line = wy * wz, wx * wz
    cells = wx * layer
    scale = 1.0 / math.sqrt(cells * places)

    swap = [(i, i ^ 1) for i in range(lax.axis_size("blk"))]
    two = shift(orbitals, "blk", -2)
    psi = lax.optimization_barrier(orbitals.reshape(states, cells))

    tmp = pltpu.VMEM((-(-9 * max(wx, wy) // 16) * 16, wz), F32)
    tail, head, hy = call(
        functools.partial(edges, shape=shape),
        [shape_of((states, layer + wz), BF16)] * 2 + [shape_of((states, 2 * (line + wz)), BF16)],
        [psi, coupling, pot_grad],
        scratch=[tmp],
    )
    hx = [shift(tail, "dx", -1), shift(head, "dx", 1)]
    hy = both_sides(hy, "dy")

    coeffs = pltpu.VMEM((3, wx, wy, wz), F32)
    ends = [pltpu.VMEM((2, 3, wy, wz), F32), pltpu.VMEM((2, 3, wx, wz), F32)]
    u, w, w_mate = [], [], []
    for layers, sides in ((range(1, wx - 1), []), ((0, wx - 1), hx)):
        if sides:
            sides, u[0] = lax.optimization_barrier((sides, u[0]))
        field = shape_of((3 * states, len(layers) * layer), BF16)
        results = call(
            functools.partial(operators, layers=layers, shape=shape),
            [field, field],
            [psi, *sides, hy, coupling, pot_grad],
            scratch=[coeffs] * 3 + [tmp, *ends],
        )
        u.append(results[0])
        w.append(results[1])
        w_mate.append(lax.ppermute(w[-1], "blk", swap))
    tall, wide = shape_of((3 * states, states), F32), shape_of((states, 3 * states), F32)
    (own,) = call(
        functools.partial(own_tiles, layer=layer, scale=scale), [tall], [*u, psi]
    )

    def cut_shapes(slots):
        shape = (slots, 3, rows, states)
        return [shape_of(shape, F32)] + [shape_of(shape, BF16)] * (places - 1)

    given = dict(layer=layer, plane=plane, scale=scale)
    two, own = lax.optimization_barrier((two, own))
    two = lax.optimization_barrier(two.reshape(states, cells))
    one = lax.ppermute(two, "blk", swap)
    mate, kept_there, *sends = call(
        functools.partial(there_tiles, **given),
        [wide, *cut_shapes(2)],
        [*w, *w_mate, two, psi, own],
        scratch=[pltpu.VMEM(wide.shape, F32)] * 2,
        us=1,
    )
    first = exchange(sends)
    one, mate = lax.optimization_barrier((one, mate))
    kept, *sends = call(
        functools.partial(here_tiles, **given),
        cut_shapes(3),
        [*u, two, one, own, mate],
        scratch=[pltpu.VMEM(tall.shape, F32)] * 2,
        us=1,
    )
    second = exchange(sends)
    first, kept = lax.optimization_barrier((first, kept))
    small = shape_of((3, rows, states), F32)
    there, ours = call(add, [small, small], [kept_there, *first])
    count = lax.axis_size("blk")
    back_two = shift(there, "blk", 2)
    odd = [((i + 2) % count, i) for i in range(1, count, 2)]
    back_one = lax.ppermute(ours, "blk", odd)
    (out,) = call(
        assemble,
        [shape_of((3, 5, rows, states), F32)],
        [kept, *second, ours, back_two, back_one],
    )
    return out


def solution(mesh):
    in_specs = (P("blk", "dx", "dy", None), P("dx", "dy", None), P(None, "dx", "dy", None))
    out_specs = P(None, None, ("blk", "dx", "dy"), None)
    return jax.shard_map(
        on_device, mesh=mesh, in_specs=in_specs, out_specs=out_specs, check_vma=False
    )
```

```python
import functools
import math

import jax
import jax.numpy as jnp
from jax import lax
from jax.experimental import pallas as pl
from jax.experimental.pallas import tpu as pltpu
from jax.sharding import PartitionSpec as P

F32, BF16 = jnp.float32, jnp.bfloat16
VMEM = pl.BlockSpec(memory_space=pltpu.VMEM)
LIMIT = 12 * 1024 * 1024
NT = (((1,), (1,)), ((), ()))
CHUNK = 16


def shape_of(shape, dtype):
    return jax.ShapeDtypeStruct(shape, dtype)


def shift(block, axis, distance):
    count = lax.axis_size(axis)
    return lax.ppermute(block, axis, [((i + distance) % count, i) for i in range(count)])


def both_sides(pair, axis):
    if lax.axis_size(axis) == 2:
        return shift(pair, axis, 1)
    tail, head = jnp.split(pair, 2, axis=1)
    return jnp.concatenate([shift(tail, axis, -1), shift(head, axis, 1)], axis=1)


def exchange(sends):
    nx, ny = lax.axis_size("dx"), lax.axis_size("dy")
    got = []
    for o, piece in reversed(list(enumerate(sends, 1))):
        ox, oy = o // ny, o % ny
        route = [
            (i * ny + j, ((i + ox) % nx) * ny + (j + oy) % ny) for i in range(nx) for j in range(ny)
        ]
        got.append(lax.ppermute(piece, ("dx", "dy"), route))
    return got


def call(body, outs, operands, scratch=(), specs=None, out_specs=None, us=0):
    run = pl.pallas_call(
        body,
        out_shape=outs,
        in_specs=specs or [VMEM] * len(operands),
        out_specs=out_specs or [VMEM] * len(outs),
        scratch_shapes=list(scratch),
        compiler_params=pltpu.CompilerParams(vmem_limit_bytes=LIMIT),
        cost_estimate=pl.CostEstimate(
            flops=0, bytes_accessed=int(us * 3e6), transcendentals=0
        ),
    )
    return list(run(*operands))


def destinations(nx, ny):
    x, y = lax.axis_index("dx"), lax.axis_index("dy")
    return [
        lax.rem(x + ox, nx) * ny + lax.rem(y + oy, ny) for ox in range(nx) for oy in range(ny)
    ]


def thirds(value):
    high = value.astype(BF16).astype(F32)
    middle = (value - high).astype(BF16).astype(F32)
    return high, middle, value - high - middle


def edges(psi, coupling, grad, tail, head, hy, tmp, *, shape):
    wx, wy, wz = shape
    layer, line = wy * wz, wx * wz
    for side, (x, y, hx) in enumerate(((wx - 1, wy - 1, tail), (0, 0, head))):
        to_y = side * (line + wz)
        hx[:, :layer] = psi[:, x * layer : (x + 1) * layer]
        for i in range(wx):
            at = i * layer + y * wz
            hy[:, to_y + i * wz : to_y + (i + 1) * wz] = psi[:, at : at + wz]
        for k in range(3):
            for n, third in enumerate(thirds(coupling[x] * grad[k, x])):
                tmp[(3 * k + n) * wy : (3 * k + n + 1) * wy] = third
        hx[: tmp.shape[0], layer:] = tmp[...].astype(BF16)
        for k in range(3):
            for n, third in enumerate(thirds(coupling[:, y] * grad[k, :, y])):
                tmp[(3 * k + n) * wx : (3 * k + n + 1) * wx] = third
        hy[: tmp.shape[0], to_y + line : to_y + line + wz] = tmp[...].astype(BF16)


def operators(*refs, layers, shape):
    psi, *refs = refs
    outer = len(refs) == 13
    hx = refs[:2]
    hy, coupling, grad, u, w, half, back, ahead, tmp, ex, ey = refs[-11:]
    wx, wy, wz = shape
    layer, line = wy * wz, wx * wz
    states = psi.shape[0]
    half[...] = 0.5 * (coupling[...][None] * grad[...])

    def unpack(ref, at, to, count):
        tmp[...] = ref[: tmp.shape[0], at : at + wz].astype(F32)
        for k in range(3):
            third = [tmp[(3 * k + n) * count : (3 * k + n + 1) * count] for n in range(3)]
            to[k] = 0.5 * (third[0] + third[1] + third[2])

    for side in range(2):
        if outer:
            unpack(hx[side], layer, ex.at[side], wy)
        unpack(hy, side * (line + wz) + line, ey.at[side], wx)
    for k in range(3):
        for x in layers:
            back[k, x] = pltpu.roll(half[k, x], 1, 1)
            ahead[k, x] = pltpu.roll(half[k, x], wz - 1, 1)

    def coeff(k, x, y):
        if x < 0 or x >= wx:
            return ex[int(x >= wx), k, y : y + 1, :]
        if y < 0 or y >= wy:
            return ey[int(y >= wy), k, x : x + 1, :]
        return half[k, x, y : y + 1, :]

    def group(step, _):
        r = pl.ds(pl.multiple_of(step * CHUNK, CHUNK), CHUNK)

        def field(x, y):
            if x < 0 or x >= wx:
                return hx[int(x >= wx)][r, y * wz : (y + 1) * wz].astype(F32)
            if y < 0 or y >= wy:
                at = int(y >= wy) * (line + wz) + x * wz
                return hy[r, at : at + wz].astype(F32)
            at = x * layer + y * wz
            return psi[r, at : at + wz].astype(F32)

        for n, x in enumerate(layers):
            for y in range(wy):
                here = field(x, y)
                xb, xa = field(x - 1, y), field(x + 1, y)
                yb, ya = field(x, y - 1), field(x, y + 1)
                zb, za = pltpu.roll(here, 1, 1), pltpu.roll(here, wz - 1, 1)
                gx, gy, gz = xa - xb, ya - yb, za - zb
                c1, c2, c3 = [coeff(k, x, y) for k in range(3)]
                cols = slice(n * layer + y * wz, n * layer + (y + 1) * wz)

                def put(ref, k, value):
                    place = pl.ds(pl.multiple_of(k * states + step * CHUNK, CHUNK), CHUNK)
                    ref[place, cols] = value.astype(BF16)

                put(u, 0, c2 * gz - c3 * gy)
                put(u, 1, c3 * gx - c1 * gz)
                put(u, 2, c1 * gy - c2 * gx)

                def dx(k):
                    return coeff(k, x + 1, y) * xa - coeff(k, x - 1, y) * xb

                def dy(k):
                    return coeff(k, x, y + 1) * ya - coeff(k, x, y - 1) * yb

                def dz(k):
                    return ahead[k, x, y : y + 1, :] * za - back[k, x, y : y + 1, :] * zb

                put(w, 0, dy(2) - dz(1))
                put(w, 1, dz(0) - dx(2))
                put(w, 2, dx(1) - dy(0))
        return 0

    lax.fori_loop(0, states // CHUNK, group, 0)


def product(fields, panel, layer, flip=False):
    inner, outer = fields
    cells = inner.shape[1] + outer.shape[1]
    total = 0.0
    for a, start, stop in (
        (inner[...], layer, cells - layer),
        (outer[:, :layer], 0, layer),
        (outer[:, layer:], cells - layer, cells),
    ):
        b = panel(slice(start, stop))
        a, b = (b, a) if flip else (a, b)
        total = total + lax.dot_general(a, b, NT, preferred_element_type=F32)
    return total


def stacked(*panels):
    return lambda cols: jnp.concatenate([panel[:, cols] for panel in panels], axis=0)


def own_tiles(*refs, layer, scale):
    u, (psi, own) = refs[:2], refs[2:]
    own[...] = product(u, stacked(psi), layer) * scale


def cut(outs, slots, plane, states):
    rows = states // math.prod(plane)
    for ref, dest in zip(outs, destinations(*plane)):
        for n, slot in enumerate(slots):
            for k in range(3):
                ref[n, k] = slot(k, dest * rows, rows).astype(ref.dtype)


def tall_rows(tile):
    states = tile.shape[0] // 3

    def rows_of(k, start, rows):
        return tile[pl.ds(pl.multiple_of(k * states + start, rows), rows), :]

    return rows_of


def wide_rows(tile):
    states = tile.shape[0]

    def rows_of(k, start, rows):
        cols = slice(k * states, (k + 1) * states)
        return tile[pl.ds(pl.multiple_of(start, rows), rows), cols]

    return rows_of


def there_tiles(*refs, layer, plane, scale):
    w, w_mate, (two, psi), refs = refs[:2], refs[2:4], refs[4:6], refs[6:]
    mate, outs, (there, there_mate) = refs[0], refs[1:-2], refs[-2:]
    states = two.shape[0]
    there[...] = product(w, stacked(two), layer, True) * scale
    both = product(w_mate, stacked(two, psi), layer, True) * scale
    there_mate[...], mate[...] = both[:states], both[states:]
    cut(outs, (wide_rows(there), wide_rows(there_mate)), plane, states)


def here_tiles(*refs, layer, plane, scale):
    u, (two, one, own, mate), refs = refs[:2], refs[2:6], refs[6:]
    outs, (here_two, here_one) = refs[:-2], refs[-2:]
    states = two.shape[0]
    both = product(u, stacked(two, one), layer) * scale
    here_two[...], here_one[...] = both[:, :states], both[:, states:]
    slots = (tall_rows(here_two), tall_rows(here_one), tall_rows(own), wide_rows(mate))
    cut(outs, slots, plane, states)


def total_of(group, n, k):
    total = group[0][n, k]
    for part in group[1:]:
        total = total + part[n, k].astype(F32)
    return total


def add(*refs):
    group, back = refs[:-1], refs[-1]
    for k in range(3):
        total = total_of(group, 0, k)
        back[0, k] = total.astype(BF16)
        back[1, k] = (total - back[0, k].astype(F32)).astype(BF16)
        back[2, k] = total_of(group, 1, k).astype(BF16)


def assemble(*refs):
    group, (back, out) = refs[:-2], refs[-2:]
    core = lax.rem(lax.axis_index("blk"), 2)
    for k in range(3):
        mate = total_of(group, 3, k)
        out[k, 0] = total_of(group, 0, k)
        out[k, 1] = jnp.where(core == 0, total_of(group, 1, k), mate)
        out[k, 2] = total_of(group, 2, k)
        out[k, 3] = jnp.where(core == 0, mate, back[2, k].astype(F32))
        out[k, 4] = back[0, k].astype(F32) + back[1, k].astype(F32)


def on_device(orbitals, coupling, pot_grad):
    states, wx, wy, wz = orbitals.shape
    shape = (wx, wy, wz)
    plane = (lax.axis_size("dx"), lax.axis_size("dy"))
    places = math.prod(plane)
    rows = states // places
    layer, line = wy * wz, wx * wz
    cells = wx * layer
    scale = 1.0 / math.sqrt(cells * places)

    swap = [(i, i ^ 1) for i in range(lax.axis_size("blk"))]
    two = shift(orbitals, "blk", -2)
    psi = lax.optimization_barrier(orbitals.reshape(states, cells))

    tmp = pltpu.VMEM((-(-9 * max(wx, wy) // 16) * 16, wz), F32)
    tail, head, hy = call(
        functools.partial(edges, shape=shape),
        [shape_of((states, layer + wz), BF16)] * 2 + [shape_of((states, 2 * (line + wz)), BF16)],
        [psi, coupling, pot_grad],
        scratch=[tmp],
    )
    hx = [shift(tail, "dx", -1), shift(head, "dx", 1)]
    hy = both_sides(hy, "dy")

    coeffs = pltpu.VMEM((3, wx, wy, wz), F32)
    ends = [pltpu.VMEM((2, 3, wy, wz), F32), pltpu.VMEM((2, 3, wx, wz), F32)]
    u, w, w_mate = [], [], []
    for layers, sides in ((range(1, wx - 1), []), ((0, wx - 1), hx)):
        if sides:
            sides, u[0] = lax.optimization_barrier((sides, u[0]))
        field = shape_of((3 * states, len(layers) * layer), BF16)
        results = call(
            functools.partial(operators, layers=layers, shape=shape),
            [field, field],
            [psi, *sides, hy, coupling, pot_grad],
            scratch=[coeffs] * 3 + [tmp, *ends],
        )
        u.append(results[0])
        w.append(results[1])
        w_mate.append(lax.ppermute(w[-1], "blk", swap))
    tall, wide = shape_of((3 * states, states), F32), shape_of((states, 3 * states), F32)
    (own,) = call(
        functools.partial(own_tiles, layer=layer, scale=scale), [tall], [*u, psi]
    )

    def cut_shapes(slots):
        shape = (slots, 3, rows, states)
        return [shape_of(shape, F32)] + [shape_of(shape, BF16)] * (places - 1)

    given = dict(layer=layer, plane=plane, scale=scale)
    two, own = lax.optimization_barrier((two, own))
    two = lax.optimization_barrier(two.reshape(states, cells))
    one = lax.ppermute(two, "blk", swap)
    mate, kept_there, *sends = call(
        functools.partial(there_tiles, **given),
        [wide, *cut_shapes(2)],
        [*w, *w_mate, two, psi],
        scratch=[pltpu.VMEM(wide.shape, F32)] * 2,
        us=1,
    )
    first = exchange(sends)
    one, mate = lax.optimization_barrier((one, mate))
    kept, *sends = call(
        functools.partial(here_tiles, **given),
        cut_shapes(4),
        [*u, two, one, own, mate],
        scratch=[pltpu.VMEM(tall.shape, F32)] * 2,
        us=1,
    )
    second = exchange(sends)
    first, kept = lax.optimization_barrier((first, kept))
    (back,) = call(add, [shape_of((3, 3, rows, states), BF16)], [kept_there, *first])
    back = shift(back, "blk", 2)
    (out,) = call(
        assemble, [shape_of((3, 5, rows, states), F32)], [kept, *second, back]
    )
    return out


def solution(mesh):
    in_specs = (P("blk", "dx", "dy", None), P("dx", "dy", None), P(None, "dx", "dy", None))
    out_specs = P(None, None, ("blk", "dx", "dy"), None)
    return jax.shard_map(
        on_device, mesh=mesh, in_specs=in_specs, out_specs=out_specs, check_vma=False
    )
```

```python
import functools
import math

import jax
import jax.numpy as jnp
from jax import lax
from jax.experimental import pallas as pl
from jax.experimental.pallas import tpu as pltpu
from jax.sharding import PartitionSpec as P

F32, BF16 = jnp.float32, jnp.bfloat16
VMEM = pl.BlockSpec(memory_space=pltpu.VMEM)
LIMIT = 12 * 1024 * 1024
NT = (((1,), (1,)), ((), ()))
CHUNK = 16


def shape_of(shape, dtype):
    return jax.ShapeDtypeStruct(shape, dtype)


def shift(block, axis, distance):
    count = lax.axis_size(axis)
    return lax.ppermute(block, axis, [((i + distance) % count, i) for i in range(count)])


def both_sides(pair, axis):
    if lax.axis_size(axis) == 2:
        return shift(pair, axis, 1)
    tail, head = jnp.split(pair, 2, axis=1)
    return jnp.concatenate([shift(tail, axis, -1), shift(head, axis, 1)], axis=1)


def exchange(sends):
    nx, ny = lax.axis_size("dx"), lax.axis_size("dy")
    got = []
    for o, piece in reversed(list(enumerate(sends, 1))):
        ox, oy = o // ny, o % ny
        route = [
            (i * ny + j, ((i + ox) % nx) * ny + (j + oy) % ny) for i in range(nx) for j in range(ny)
        ]
        got.append(lax.ppermute(piece, ("dx", "dy"), route))
    return got


def call(body, outs, operands, scratch=(), specs=None, out_specs=None, us=0):
    run = pl.pallas_call(
        body,
        out_shape=outs,
        in_specs=specs or [VMEM] * len(operands),
        out_specs=out_specs or [VMEM] * len(outs),
        scratch_shapes=list(scratch),
        compiler_params=pltpu.CompilerParams(vmem_limit_bytes=LIMIT),
        cost_estimate=pl.CostEstimate(
            flops=0, bytes_accessed=int(us * 3e6), transcendentals=0
        ),
    )
    return list(run(*operands))


def destinations(nx, ny):
    x, y = lax.axis_index("dx"), lax.axis_index("dy")
    return [
        lax.rem(x + ox, nx) * ny + lax.rem(y + oy, ny) for ox in range(nx) for oy in range(ny)
    ]


def thirds(value):
    high = value.astype(BF16).astype(F32)
    middle = (value - high).astype(BF16).astype(F32)
    return high, middle, value - high - middle


def edges(psi, coupling, grad, tail, head, hy, tmp, *, shape):
    wx, wy, wz = shape
    layer, line = wy * wz, wx * wz
    for side, (x, y, hx) in enumerate(((wx - 1, wy - 1, tail), (0, 0, head))):
        to_y = side * (line + wz)
        hx[:, :layer] = psi[:, x * layer : (x + 1) * layer]
        for i in range(wx):
            at = i * layer + y * wz
            hy[:, to_y + i * wz : to_y + (i + 1) * wz] = psi[:, at : at + wz]
        for k in range(3):
            for n, third in enumerate(thirds(coupling[x] * grad[k, x])):
                tmp[(3 * k + n) * wy : (3 * k + n + 1) * wy] = third
        hx[: tmp.shape[0], layer:] = tmp[...].astype(BF16)
        for k in range(3):
            for n, third in enumerate(thirds(coupling[:, y] * grad[k, :, y])):
                tmp[(3 * k + n) * wx : (3 * k + n + 1) * wx] = third
        hy[: tmp.shape[0], to_y + line : to_y + line + wz] = tmp[...].astype(BF16)


def operators(*refs, layers, shape):
    psi, *refs = refs
    outer = len(refs) == 13
    hx = refs[:2]
    hy, coupling, grad, u, w, half, back, ahead, tmp, ex, ey = refs[-11:]
    wx, wy, wz = shape
    layer, line = wy * wz, wx * wz
    states = psi.shape[0]
    half[...] = 0.5 * (coupling[...][None] * grad[...])

    def unpack(ref, at, to, count):
        tmp[...] = ref[: tmp.shape[0], at : at + wz].astype(F32)
        for k in range(3):
            third = [tmp[(3 * k + n) * count : (3 * k + n + 1) * count] for n in range(3)]
            to[k] = 0.5 * (third[0] + third[1] + third[2])

    for side in range(2):
        if outer:
            unpack(hx[side], layer, ex.at[side], wy)
        unpack(hy, side * (line + wz) + line, ey.at[side], wx)
    for k in range(3):
        for x in layers:
            back[k, x] = pltpu.roll(half[k, x], 1, 1)
            ahead[k, x] = pltpu.roll(half[k, x], wz - 1, 1)

    def coeff(k, x, y):
        if x < 0 or x >= wx:
            return ex[int(x >= wx), k, y : y + 1, :]
        if y < 0 or y >= wy:
            return ey[int(y >= wy), k, x : x + 1, :]
        return half[k, x, y : y + 1, :]

    def group(step, _):
        r = pl.ds(pl.multiple_of(step * CHUNK, CHUNK), CHUNK)

        def field(x, y):
            if x < 0 or x >= wx:
                return hx[int(x >= wx)][r, y * wz : (y + 1) * wz].astype(F32)
            if y < 0 or y >= wy:
                at = int(y >= wy) * (line + wz) + x * wz
                return hy[r, at : at + wz].astype(F32)
            at = x * layer + y * wz
            return psi[r, at : at + wz].astype(F32)

        for n, x in enumerate(layers):
            for y in range(wy):
                here = field(x, y)
                xb, xa = field(x - 1, y), field(x + 1, y)
                yb, ya = field(x, y - 1), field(x, y + 1)
                zb, za = pltpu.roll(here, 1, 1), pltpu.roll(here, wz - 1, 1)
                gx, gy, gz = xa - xb, ya - yb, za - zb
                c1, c2, c3 = [coeff(k, x, y) for k in range(3)]
                cols = slice(n * layer + y * wz, n * layer + (y + 1) * wz)

                def put(ref, k, value):
                    place = pl.ds(pl.multiple_of(k * states + step * CHUNK, CHUNK), CHUNK)
                    ref[place, cols] = value.astype(BF16)

                put(u, 0, c2 * gz - c3 * gy)
                put(u, 1, c3 * gx - c1 * gz)
                put(u, 2, c1 * gy - c2 * gx)

                def dx(k):
                    return coeff(k, x + 1, y) * xa - coeff(k, x - 1, y) * xb

                def dy(k):
                    return coeff(k, x, y + 1) * ya - coeff(k, x, y - 1) * yb

                def dz(k):
                    return ahead[k, x, y : y + 1, :] * za - back[k, x, y : y + 1, :] * zb

                put(w, 0, dy(2) - dz(1))
                put(w, 1, dz(0) - dx(2))
                put(w, 2, dx(1) - dy(0))
        return 0

    lax.fori_loop(0, states // CHUNK, group, 0)


def product(fields, panel, layer, flip=False):
    inner, outer = fields
    cells = inner.shape[1] + outer.shape[1]
    total = 0.0
    for a, start, stop in (
        (inner[...], layer, cells - layer),
        (outer[:, :layer], 0, layer),
        (outer[:, layer:], cells - layer, cells),
    ):
        b = panel(slice(start, stop))
        a, b = (b, a) if flip else (a, b)
        total = total + lax.dot_general(a, b, NT, preferred_element_type=F32)
    return total


def stacked(*panels):
    return lambda cols: jnp.concatenate([panel[:, cols] for panel in panels], axis=0)


def own_tiles(*refs, layer, scale):
    u, (psi, own) = refs[:2], refs[2:]
    own[...] = product(u, stacked(psi), layer) * scale


def cut(outs, slots, plane, states):
    rows = states // math.prod(plane)
    for ref, dest in zip(outs, destinations(*plane)):
        for n, slot in enumerate(slots):
            for k in range(3):
                ref[n, k] = slot(k, dest * rows, rows).astype(ref.dtype)


def tall_rows(tile):
    states = tile.shape[0] // 3

    def rows_of(k, start, rows):
        return tile[pl.ds(pl.multiple_of(k * states + start, rows), rows), :]

    return rows_of


def wide_rows(tile):
    states = tile.shape[0]

    def rows_of(k, start, rows):
        cols = slice(k * states, (k + 1) * states)
        return tile[pl.ds(pl.multiple_of(start, rows), rows), cols]

    return rows_of


def either(first, second):
    core = lax.rem(lax.axis_index("blk"), 2)
    return lambda *place: jnp.where(core == 0, first(*place), second(*place))


def there_tiles(*refs, layer, plane, scale):
    w, w_mate, (two, psi, own), refs = refs[:2], refs[2:4], refs[4:7], refs[7:]
    mate, outs, (there, there_mate) = refs[0], refs[1:-2], refs[-2:]
    states = two.shape[0]
    there[...] = product(w, stacked(two), layer, True) * scale
    both = product(w_mate, stacked(two, psi), layer, True) * scale
    there_mate[...], mate[...] = both[:states], both[states:]
    slots = (wide_rows(there), either(tall_rows(own), wide_rows(there_mate)))
    cut(outs, slots, plane, states)


def here_tiles(*refs, layer, plane, scale):
    u, (two, one, own, mate), refs = refs[:2], refs[2:6], refs[6:]
    outs, (here_two, here_one) = refs[:-2], refs[-2:]
    states = two.shape[0]
    both = product(u, stacked(two, one), layer) * scale
    here_two[...], here_one[...] = both[:, :states], both[:, states:]
    slots = (
        tall_rows(here_two), wide_rows(mate), either(tall_rows(here_one), tall_rows(own))
    )
    cut(outs, slots, plane, states)


def total_of(group, n, k):
    total = group[0][n, k]
    for part in group[1:]:
        total = total + part[n, k].astype(F32)
    return total


def add(*refs):
    group, (ours, back) = refs[:-2], refs[-2:]
    core = lax.rem(lax.axis_index("blk"), 2)
    for k in range(3):
        total, other = total_of(group, 0, k), total_of(group, 1, k)
        high = total.astype(BF16)
        ours[k], back[0, k] = other, high
        back[1, k] = jnp.where(core == 0, total - high.astype(F32), other).astype(BF16)


def assemble(*refs):
    group, (ours, back, out) = refs[:-3], refs[-3:]
    core = lax.rem(lax.axis_index("blk"), 2)
    for k in range(3):
        mate, third = total_of(group, 1, k), total_of(group, 2, k)
        first, second = back[0, k].astype(F32), back[1, k].astype(F32)
        out[k, 0] = total_of(group, 0, k)
        out[k, 1] = jnp.where(core == 0, third, mate)
        out[k, 2] = jnp.where(core == 0, ours[k], third)
        out[k, 3] = jnp.where(core == 0, mate, second)
        out[k, 4] = jnp.where(core == 0, first + second, first)


def on_device(orbitals, coupling, pot_grad):
    states, wx, wy, wz = orbitals.shape
    shape = (wx, wy, wz)
    plane = (lax.axis_size("dx"), lax.axis_size("dy"))
    places = math.prod(plane)
    rows = states // places
    layer, line = wy * wz, wx * wz
    cells = wx * layer
    scale = 1.0 / math.sqrt(cells * places)

    swap = [(i, i ^ 1) for i in range(lax.axis_size("blk"))]
    two = shift(orbitals, "blk", -2)
    psi = lax.optimization_barrier(orbitals.reshape(states, cells))

    tmp = pltpu.VMEM((-(-9 * max(wx, wy) // 16) * 16, wz), F32)
    tail, head, hy = call(
        functools.partial(edges, shape=shape),
        [shape_of((states, layer + wz), BF16)] * 2 + [shape_of((states, 2 * (line + wz)), BF16)],
        [psi, coupling, pot_grad],
        scratch=[tmp],
    )
    hx = [shift(tail, "dx", -1), shift(head, "dx", 1)]
    hy = both_sides(hy, "dy")

    coeffs = pltpu.VMEM((3, wx, wy, wz), F32)
    ends = [pltpu.VMEM((2, 3, wy, wz), F32), pltpu.VMEM((2, 3, wx, wz), F32)]
    u, w, w_mate = [], [], []
    for layers, sides in ((range(1, wx - 1), []), ((0, wx - 1), hx)):
        if sides:
            sides, u[0] = lax.optimization_barrier((sides, u[0]))
        field = shape_of((3 * states, len(layers) * layer), BF16)
        results = call(
            functools.partial(operators, layers=layers, shape=shape),
            [field, field],
            [psi, *sides, hy, coupling, pot_grad],
            scratch=[coeffs] * 3 + [tmp, *ends],
        )
        u.append(results[0])
        w.append(results[1])
        w_mate.append(lax.ppermute(w[-1], "blk", swap))
    tall, wide = shape_of((3 * states, states), F32), shape_of((states, 3 * states), F32)
    (own,) = call(
        functools.partial(own_tiles, layer=layer, scale=scale), [tall], [*u, psi]
    )

    def cut_shapes(slots):
        shape = (slots, 3, rows, states)
        return [shape_of(shape, F32)] + [shape_of(shape, BF16)] * (places - 1)

    given = dict(layer=layer, plane=plane, scale=scale)
    two, own = lax.optimization_barrier((two, own))
    two = lax.optimization_barrier(two.reshape(states, cells))
    one = lax.ppermute(two, "blk", swap)
    mate, kept_there, *sends = call(
        functools.partial(there_tiles, **given),
        [wide, *cut_shapes(2)],
        [*w, *w_mate, two, psi, own],
        scratch=[pltpu.VMEM(wide.shape, F32)] * 2,
        us=1,
    )
    first = exchange(sends)
    one, mate = lax.optimization_barrier((one, mate))
    kept, *sends = call(
        functools.partial(here_tiles, **given),
        cut_shapes(3),
        [*u, two, one, own, mate],
        scratch=[pltpu.VMEM(tall.shape, F32)] * 2,
        us=1,
    )
    second = exchange(sends)
    first, kept = lax.optimization_barrier((first, kept))
    small = (3, rows, states)
    ours, back = call(
        add, [shape_of(small, F32), shape_of((2, *small), BF16)], [kept_there, *first]
    )
    back = shift(back, "blk", 2)
    (out,) = call(
        assemble, [shape_of((3, 5, rows, states), F32)], [kept, *second, ours, back]
    )
    return out


def solution(mesh):
    in_specs = (P("blk", "dx", "dy", None), P("dx", "dy", None), P(None, "dx", "dy", None))
    out_specs = P(None, None, ("blk", "dx", "dy"), None)
    return jax.shard_map(
        on_device, mesh=mesh, in_specs=in_specs, out_specs=out_specs, check_vma=False
    )
```

```python
import functools
import math

import jax
import jax.numpy as jnp
from jax import lax
from jax.experimental import pallas as pl
from jax.experimental.pallas import tpu as pltpu
from jax.sharding import PartitionSpec as P

F32, BF16 = jnp.float32, jnp.bfloat16
VMEM = pl.BlockSpec(memory_space=pltpu.VMEM)
ANY = pl.BlockSpec(memory_space=pl.ANY)
LIMIT = 12 * 1024 * 1024
NT = (((1,), (1,)), ((), ()))
CHUNK = 16


def shape_of(shape, dtype):
    return jax.ShapeDtypeStruct(shape, dtype)


def shift(block, axis, distance):
    count = lax.axis_size(axis)
    return lax.ppermute(block, axis, [((i + distance) % count, i) for i in range(count)])


def both_sides(pair, axis):
    if lax.axis_size(axis) == 2:
        return shift(pair, axis, 1)
    tail, head = jnp.split(pair, 2, axis=1)
    return jnp.concatenate([shift(tail, axis, -1), shift(head, axis, 1)], axis=1)


def exchange(sends):
    nx, ny = lax.axis_size("dx"), lax.axis_size("dy")
    got = []
    for o, piece in reversed(list(enumerate(sends, 1))):
        ox, oy = o // ny, o % ny
        route = [
            (i * ny + j, ((i + ox) % nx) * ny + (j + oy) % ny) for i in range(nx) for j in range(ny)
        ]
        got.append(lax.ppermute(piece, ("dx", "dy"), route))
    return got


def call(body, outs, operands, scratch=(), specs=None, out_specs=None, us=0, aliases=None):
    run = pl.pallas_call(
        body,
        out_shape=outs,
        in_specs=specs or [VMEM] * len(operands),
        out_specs=out_specs or [VMEM] * len(outs),
        scratch_shapes=list(scratch),
        input_output_aliases=aliases or {},
        compiler_params=pltpu.CompilerParams(vmem_limit_bytes=LIMIT),
        cost_estimate=pl.CostEstimate(
            flops=0, bytes_accessed=int(us * 3e6), transcendentals=0
        ),
    )
    return list(run(*operands))


def destinations(nx, ny):
    x, y = lax.axis_index("dx"), lax.axis_index("dy")
    return [
        lax.rem(x + ox, nx) * ny + lax.rem(y + oy, ny) for ox in range(nx) for oy in range(ny)
    ]


def thirds(value):
    high = value.astype(BF16).astype(F32)
    middle = (value - high).astype(BF16).astype(F32)
    return high, middle, value - high - middle


def edges(psi, coupling, grad, tail, head, hy, tmp, *, shape):
    wx, wy, wz = shape
    layer, line = wy * wz, wx * wz
    for side, (x, y, hx) in enumerate(((wx - 1, wy - 1, tail), (0, 0, head))):
        to_y = side * (line + wz)
        hx[:, :layer] = psi[:, x * layer : (x + 1) * layer]
        for i in range(wx):
            at = i * layer + y * wz
            hy[:, to_y + i * wz : to_y + (i + 1) * wz] = psi[:, at : at + wz]
        for k in range(3):
            for n, third in enumerate(thirds(coupling[x] * grad[k, x])):
                tmp[(3 * k + n) * wy : (3 * k + n + 1) * wy] = third
        hx[: tmp.shape[0], layer:] = tmp[...].astype(BF16)
        for k in range(3):
            for n, third in enumerate(thirds(coupling[:, y] * grad[k, :, y])):
                tmp[(3 * k + n) * wx : (3 * k + n + 1) * wx] = third
        hy[: tmp.shape[0], to_y + line : to_y + line + wz] = tmp[...].astype(BF16)


def operators(*refs, layers, shape):
    psi, *refs = refs
    outer = len(refs) == 13
    hx = refs[:2]
    hy, coupling, grad, u, w, half, back, ahead, tmp, ex, ey = refs[-11:]
    wx, wy, wz = shape
    layer, line = wy * wz, wx * wz
    states = psi.shape[0]
    half[...] = 0.5 * (coupling[...][None] * grad[...])

    def unpack(ref, at, to, count):
        tmp[...] = ref[: tmp.shape[0], at : at + wz].astype(F32)
        for k in range(3):
            third = [tmp[(3 * k + n) * count : (3 * k + n + 1) * count] for n in range(3)]
            to[k] = 0.5 * (third[0] + third[1] + third[2])

    for side in range(2):
        if outer:
            unpack(hx[side], layer, ex.at[side], wy)
        unpack(hy, side * (line + wz) + line, ey.at[side], wx)
    for k in range(3):
        for x in layers:
            back[k, x] = pltpu.roll(half[k, x], 1, 1)
            ahead[k, x] = pltpu.roll(half[k, x], wz - 1, 1)

    def coeff(k, x, y):
        if x < 0 or x >= wx:
            return ex[int(x >= wx), k, y : y + 1, :]
        if y < 0 or y >= wy:
            return ey[int(y >= wy), k, x : x + 1, :]
        return half[k, x, y : y + 1, :]

    def group(step, _):
        r = pl.ds(pl.multiple_of(step * CHUNK, CHUNK), CHUNK)

        def field(x, y):
            if x < 0 or x >= wx:
                return hx[int(x >= wx)][r, y * wz : (y + 1) * wz].astype(F32)
            if y < 0 or y >= wy:
                at = int(y >= wy) * (line + wz) + x * wz
                return hy[r, at : at + wz].astype(F32)
            at = x * layer + y * wz
            return psi[r, at : at + wz].astype(F32)

        for n, x in enumerate(layers):
            for y in range(wy):
                here = field(x, y)
                xb, xa = field(x - 1, y), field(x + 1, y)
                yb, ya = field(x, y - 1), field(x, y + 1)
                zb, za = pltpu.roll(here, 1, 1), pltpu.roll(here, wz - 1, 1)
                gx, gy, gz = xa - xb, ya - yb, za - zb
                c1, c2, c3 = [coeff(k, x, y) for k in range(3)]
                cols = slice(n * layer + y * wz, n * layer + (y + 1) * wz)

                def put(ref, k, value):
                    place = pl.ds(pl.multiple_of(k * states + step * CHUNK, CHUNK), CHUNK)
                    ref[place, cols] = value.astype(BF16)

                put(u, 0, c2 * gz - c3 * gy)
                put(u, 1, c3 * gx - c1 * gz)
                put(u, 2, c1 * gy - c2 * gx)

                def dx(k):
                    return coeff(k, x + 1, y) * xa - coeff(k, x - 1, y) * xb

                def dy(k):
                    return coeff(k, x, y + 1) * ya - coeff(k, x, y - 1) * yb

                def dz(k):
                    return ahead[k, x, y : y + 1, :] * za - back[k, x, y : y + 1, :] * zb

                put(w, 0, dy(2) - dz(1))
                put(w, 1, dz(0) - dx(2))
                put(w, 2, dx(1) - dy(0))
        return 0

    lax.fori_loop(0, states // CHUNK, group, 0)


def product(fields, panel, layer, flip=False):
    inner, outer = fields
    cells = inner.shape[1] + outer.shape[1]
    total = 0.0
    for a, start, stop in (
        (inner[...], layer, cells - layer),
        (outer[:, :layer], 0, layer),
        (outer[:, layer:], cells - layer, cells),
    ):
        b = panel(slice(start, stop))
        a, b = (b, a) if flip else (a, b)
        total = total + lax.dot_general(a, b, NT, preferred_element_type=F32)
    return total


def stacked(*panels):
    return lambda cols: jnp.concatenate([panel[:, cols] for panel in panels], axis=0)


def own_tiles(*refs, layer, scale):
    u, (psi, own) = refs[:2], refs[2:]
    own[...] = product(u, stacked(psi), layer) * scale


def cut(outs, slots, plane, states):
    rows = states // math.prod(plane)
    for ref, dest in zip(outs, destinations(*plane)):
        for n, slot in enumerate(slots):
            for k in range(3):
                ref[n, k] = slot(k, dest * rows, rows).astype(ref.dtype)


def tall_rows(tile):
    states = tile.shape[0] // 3

    def rows_of(k, start, rows):
        return tile[pl.ds(pl.multiple_of(k * states + start, rows), rows), :]

    return rows_of


def wide_rows(tile):
    states = tile.shape[0]

    def rows_of(k, start, rows):
        cols = slice(k * states, (k + 1) * states)
        return tile[pl.ds(pl.multiple_of(start, rows), rows), cols]

    return rows_of


def either(first, second):
    core = lax.rem(lax.axis_index("blk"), 2)
    return lambda *place: jnp.where(core == 0, first(*place), second(*place))


def there_tiles(*refs, layer, plane, scale):
    w, w_mate, (two, psi, own), refs = refs[:2], refs[2:4], refs[4:7], refs[7:]
    mate, outs, (there, there_mate) = refs[0], refs[1:-2], refs[-2:]
    states = two.shape[0]
    there[...] = product(w, stacked(two), layer, True) * scale
    both = product(w_mate, stacked(two, psi), layer, True) * scale
    there_mate[...], mate[...] = both[:states], both[states:]
    slots = (wide_rows(there), either(tall_rows(own), wide_rows(there_mate)))
    cut(outs, slots, plane, states)


def here_tiles(*refs, layer, plane, scale):
    u, (two, one, own, mate), refs = refs[:2], refs[2:6], refs[6:]
    outs, (here_two, here_one) = refs[:-2], refs[-2:]
    states = two.shape[0]
    both = product(u, stacked(two, one), layer) * scale
    here_two[...], here_one[...] = both[:, :states], both[:, states:]
    slots = (
        tall_rows(here_two), wide_rows(mate), either(tall_rows(here_one), tall_rows(own))
    )
    cut(outs, slots, plane, states)


def total_of(group, n, k):
    total = group[0][n, k]
    for part in group[1:]:
        total = total + part[n, k].astype(F32)
    return total


def add(*refs):
    group, (ours, back) = refs[:-2], refs[-2:]
    core = lax.rem(lax.axis_index("blk"), 2)
    for k in range(3):
        total, other = total_of(group, 0, k), total_of(group, 1, k)
        high = total.astype(BF16)
        ours[k], back[0, k] = other, high
        back[1, k] = jnp.where(core == 0, total - high.astype(F32), other).astype(BF16)


def assemble(*refs):
    group, (ours, out) = refs[:-2], refs[-2:]
    core = lax.rem(lax.axis_index("blk"), 2)
    for k in range(3):
        mate, third = total_of(group, 1, k), total_of(group, 2, k)
        out[k, 0] = total_of(group, 0, k)
        out[k, 1] = jnp.where(core == 0, third, mate)
        out[k, 2] = jnp.where(core == 0, ours[k], third)
        out[k, 3] = mate
        out[k, 4] = mate


def place_back(back, _, out, tiles, sems):
    core = lax.rem(lax.axis_index("blk"), 2)
    copies = [
        pltpu.make_async_copy(tiles.at[n], out.at[:, 4 - n], sems.at[n]) for n in range(2)
    ]
    for k in range(3):
        first, second = back[0, k].astype(F32), back[1, k].astype(F32)
        tiles[0, k] = jnp.where(core == 0, first + second, first)
        tiles[1, k] = second
    copies[0].start()

    @pl.when(core == 1)
    def _():
        copies[1].start()
        copies[1].wait()

    copies[0].wait()


def on_device(orbitals, coupling, pot_grad):
    states, wx, wy, wz = orbitals.shape
    shape = (wx, wy, wz)
    plane = (lax.axis_size("dx"), lax.axis_size("dy"))
    places = math.prod(plane)
    rows = states // places
    layer, line = wy * wz, wx * wz
    cells = wx * layer
    scale = 1.0 / math.sqrt(cells * places)

    swap = [(i, i ^ 1) for i in range(lax.axis_size("blk"))]
    two = shift(orbitals, "blk", -2)
    psi = lax.optimization_barrier(orbitals.reshape(states, cells))

    tmp = pltpu.VMEM((-(-9 * max(wx, wy) // 16) * 16, wz), F32)
    tail, head, hy = call(
        functools.partial(edges, shape=shape),
        [shape_of((states, layer + wz), BF16)] * 2 + [shape_of((states, 2 * (line + wz)), BF16)],
        [psi, coupling, pot_grad],
        scratch=[tmp],
    )
    hx = [shift(tail, "dx", -1), shift(head, "dx", 1)]
    hy = both_sides(hy, "dy")

    coeffs = pltpu.VMEM((3, wx, wy, wz), F32)
    ends = [pltpu.VMEM((2, 3, wy, wz), F32), pltpu.VMEM((2, 3, wx, wz), F32)]
    u, w, w_mate = [], [], []
    for layers, sides in ((range(1, wx - 1), []), ((0, wx - 1), hx)):
        if sides:
            sides, u[0] = lax.optimization_barrier((sides, u[0]))
        field = shape_of((3 * states, len(layers) * layer), BF16)
        results = call(
            functools.partial(operators, layers=layers, shape=shape),
            [field, field],
            [psi, *sides, hy, coupling, pot_grad],
            scratch=[coeffs] * 3 + [tmp, *ends],
        )
        u.append(results[0])
        w.append(results[1])
        w_mate.append(lax.ppermute(w[-1], "blk", swap))
    tall, wide = shape_of((3 * states, states), F32), shape_of((states, 3 * states), F32)
    (own,) = call(
        functools.partial(own_tiles, layer=layer, scale=scale), [tall], [*u, psi]
    )

    def cut_shapes(slots):
        shape = (slots, 3, rows, states)
        return [shape_of(shape, F32)] + [shape_of(shape, BF16)] * (places - 1)

    given = dict(layer=layer, plane=plane, scale=scale)
    two, own = lax.optimization_barrier((two, own))
    two = lax.optimization_barrier(two.reshape(states, cells))
    one = lax.ppermute(two, "blk", swap)
    mate, kept_there, *sends = call(
        functools.partial(there_tiles, **given),
        [wide, *cut_shapes(2)],
        [*w, *w_mate, two, psi, own],
        scratch=[pltpu.VMEM(wide.shape, F32)] * 2,
        us=1,
    )
    first = exchange(sends)
    one, mate = lax.optimization_barrier((one, mate))
    kept, *sends = call(
        functools.partial(here_tiles, **given),
        cut_shapes(3),
        [*u, two, one, own, mate],
        scratch=[pltpu.VMEM(tall.shape, F32)] * 2,
        us=1,
    )
    second = exchange(sends)
    first, kept = lax.optimization_barrier((first, kept))
    small = (3, rows, states)
    ours, back = call(
        add, [shape_of(small, F32), shape_of((2, *small), BF16)], [kept_there, *first]
    )
    back = shift(back, "blk", 2)
    result = shape_of((3, 5, rows, states), F32)
    (out,) = call(assemble, [result], [kept, *second, ours])
    (out,) = call(
        place_back,
        [result],
        [back, out],
        scratch=[pltpu.VMEM((2, *small), F32), pltpu.SemaphoreType.DMA((2,))],
        specs=[VMEM, ANY],
        out_specs=[ANY],
        aliases={1: 0},
    )
    return out


def solution(mesh):
    in_specs = (P("blk", "dx", "dy", None), P("dx", "dy", None), P(None, "dx", "dy", None))
    out_specs = P(None, None, ("blk", "dx", "dy"), None)
    return jax.shard_map(
        on_device, mesh=mesh, in_specs=in_specs, out_specs=out_specs, check_vma=False
    )
```

```python
import functools
import math

import jax
import jax.numpy as jnp
from jax import lax
from jax.experimental import pallas as pl
from jax.experimental.pallas import tpu as pltpu
from jax.sharding import PartitionSpec as P

F32, BF16 = jnp.float32, jnp.bfloat16
VMEM = pl.BlockSpec(memory_space=pltpu.VMEM)
LIMIT = 12 * 1024 * 1024
NT = (((1,), (1,)), ((), ()))
CHUNK = 16


def shape_of(shape, dtype):
    return jax.ShapeDtypeStruct(shape, dtype)


def shift(block, axis, distance):
    count = lax.axis_size(axis)
    return lax.ppermute(block, axis, [((i + distance) % count, i) for i in range(count)])


def both_sides(pair, axis):
    if lax.axis_size(axis) == 2:
        return shift(pair, axis, 1)
    tail, head = jnp.split(pair, 2, axis=1)
    return jnp.concatenate([shift(tail, axis, -1), shift(head, axis, 1)], axis=1)


def exchange(sends):
    nx, ny = lax.axis_size("dx"), lax.axis_size("dy")
    got = []
    for o, piece in reversed(list(enumerate(sends, 1))):
        ox, oy = o // ny, o % ny
        route = [
            (i * ny + j, ((i + ox) % nx) * ny + (j + oy) % ny) for i in range(nx) for j in range(ny)
        ]
        got.append(lax.ppermute(piece, ("dx", "dy"), route))
    return got


def call(body, outs, operands, scratch=(), specs=None, out_specs=None, us=0):
    run = pl.pallas_call(
        body,
        out_shape=outs,
        in_specs=specs or [VMEM] * len(operands),
        out_specs=out_specs or [VMEM] * len(outs),
        scratch_shapes=list(scratch),
        compiler_params=pltpu.CompilerParams(vmem_limit_bytes=LIMIT),
        cost_estimate=pl.CostEstimate(
            flops=0, bytes_accessed=int(us * 3e6), transcendentals=0
        ),
    )
    return list(run(*operands))


def destinations(nx, ny):
    x, y = lax.axis_index("dx"), lax.axis_index("dy")
    return [
        lax.rem(x + ox, nx) * ny + lax.rem(y + oy, ny) for ox in range(nx) for oy in range(ny)
    ]


def thirds(value):
    high = value.astype(BF16).astype(F32)
    middle = (value - high).astype(BF16).astype(F32)
    return high, middle, value - high - middle


def edges(psi, coupling, grad, tail, head, hy, tmp, *, shape):
    wx, wy, wz = shape
    layer, line = wy * wz, wx * wz
    for side, (x, y, hx) in enumerate(((wx - 1, wy - 1, tail), (0, 0, head))):
        to_y = side * (line + wz)
        hx[:, :layer] = psi[:, x * layer : (x + 1) * layer]
        for i in range(wx):
            at = i * layer + y * wz
            hy[:, to_y + i * wz : to_y + (i + 1) * wz] = psi[:, at : at + wz]
        for k in range(3):
            for n, third in enumerate(thirds(coupling[x] * grad[k, x])):
                tmp[(3 * k + n) * wy : (3 * k + n + 1) * wy] = third
        hx[: tmp.shape[0], layer:] = tmp[...].astype(BF16)
        for k in range(3):
            for n, third in enumerate(thirds(coupling[:, y] * grad[k, :, y])):
                tmp[(3 * k + n) * wx : (3 * k + n + 1) * wx] = third
        hy[: tmp.shape[0], to_y + line : to_y + line + wz] = tmp[...].astype(BF16)


def operators(*refs, layers, shape):
    psi, *refs = refs
    outer = len(refs) == 13
    hx = refs[:2]
    hy, coupling, grad, u, w, half, back, ahead, tmp, ex, ey = refs[-11:]
    wx, wy, wz = shape
    layer, line = wy * wz, wx * wz
    states = psi.shape[0]
    half[...] = 0.5 * (coupling[...][None] * grad[...])

    def unpack(ref, at, to, count):
        tmp[...] = ref[: tmp.shape[0], at : at + wz].astype(F32)
        for k in range(3):
            third = [tmp[(3 * k + n) * count : (3 * k + n + 1) * count] for n in range(3)]
            to[k] = 0.5 * (third[0] + third[1] + third[2])

    for side in range(2):
        if outer:
            unpack(hx[side], layer, ex.at[side], wy)
        unpack(hy, side * (line + wz) + line, ey.at[side], wx)
    for k in range(3):
        for x in layers:
            back[k, x] = pltpu.roll(half[k, x], 1, 1)
            ahead[k, x] = pltpu.roll(half[k, x], wz - 1, 1)

    def coeff(k, x, y):
        if x < 0 or x >= wx:
            return ex[int(x >= wx), k, y : y + 1, :]
        if y < 0 or y >= wy:
            return ey[int(y >= wy), k, x : x + 1, :]
        return half[k, x, y : y + 1, :]

    def group(step, _):
        r = pl.ds(pl.multiple_of(step * CHUNK, CHUNK), CHUNK)

        def field(x, y):
            if x < 0 or x >= wx:
                return hx[int(x >= wx)][r, y * wz : (y + 1) * wz].astype(F32)
            if y < 0 or y >= wy:
                at = int(y >= wy) * (line + wz) + x * wz
                return hy[r, at : at + wz].astype(F32)
            at = x * layer + y * wz
            return psi[r, at : at + wz].astype(F32)

        for n, x in enumerate(layers):
            for y in range(wy):
                here = field(x, y)
                xb, xa = field(x - 1, y), field(x + 1, y)
                yb, ya = field(x, y - 1), field(x, y + 1)
                zb, za = pltpu.roll(here, 1, 1), pltpu.roll(here, wz - 1, 1)
                gx, gy, gz = xa - xb, ya - yb, za - zb
                c1, c2, c3 = [coeff(k, x, y) for k in range(3)]
                cols = slice(n * layer + y * wz, n * layer + (y + 1) * wz)

                def put(ref, k, value):
                    place = pl.ds(pl.multiple_of(k * states + step * CHUNK, CHUNK), CHUNK)
                    ref[place, cols] = value.astype(BF16)

                put(u, 0, c2 * gz - c3 * gy)
                put(u, 1, c3 * gx - c1 * gz)
                put(u, 2, c1 * gy - c2 * gx)

                def dx(k):
                    return coeff(k, x + 1, y) * xa - coeff(k, x - 1, y) * xb

                def dy(k):
                    return coeff(k, x, y + 1) * ya - coeff(k, x, y - 1) * yb

                def dz(k):
                    return ahead[k, x, y : y + 1, :] * za - back[k, x, y : y + 1, :] * zb

                put(w, 0, dy(2) - dz(1))
                put(w, 1, dz(0) - dx(2))
                put(w, 2, dx(1) - dy(0))
        return 0

    lax.fori_loop(0, states // CHUNK, group, 0)


def product(fields, panel, layer, flip=False):
    inner, outer = fields
    cells = inner.shape[1] + outer.shape[1]
    total = 0.0
    for a, start, stop in (
        (inner[...], layer, cells - layer),
        (outer[:, :layer], 0, layer),
        (outer[:, layer:], cells - layer, cells),
    ):
        b = panel(slice(start, stop))
        a, b = (b, a) if flip else (a, b)
        total = total + lax.dot_general(a, b, NT, preferred_element_type=F32)
    return total


def stacked(*panels):
    return lambda cols: jnp.concatenate([panel[:, cols] for panel in panels], axis=0)


def own_tiles(*refs, layer, scale):
    u, (psi, own) = refs[:2], refs[2:]
    own[...] = product(u, stacked(psi), layer) * scale


def cut(outs, slots, plane, states):
    rows = states // math.prod(plane)
    for ref, dest in zip(outs, destinations(*plane)):
        for n, slot in enumerate(slots):
            for k in range(3):
                ref[n, k] = slot(k, dest * rows, rows).astype(ref.dtype)


def tall_rows(tile):
    states = tile.shape[0] // 3

    def rows_of(k, start, rows):
        return tile[pl.ds(pl.multiple_of(k * states + start, rows), rows), :]

    return rows_of


def wide_rows(tile):
    states = tile.shape[0]

    def rows_of(k, start, rows):
        cols = slice(k * states, (k + 1) * states)
        return tile[pl.ds(pl.multiple_of(start, rows), rows), cols]

    return rows_of


def either(first, second):
    core = lax.rem(lax.axis_index("blk"), 2)
    return lambda *place: jnp.where(core == 0, first(*place), second(*place))


def there_tiles(*refs, layer, plane, scale):
    w, w_mate, (two, psi, own), refs = refs[:2], refs[2:4], refs[4:7], refs[7:]
    mate, outs, (there, there_mate) = refs[0], refs[1:-2], refs[-2:]
    states = two.shape[0]
    there[...] = product(w, stacked(two), layer, True) * scale
    both = product(w_mate, stacked(two, psi), layer, True) * scale
    there_mate[...], mate[...] = both[:states], both[states:]
    slots = (wide_rows(there), either(tall_rows(own), wide_rows(there_mate)))
    cut(outs, slots, plane, states)


def here_tiles(*refs, layer, plane, scale):
    u, (two, one, own, mate), refs = refs[:2], refs[2:6], refs[6:]
    outs, (here_two, here_one) = refs[:-2], refs[-2:]
    states = two.shape[0]
    both = product(u, stacked(two, one), layer) * scale
    here_two[...], here_one[...] = both[:, :states], both[:, states:]
    slots = (
        tall_rows(here_two), wide_rows(mate), either(tall_rows(here_one), tall_rows(own))
    )
    cut(outs, slots, plane, states)


def total_of(group, n, k):
    total = group[0][n, k]
    for part in group[1:]:
        total = total + part[n, k].astype(F32)
    return total


def add(*refs):
    group, (ours, back) = refs[:-2], refs[-2:]
    core = lax.rem(lax.axis_index("blk"), 2)
    for k in range(3):
        total, other = total_of(group, 0, k), total_of(group, 1, k)
        high = total.astype(BF16)
        ours[k], back[0, k] = other, high
        back[1, k] = jnp.where(core == 0, total - high.astype(F32), other).astype(BF16)


def assemble(*refs):
    group, (ours, back, out, tiles, sems) = refs[:-5], refs[-5:]
    core = lax.rem(lax.axis_index("blk"), 2)
    copies = [
        pltpu.make_async_copy(tiles.at[t], out.at[:, t], sems.at[t]) for t in range(5)
    ]

    def fill(t, value):
        for k in range(3):
            tiles[t, k] = value(k)
        copies[t].start()

    def returned(k):
        first = back[0, k].astype(F32)
        return jnp.where(core == 0, first + back[1, k].astype(F32), first)

    def third(k):
        return total_of(group, 2, k)

    def mate(k):
        return total_of(group, 1, k)

    fill(0, lambda k: total_of(group, 0, k))
    fill(1, lambda k: jnp.where(core == 0, third(k), mate(k)))
    fill(2, lambda k: jnp.where(core == 0, ours[k], third(k)))
    fill(3, lambda k: jnp.where(core == 0, mate(k), back[1, k].astype(F32)))
    fill(4, returned)
    for copy in copies:
        copy.wait()


def on_device(orbitals, coupling, pot_grad):
    states, wx, wy, wz = orbitals.shape
    shape = (wx, wy, wz)
    plane = (lax.axis_size("dx"), lax.axis_size("dy"))
    places = math.prod(plane)
    rows = states // places
    layer, line = wy * wz, wx * wz
    cells = wx * layer
    scale = 1.0 / math.sqrt(cells * places)

    swap = [(i, i ^ 1) for i in range(lax.axis_size("blk"))]
    two = shift(orbitals, "blk", -2)
    psi = lax.optimization_barrier(orbitals.reshape(states, cells))

    tmp = pltpu.VMEM((-(-9 * max(wx, wy) // 16) * 16, wz), F32)
    tail, head, hy = call(
        functools.partial(edges, shape=shape),
        [shape_of((states, layer + wz), BF16)] * 2 + [shape_of((states, 2 * (line + wz)), BF16)],
        [psi, coupling, pot_grad],
        scratch=[tmp],
    )
    hx = [shift(tail, "dx", -1), shift(head, "dx", 1)]
    hy = both_sides(hy, "dy")

    coeffs = pltpu.VMEM((3, wx, wy, wz), F32)
    ends = [pltpu.VMEM((2, 3, wy, wz), F32), pltpu.VMEM((2, 3, wx, wz), F32)]
    u, w, w_mate = [], [], []
    for layers, sides in ((range(1, wx - 1), []), ((0, wx - 1), hx)):
        if sides:
            sides, u[0] = lax.optimization_barrier((sides, u[0]))
        field = shape_of((3 * states, len(layers) * layer), BF16)
        results = call(
            functools.partial(operators, layers=layers, shape=shape),
            [field, field],
            [psi, *sides, hy, coupling, pot_grad],
            scratch=[coeffs] * 3 + [tmp, *ends],
        )
        u.append(results[0])
        w.append(results[1])
        w_mate.append(lax.ppermute(w[-1], "blk", swap))
    tall, wide = shape_of((3 * states, states), F32), shape_of((states, 3 * states), F32)
    (own,) = call(
        functools.partial(own_tiles, layer=layer, scale=scale), [tall], [*u, psi]
    )

    def cut_shapes(slots):
        shape = (slots, 3, rows, states)
        return [shape_of(shape, F32)] + [shape_of(shape, BF16)] * (places - 1)

    given = dict(layer=layer, plane=plane, scale=scale)
    two, own = lax.optimization_barrier((two, own))
    two = lax.optimization_barrier(two.reshape(states, cells))
    one = lax.ppermute(two, "blk", swap)
    mate, kept_there, *sends = call(
        functools.partial(there_tiles, **given),
        [wide, *cut_shapes(2)],
        [*w, *w_mate, two, psi, own],
        scratch=[pltpu.VMEM(wide.shape, F32)] * 2,
        us=1,
    )
    first = exchange(sends)
    one, mate = lax.optimization_barrier((one, mate))
    kept, *sends = call(
        functools.partial(here_tiles, **given),
        cut_shapes(3),
        [*u, two, one, own, mate],
        scratch=[pltpu.VMEM(tall.shape, F32)] * 2,
        us=1,
    )
    second = exchange(sends)
    first, kept = lax.optimization_barrier((first, kept))
    small = (3, rows, states)
    ours, back = call(
        add, [shape_of(small, F32), shape_of((2, *small), BF16)], [kept_there, *first]
    )
    back = shift(back, "blk", 2)
    (out,) = call(
        assemble,
        [shape_of((3, 5, rows, states), F32)],
        [kept, *second, ours, back],
        scratch=[pltpu.VMEM((5, *small), F32), pltpu.SemaphoreType.DMA((5,))],
        out_specs=[pl.BlockSpec(memory_space=pl.ANY)],
    )
    return out


def solution(mesh):
    in_specs = (P("blk", "dx", "dy", None), P("dx", "dy", None), P(None, "dx", "dy", None))
    out_specs = P(None, None, ("blk", "dx", "dy"), None)
    return jax.shard_map(
        on_device, mesh=mesh, in_specs=in_specs, out_specs=out_specs, check_vma=False
    )
```

```python
import functools
import math

import jax
import jax.numpy as jnp
from jax import lax
from jax.experimental import pallas as pl
from jax.experimental.pallas import tpu as pltpu
from jax.sharding import PartitionSpec as P

F32, BF16 = jnp.float32, jnp.bfloat16
VMEM = pl.BlockSpec(memory_space=pltpu.VMEM)
LIMIT = 12 * 1024 * 1024
NT = (((1,), (1,)), ((), ()))
CHUNK = 16


def shape_of(shape, dtype):
    return jax.ShapeDtypeStruct(shape, dtype)


def shift(block, axis, distance):
    count = lax.axis_size(axis)
    return lax.ppermute(block, axis, [((i + distance) % count, i) for i in range(count)])


def both_sides(pair, axis):
    if lax.axis_size(axis) == 2:
        return shift(pair, axis, 1)
    tail, head = jnp.split(pair, 2, axis=1)
    return jnp.concatenate([shift(tail, axis, -1), shift(head, axis, 1)], axis=1)


def exchange(sends):
    nx, ny = lax.axis_size("dx"), lax.axis_size("dy")
    got = []
    for o, piece in reversed(list(enumerate(sends, 1))):
        ox, oy = o // ny, o % ny
        route = [
            (i * ny + j, ((i + ox) % nx) * ny + (j + oy) % ny) for i in range(nx) for j in range(ny)
        ]
        got.append(lax.ppermute(piece, ("dx", "dy"), route))
    return got


def call(body, outs, operands, scratch=(), specs=None, out_specs=None, us=0):
    run = pl.pallas_call(
        body,
        out_shape=outs,
        in_specs=specs or [VMEM] * len(operands),
        out_specs=out_specs or [VMEM] * len(outs),
        scratch_shapes=list(scratch),
        compiler_params=pltpu.CompilerParams(vmem_limit_bytes=LIMIT),
        cost_estimate=pl.CostEstimate(
            flops=0, bytes_accessed=int(us * 3e6), transcendentals=0
        ),
    )
    return list(run(*operands))


def destinations(nx, ny):
    x, y = lax.axis_index("dx"), lax.axis_index("dy")
    return [
        lax.rem(x + ox, nx) * ny + lax.rem(y + oy, ny) for ox in range(nx) for oy in range(ny)
    ]


def thirds(value):
    high = value.astype(BF16).astype(F32)
    middle = (value - high).astype(BF16).astype(F32)
    return high, middle, value - high - middle


def edges(psi, coupling, grad, tail, head, hy, tmp, *, shape):
    wx, wy, wz = shape
    layer, line = wy * wz, wx * wz
    for side, (x, y, hx) in enumerate(((wx - 1, wy - 1, tail), (0, 0, head))):
        to_y = side * (line + wz)
        hx[:, :layer] = psi[:, x * layer : (x + 1) * layer]
        for i in range(wx):
            at = i * layer + y * wz
            hy[:, to_y + i * wz : to_y + (i + 1) * wz] = psi[:, at : at + wz]
        for k in range(3):
            for n, third in enumerate(thirds(coupling[x] * grad[k, x])):
                tmp[(3 * k + n) * wy : (3 * k + n + 1) * wy] = third
        hx[: tmp.shape[0], layer:] = tmp[...].astype(BF16)
        for k in range(3):
            for n, third in enumerate(thirds(coupling[:, y] * grad[k, :, y])):
                tmp[(3 * k + n) * wx : (3 * k + n + 1) * wx] = third
        hy[: tmp.shape[0], to_y + line : to_y + line + wz] = tmp[...].astype(BF16)


def operators(*refs, layers, shape):
    psi, *refs = refs
    outer = len(refs) == 13
    hx = refs[:2]
    hy, coupling, grad, u, w, half, back, ahead, tmp, ex, ey = refs[-11:]
    wx, wy, wz = shape
    layer, line = wy * wz, wx * wz
    states = psi.shape[0]
    half[...] = 0.5 * (coupling[...][None] * grad[...])

    def unpack(ref, at, to, count):
        tmp[...] = ref[: tmp.shape[0], at : at + wz].astype(F32)
        for k in range(3):
            third = [tmp[(3 * k + n) * count : (3 * k + n + 1) * count] for n in range(3)]
            to[k] = 0.5 * (third[0] + third[1] + third[2])

    for side in range(2):
        if outer:
            unpack(hx[side], layer, ex.at[side], wy)
        unpack(hy, side * (line + wz) + line, ey.at[side], wx)
    for k in range(3):
        for x in layers:
            back[k, x] = pltpu.roll(half[k, x], 1, 1)
            ahead[k, x] = pltpu.roll(half[k, x], wz - 1, 1)

    def coeff(k, x, y):
        if x < 0 or x >= wx:
            return ex[int(x >= wx), k, y : y + 1, :]
        if y < 0 or y >= wy:
            return ey[int(y >= wy), k, x : x + 1, :]
        return half[k, x, y : y + 1, :]

    def group(step, _):
        r = pl.ds(pl.multiple_of(step * CHUNK, CHUNK), CHUNK)

        def field(x, y):
            if x < 0 or x >= wx:
                return hx[int(x >= wx)][r, y * wz : (y + 1) * wz].astype(F32)
            if y < 0 or y >= wy:
                at = int(y >= wy) * (line + wz) + x * wz
                return hy[r, at : at + wz].astype(F32)
            at = x * layer + y * wz
            return psi[r, at : at + wz].astype(F32)

        for n, x in enumerate(layers):
            for y in range(wy):
                here = field(x, y)
                xb, xa = field(x - 1, y), field(x + 1, y)
                yb, ya = field(x, y - 1), field(x, y + 1)
                zb, za = pltpu.roll(here, 1, 1), pltpu.roll(here, wz - 1, 1)
                gx, gy, gz = xa - xb, ya - yb, za - zb
                c1, c2, c3 = [coeff(k, x, y) for k in range(3)]
                cols = slice(n * layer + y * wz, n * layer + (y + 1) * wz)

                def put(ref, k, value):
                    place = pl.ds(pl.multiple_of(k * states + step * CHUNK, CHUNK), CHUNK)
                    ref[place, cols] = value.astype(BF16)

                put(u, 0, c2 * gz - c3 * gy)
                put(u, 1, c3 * gx - c1 * gz)
                put(u, 2, c1 * gy - c2 * gx)

                def dx(k):
                    return coeff(k, x + 1, y) * xa - coeff(k, x - 1, y) * xb

                def dy(k):
                    return coeff(k, x, y + 1) * ya - coeff(k, x, y - 1) * yb

                def dz(k):
                    return ahead[k, x, y : y + 1, :] * za - back[k, x, y : y + 1, :] * zb

                put(w, 0, dy(2) - dz(1))
                put(w, 1, dz(0) - dx(2))
                put(w, 2, dx(1) - dy(0))
        return 0

    lax.fori_loop(0, states // CHUNK, group, 0)


def product(fields, panel, layer, flip=False):
    inner, outer = fields
    cells = inner.shape[1] + outer.shape[1]
    total = 0.0
    for a, start, stop in (
        (inner[...], layer, cells - layer),
        (outer[:, :layer], 0, layer),
        (outer[:, layer:], cells - layer, cells),
    ):
        b = panel(slice(start, stop))
        a, b = (b, a) if flip else (a, b)
        total = total + lax.dot_general(a, b, NT, preferred_element_type=F32)
    return total


def stacked(*panels):
    return lambda cols: jnp.concatenate([panel[:, cols] for panel in panels], axis=0)


def own_tiles(*refs, layer, scale):
    u, (psi, own) = refs[:2], refs[2:]
    own[...] = product(u, stacked(psi), layer) * scale


def cut(outs, slots, plane, states):
    rows = states // math.prod(plane)
    for ref, dest in zip(outs, destinations(*plane)):
        for n, slot in enumerate(slots):
            for k in range(3):
                ref[n, k] = slot(k, dest * rows, rows).astype(ref.dtype)


def tall_rows(tile):
    states = tile.shape[0] // 3

    def rows_of(k, start, rows):
        return tile[pl.ds(pl.multiple_of(k * states + start, rows), rows), :]

    return rows_of


def wide_rows(tile):
    states = tile.shape[0]

    def rows_of(k, start, rows):
        cols = slice(k * states, (k + 1) * states)
        return tile[pl.ds(pl.multiple_of(start, rows), rows), cols]

    return rows_of


def either(first, second):
    core = lax.rem(lax.axis_index("blk"), 2)
    return lambda *place: jnp.where(core == 0, first(*place), second(*place))


def there_tiles(*refs, layer, plane, scale):
    w, w_mate, (two, psi, own), refs = refs[:2], refs[2:4], refs[4:7], refs[7:]
    mate, outs, (there, there_mate) = refs[0], refs[1:-2], refs[-2:]
    states, cells = two.shape
    rows = stacked(two, psi)
    sums = [0.0, 0.0, 0.0]
    for part, at, start, stop in (
        (0, 0, layer, cells - layer), (1, 0, 0, layer), (1, layer, cells - layer, cells)
    ):
        cols, both = slice(at, at + stop - start), rows(slice(start, stop))
        ours, theirs = w[part], w_mate[part]
        middle = jnp.concatenate([ours[2 * states :, cols], theirs[:states, cols]], axis=0)
        pairs = (
            (two[:, start:stop], ours[: 2 * states, cols]),
            (both, middle),
            (both, theirs[states:, cols]),
        )
        for n, (a, b) in enumerate(pairs):
            sums[n] = sums[n] + lax.dot_general(a, b, NT, preferred_element_type=F32)
    first, second, third = [total * scale for total in sums]
    there[:, : 2 * states], there[:, 2 * states :] = first, second[:states, :states]
    there_mate[:, :states], there_mate[:, states:] = second[:states, states:], third[:states]
    mate[:, :states], mate[:, states:] = second[states:, states:], third[states:]
    slots = (wide_rows(there), either(tall_rows(own), wide_rows(there_mate)))
    cut(outs, slots, plane, states)


def here_tiles(*refs, layer, plane, scale):
    u, (two, one, own, mate), refs = refs[:2], refs[2:6], refs[6:]
    outs, (here_two, here_one) = refs[:-2], refs[-2:]
    states = two.shape[0]
    both = product(u, stacked(two, one), layer) * scale
    here_two[...], here_one[...] = both[:, :states], both[:, states:]
    slots = (
        tall_rows(here_two), wide_rows(mate), either(tall_rows(here_one), tall_rows(own))
    )
    cut(outs, slots, plane, states)


def total_of(group, n, k):
    total = group[0][n, k]
    for part in group[1:]:
        total = total + part[n, k].astype(F32)
    return total


def add(*refs):
    group, (ours, back) = refs[:-2], refs[-2:]
    core = lax.rem(lax.axis_index("blk"), 2)
    for k in range(3):
        total, other = total_of(group, 0, k), total_of(group, 1, k)
        high = total.astype(BF16)
        ours[k], back[0, k] = other, high
        back[1, k] = jnp.where(core == 0, total - high.astype(F32), other).astype(BF16)


def assemble(*refs):
    group, (ours, back, out) = refs[:-3], refs[-3:]
    core = lax.rem(lax.axis_index("blk"), 2)
    for k in range(3):
        mate, third = total_of(group, 1, k), total_of(group, 2, k)
        first, second = back[0, k].astype(F32), back[1, k].astype(F32)
        out[k, 0] = total_of(group, 0, k)
        out[k, 1] = jnp.where(core == 0, third, mate)
        out[k, 2] = jnp.where(core == 0, ours[k], third)
        out[k, 3] = jnp.where(core == 0, mate, second)
        out[k, 4] = jnp.where(core == 0, first + second, first)


def on_device(orbitals, coupling, pot_grad):
    states, wx, wy, wz = orbitals.shape
    shape = (wx, wy, wz)
    plane = (lax.axis_size("dx"), lax.axis_size("dy"))
    places = math.prod(plane)
    rows = states // places
    layer, line = wy * wz, wx * wz
    cells = wx * layer
    scale = 1.0 / math.sqrt(cells * places)

    swap = [(i, i ^ 1) for i in range(lax.axis_size("blk"))]
    two = shift(orbitals, "blk", -2)
    psi = lax.optimization_barrier(orbitals.reshape(states, cells))

    tmp = pltpu.VMEM((-(-9 * max(wx, wy) // 16) * 16, wz), F32)
    tail, head, hy = call(
        functools.partial(edges, shape=shape),
        [shape_of((states, layer + wz), BF16)] * 2 + [shape_of((states, 2 * (line + wz)), BF16)],
        [psi, coupling, pot_grad],
        scratch=[tmp],
    )
    hx = [shift(tail, "dx", -1), shift(head, "dx", 1)]
    hy = both_sides(hy, "dy")

    coeffs = pltpu.VMEM((3, wx, wy, wz), F32)
    ends = [pltpu.VMEM((2, 3, wy, wz), F32), pltpu.VMEM((2, 3, wx, wz), F32)]
    u, w, w_mate = [], [], []
    for layers, sides in ((range(1, wx - 1), []), ((0, wx - 1), hx)):
        if sides:
            sides, u[0] = lax.optimization_barrier((sides, u[0]))
        field = shape_of((3 * states, len(layers) * layer), BF16)
        results = call(
            functools.partial(operators, layers=layers, shape=shape),
            [field, field],
            [psi, *sides, hy, coupling, pot_grad],
            scratch=[coeffs] * 3 + [tmp, *ends],
        )
        u.append(results[0])
        w.append(results[1])
        w_mate.append(lax.ppermute(w[-1], "blk", swap))
    tall, wide = shape_of((3 * states, states), F32), shape_of((states, 3 * states), F32)
    (own,) = call(
        functools.partial(own_tiles, layer=layer, scale=scale), [tall], [*u, psi]
    )

    def cut_shapes(slots):
        shape = (slots, 3, rows, states)
        return [shape_of(shape, F32)] + [shape_of(shape, BF16)] * (places - 1)

    given = dict(layer=layer, plane=plane, scale=scale)
    two, own = lax.optimization_barrier((two, own))
    two = lax.optimization_barrier(two.reshape(states, cells))
    one = lax.ppermute(two, "blk", swap)
    mate, kept_there, *sends = call(
        functools.partial(there_tiles, **given),
        [wide, *cut_shapes(2)],
        [*w, *w_mate, two, psi, own],
        scratch=[pltpu.VMEM(wide.shape, F32)] * 2,
        us=1,
    )
    first = exchange(sends)
    one, mate = lax.optimization_barrier((one, mate))
    kept, *sends = call(
        functools.partial(here_tiles, **given),
        cut_shapes(3),
        [*u, two, one, own, mate],
        scratch=[pltpu.VMEM(tall.shape, F32)] * 2,
        us=1,
    )
    second = exchange(sends)
    first, kept = lax.optimization_barrier((first, kept))
    small = (3, rows, states)
    ours, back = call(
        add, [shape_of(small, F32), shape_of((2, *small), BF16)], [kept_there, *first]
    )
    back = shift(back, "blk", 2)
    (out,) = call(
        assemble, [shape_of((3, 5, rows, states), F32)], [kept, *second, ours, back]
    )
    return out


def solution(mesh):
    in_specs = (P("blk", "dx", "dy", None), P("dx", "dy", None), P(None, "dx", "dy", None))
    out_specs = P(None, None, ("blk", "dx", "dy"), None)
    return jax.shard_map(
        on_device, mesh=mesh, in_specs=in_specs, out_specs=out_specs, check_vma=False
    )
```

```python
import functools
import math

import jax
import jax.numpy as jnp
from jax import lax
from jax.experimental import pallas as pl
from jax.experimental.pallas import tpu as pltpu
from jax.sharding import PartitionSpec as P

F32, BF16 = jnp.float32, jnp.bfloat16
VMEM = pl.BlockSpec(memory_space=pltpu.VMEM)
LIMIT = 12 * 1024 * 1024
NT = (((1,), (1,)), ((), ()))
CHUNK = 16


def shape_of(shape, dtype):
    return jax.ShapeDtypeStruct(shape, dtype)


def shift(block, axis, distance):
    count = lax.axis_size(axis)
    return lax.ppermute(block, axis, [((i + distance) % count, i) for i in range(count)])


def both_sides(pair, axis):
    if lax.axis_size(axis) == 2:
        return shift(pair, axis, 1)
    tail, head = jnp.split(pair, 2, axis=1)
    return jnp.concatenate([shift(tail, axis, -1), shift(head, axis, 1)], axis=1)


def exchange(sends):
    nx, ny = lax.axis_size("dx"), lax.axis_size("dy")
    got = []
    for o, piece in reversed(list(enumerate(sends, 1))):
        ox, oy = o // ny, o % ny
        route = [
            (i * ny + j, ((i + ox) % nx) * ny + (j + oy) % ny) for i in range(nx) for j in range(ny)
        ]
        got.append(lax.ppermute(piece, ("dx", "dy"), route))
    return got


def call(body, outs, operands, scratch=(), specs=None, out_specs=None, us=0):
    run = pl.pallas_call(
        body,
        out_shape=outs,
        in_specs=specs or [VMEM] * len(operands),
        out_specs=out_specs or [VMEM] * len(outs),
        scratch_shapes=list(scratch),
        compiler_params=pltpu.CompilerParams(vmem_limit_bytes=LIMIT),
        cost_estimate=pl.CostEstimate(
            flops=0, bytes_accessed=int(us * 3e6), transcendentals=0
        ),
    )
    return list(run(*operands))


def destinations(nx, ny):
    x, y = lax.axis_index("dx"), lax.axis_index("dy")
    return [
        lax.rem(x + ox, nx) * ny + lax.rem(y + oy, ny) for ox in range(nx) for oy in range(ny)
    ]


def thirds(value):
    high = value.astype(BF16).astype(F32)
    middle = (value - high).astype(BF16).astype(F32)
    return high, middle, value - high - middle


def edges(psi, coupling, grad, tail, head, hy, tmp, *, shape):
    wx, wy, wz = shape
    layer, line = wy * wz, wx * wz
    for side, (x, y, hx) in enumerate(((wx - 1, wy - 1, tail), (0, 0, head))):
        to_y = side * (line + wz)
        hx[:, :layer] = psi[:, x * layer : (x + 1) * layer]
        for i in range(wx):
            at = i * layer + y * wz
            hy[:, to_y + i * wz : to_y + (i + 1) * wz] = psi[:, at : at + wz]
        for k in range(3):
            for n, third in enumerate(thirds(coupling[x] * grad[k, x])):
                tmp[(3 * k + n) * wy : (3 * k + n + 1) * wy] = third
        hx[: tmp.shape[0], layer:] = tmp[...].astype(BF16)
        for k in range(3):
            for n, third in enumerate(thirds(coupling[:, y] * grad[k, :, y])):
                tmp[(3 * k + n) * wx : (3 * k + n + 1) * wx] = third
        hy[: tmp.shape[0], to_y + line : to_y + line + wz] = tmp[...].astype(BF16)


def operators(*refs, layers, shape):
    psi, *refs = refs
    outer = len(refs) == 13
    hx = refs[:2]
    hy, coupling, grad, u, w, half, back, ahead, tmp, ex, ey = refs[-11:]
    wx, wy, wz = shape
    layer, line = wy * wz, wx * wz
    states = psi.shape[0]
    half[...] = 0.5 * (coupling[...][None] * grad[...])

    def unpack(ref, at, to, count):
        tmp[...] = ref[: tmp.shape[0], at : at + wz].astype(F32)
        for k in range(3):
            third = [tmp[(3 * k + n) * count : (3 * k + n + 1) * count] for n in range(3)]
            to[k] = 0.5 * (third[0] + third[1] + third[2])

    for side in range(2):
        if outer:
            unpack(hx[side], layer, ex.at[side], wy)
        unpack(hy, side * (line + wz) + line, ey.at[side], wx)
    for k in range(3):
        for x in layers:
            back[k, x] = pltpu.roll(half[k, x], 1, 1)
            ahead[k, x] = pltpu.roll(half[k, x], wz - 1, 1)

    def coeff(k, x, y):
        if x < 0 or x >= wx:
            return ex[int(x >= wx), k, y : y + 1, :]
        if y < 0 or y >= wy:
            return ey[int(y >= wy), k, x : x + 1, :]
        return half[k, x, y : y + 1, :]

    def group(step, _):
        r = pl.ds(pl.multiple_of(step * CHUNK, CHUNK), CHUNK)

        def field(x, y):
            if x < 0 or x >= wx:
                return hx[int(x >= wx)][r, y * wz : (y + 1) * wz].astype(F32)
            if y < 0 or y >= wy:
                at = int(y >= wy) * (line + wz) + x * wz
                return hy[r, at : at + wz].astype(F32)
            at = x * layer + y * wz
            return psi[r, at : at + wz].astype(F32)

        for n, x in enumerate(layers):
            for y in range(wy):
                here = field(x, y)
                xb, xa = field(x - 1, y), field(x + 1, y)
                yb, ya = field(x, y - 1), field(x, y + 1)
                zb, za = pltpu.roll(here, 1, 1), pltpu.roll(here, wz - 1, 1)
                gx, gy, gz = xa - xb, ya - yb, za - zb
                c1, c2, c3 = [coeff(k, x, y) for k in range(3)]
                cols = slice(n * layer + y * wz, n * layer + (y + 1) * wz)

                def put(ref, k, value):
                    place = pl.ds(pl.multiple_of(k * states + step * CHUNK, CHUNK), CHUNK)
                    ref[place, cols] = value.astype(BF16)

                put(u, 0, c2 * gz - c3 * gy)
                put(u, 1, c3 * gx - c1 * gz)
                put(u, 2, c1 * gy - c2 * gx)

                def dx(k):
                    return coeff(k, x + 1, y) * xa - coeff(k, x - 1, y) * xb

                def dy(k):
                    return coeff(k, x, y + 1) * ya - coeff(k, x, y - 1) * yb

                def dz(k):
                    return ahead[k, x, y : y + 1, :] * za - back[k, x, y : y + 1, :] * zb

                put(w, 0, dy(2) - dz(1))
                put(w, 1, dz(0) - dx(2))
                put(w, 2, dx(1) - dy(0))
        return 0

    lax.fori_loop(0, states // CHUNK, group, 0)


def product(fields, panel, layer, flip=False):
    inner, outer = fields
    cells = inner.shape[1] + outer.shape[1]
    total = 0.0
    for a, start, stop in (
        (inner[...], layer, cells - layer),
        (outer[:, :layer], 0, layer),
        (outer[:, layer:], cells - layer, cells),
    ):
        b = panel(slice(start, stop))
        a, b = (b, a) if flip else (a, b)
        total = total + lax.dot_general(a, b, NT, preferred_element_type=F32)
    return total


def stacked(*panels):
    return lambda cols: jnp.concatenate([panel[:, cols] for panel in panels], axis=0)


def own_tiles(*refs, layer, scale):
    u, (psi, own) = refs[:2], refs[2:]
    own[...] = product(u, stacked(psi), layer) * scale


def cut(outs, slots, plane, states):
    rows = states // math.prod(plane)
    for ref, dest in zip(outs, destinations(*plane)):
        for n, slot in enumerate(slots):
            for k in range(3):
                ref[n, k] = slot(k, dest * rows, rows).astype(ref.dtype)


def tall_rows(tile):
    states = tile.shape[0] // 3

    def rows_of(k, start, rows):
        return tile[pl.ds(pl.multiple_of(k * states + start, rows), rows), :]

    return rows_of


def wide_rows(tile):
    states = tile.shape[0]

    def rows_of(k, start, rows):
        cols = slice(k * states, (k + 1) * states)
        return tile[pl.ds(pl.multiple_of(start, rows), rows), cols]

    return rows_of


def either(first, second):
    core = lax.rem(lax.axis_index("blk"), 2)
    return lambda *place: jnp.where(core == 0, first(*place), second(*place))


def there_tiles(*refs, layer, plane, scale):
    w, w_mate, (two, psi, own), refs = refs[:2], refs[2:4], refs[4:7], refs[7:]
    mate, outs, (there, there_mate) = refs[0], refs[1:-2], refs[-2:]
    states, cells = two.shape
    rows = stacked(two, psi)
    places = ((0, 0, layer, cells - layer), (1, 0, 0, layer), (1, layer, cells - layer, cells))

    def total(pair):
        value = 0.0
        for part, at, start, stop in places:
            a, b = pair(w[part], w_mate[part], slice(at, at + stop - start), slice(start, stop))
            value = value + lax.dot_general(a, b, NT, preferred_element_type=F32)
        return value * scale

    def middle(ours, theirs, cols, panel_cols):
        parts = [ours[2 * states :, cols], theirs[:states, cols]]
        return rows(panel_cols), jnp.concatenate(parts, axis=0)

    there[:, : 2 * states] = total(lambda ours, _, cols, at: (two[:, at], ours[: 2 * states, cols]))
    second = total(middle)
    there[:, 2 * states :] = second[:states, :states]
    there_mate[:, :states], mate[:, :states] = second[:states, states:], second[states:, states:]
    core = lax.rem(lax.axis_index("blk"), 2)

    @pl.when(core == 0)
    def _():
        mate[:, states:] = total(lambda _, theirs, cols, at: (psi[:, at], theirs[states:, cols]))

    @pl.when(core == 1)
    def _():
        third = total(lambda _, theirs, cols, at: (rows(at), theirs[states:, cols]))
        there_mate[:, states:], mate[:, states:] = third[:states], third[states:]

    slots = (wide_rows(there), either(tall_rows(own), wide_rows(there_mate)))
    cut(outs, slots, plane, states)


def here_tiles(*refs, layer, plane, scale):
    u, (two, one, own, mate), refs = refs[:2], refs[2:6], refs[6:]
    outs, (here_two, here_one) = refs[:-2], refs[-2:]
    states = two.shape[0]
    both = product(u, stacked(two, one), layer) * scale
    here_two[...], here_one[...] = both[:, :states], both[:, states:]
    slots = (
        tall_rows(here_two), wide_rows(mate), either(tall_rows(here_one), tall_rows(own))
    )
    cut(outs, slots, plane, states)


def total_of(group, n, k):
    total = group[0][n, k]
    for part in group[1:]:
        total = total + part[n, k].astype(F32)
    return total


def add(*refs):
    group, (ours, back) = refs[:-2], refs[-2:]
    core = lax.rem(lax.axis_index("blk"), 2)
    for k in range(3):
        total, other = total_of(group, 0, k), total_of(group, 1, k)
        high = total.astype(BF16)
        ours[k], back[0, k] = other, high
        back[1, k] = jnp.where(core == 0, total - high.astype(F32), other).astype(BF16)


def assemble(*refs):
    group, (ours, back, out) = refs[:-3], refs[-3:]
    core = lax.rem(lax.axis_index("blk"), 2)
    for k in range(3):
        mate, third = total_of(group, 1, k), total_of(group, 2, k)
        first, second = back[0, k].astype(F32), back[1, k].astype(F32)
        out[k, 0] = total_of(group, 0, k)
        out[k, 1] = jnp.where(core == 0, third, mate)
        out[k, 2] = jnp.where(core == 0, ours[k], third)
        out[k, 3] = jnp.where(core == 0, mate, second)
        out[k, 4] = jnp.where(core == 0, first + second, first)


def on_device(orbitals, coupling, pot_grad):
    states, wx, wy, wz = orbitals.shape
    shape = (wx, wy, wz)
    plane = (lax.axis_size("dx"), lax.axis_size("dy"))
    places = math.prod(plane)
    rows = states // places
    layer, line = wy * wz, wx * wz
    cells = wx * layer
    scale = 1.0 / math.sqrt(cells * places)

    swap = [(i, i ^ 1) for i in range(lax.axis_size("blk"))]
    two = shift(orbitals, "blk", -2)
    psi = lax.optimization_barrier(orbitals.reshape(states, cells))

    tmp = pltpu.VMEM((-(-9 * max(wx, wy) // 16) * 16, wz), F32)
    tail, head, hy = call(
        functools.partial(edges, shape=shape),
        [shape_of((states, layer + wz), BF16)] * 2 + [shape_of((states, 2 * (line + wz)), BF16)],
        [psi, coupling, pot_grad],
        scratch=[tmp],
    )
    hx = [shift(tail, "dx", -1), shift(head, "dx", 1)]
    hy = both_sides(hy, "dy")

    coeffs = pltpu.VMEM((3, wx, wy, wz), F32)
    ends = [pltpu.VMEM((2, 3, wy, wz), F32), pltpu.VMEM((2, 3, wx, wz), F32)]
    u, w, w_mate = [], [], []
    for layers, sides in ((range(1, wx - 1), []), ((0, wx - 1), hx)):
        if sides:
            sides, u[0] = lax.optimization_barrier((sides, u[0]))
        field = shape_of((3 * states, len(layers) * layer), BF16)
        results = call(
            functools.partial(operators, layers=layers, shape=shape),
            [field, field],
            [psi, *sides, hy, coupling, pot_grad],
            scratch=[coeffs] * 3 + [tmp, *ends],
        )
        u.append(results[0])
        w.append(results[1])
        w_mate.append(lax.ppermute(w[-1], "blk", swap))
    tall, wide = shape_of((3 * states, states), F32), shape_of((states, 3 * states), F32)
    (own,) = call(
        functools.partial(own_tiles, layer=layer, scale=scale), [tall], [*u, psi]
    )

    def cut_shapes(slots):
        shape = (slots, 3, rows, states)
        return [shape_of(shape, F32)] + [shape_of(shape, BF16)] * (places - 1)

    given = dict(layer=layer, plane=plane, scale=scale)
    two, own = lax.optimization_barrier((two, own))
    two = lax.optimization_barrier(two.reshape(states, cells))
    one = lax.ppermute(two, "blk", swap)
    mate, kept_there, *sends = call(
        functools.partial(there_tiles, **given),
        [wide, *cut_shapes(2)],
        [*w, *w_mate, two, psi, own],
        scratch=[pltpu.VMEM(wide.shape, F32)] * 2,
        us=1,
    )
    first = exchange(sends)
    one, mate = lax.optimization_barrier((one, mate))
    kept, *sends = call(
        functools.partial(here_tiles, **given),
        cut_shapes(3),
        [*u, two, one, own, mate],
        scratch=[pltpu.VMEM(tall.shape, F32)] * 2,
        us=1,
    )
    second = exchange(sends)
    first, kept = lax.optimization_barrier((first, kept))
    small = (3, rows, states)
    ours, back = call(
        add, [shape_of(small, F32), shape_of((2, *small), BF16)], [kept_there, *first]
    )
    back = shift(back, "blk", 2)
    (out,) = call(
        assemble, [shape_of((3, 5, rows, states), F32)], [kept, *second, ours, back]
    )
    return out


def solution(mesh):
    in_specs = (P("blk", "dx", "dy", None), P("dx", "dy", None), P(None, "dx", "dy", None))
    out_specs = P(None, None, ("blk", "dx", "dy"), None)
    return jax.shard_map(
        on_device, mesh=mesh, in_specs=in_specs, out_specs=out_specs, check_vma=False
    )
```

```python
import functools
import math

import jax
import jax.numpy as jnp
from jax import lax
from jax.experimental import pallas as pl
from jax.experimental.pallas import tpu as pltpu
from jax.sharding import PartitionSpec as P

F32, BF16 = jnp.float32, jnp.bfloat16
VMEM = pl.BlockSpec(memory_space=pltpu.VMEM)
LIMIT = 12 * 1024 * 1024
NT = (((1,), (1,)), ((), ()))
CHUNK = 16


def shape_of(shape, dtype):
    return jax.ShapeDtypeStruct(shape, dtype)


def shift(block, axis, distance):
    count = lax.axis_size(axis)
    return lax.ppermute(block, axis, [((i + distance) % count, i) for i in range(count)])


def both_sides(pair, axis):
    if lax.axis_size(axis) == 2:
        return shift(pair, axis, 1)
    tail, head = jnp.split(pair, 2, axis=1)
    return jnp.concatenate([shift(tail, axis, -1), shift(head, axis, 1)], axis=1)


def exchange(sends):
    nx, ny = lax.axis_size("dx"), lax.axis_size("dy")
    got = []
    for o, piece in reversed(list(enumerate(sends, 1))):
        ox, oy = o // ny, o % ny
        route = [
            (i * ny + j, ((i + ox) % nx) * ny + (j + oy) % ny) for i in range(nx) for j in range(ny)
        ]
        got.append(lax.ppermute(piece, ("dx", "dy"), route))
    return got


def call(body, outs, operands, scratch=(), specs=None, out_specs=None, us=0):
    run = pl.pallas_call(
        body,
        out_shape=outs,
        in_specs=specs or [VMEM] * len(operands),
        out_specs=out_specs or [VMEM] * len(outs),
        scratch_shapes=list(scratch),
        compiler_params=pltpu.CompilerParams(vmem_limit_bytes=LIMIT),
        cost_estimate=pl.CostEstimate(
            flops=0, bytes_accessed=int(us * 3e6), transcendentals=0
        ),
    )
    return list(run(*operands))


def destinations(nx, ny):
    x, y = lax.axis_index("dx"), lax.axis_index("dy")
    return [
        lax.rem(x + ox, nx) * ny + lax.rem(y + oy, ny) for ox in range(nx) for oy in range(ny)
    ]


def thirds(value):
    high = value.astype(BF16).astype(F32)
    middle = (value - high).astype(BF16).astype(F32)
    return high, middle, value - high - middle


def edges(psi, coupling, grad, tail, head, hy, tmp, *, shape):
    wx, wy, wz = shape
    layer, line = wy * wz, wx * wz
    for side, (x, y, hx) in enumerate(((wx - 1, wy - 1, tail), (0, 0, head))):
        to_y = side * (line + wz)
        hx[:, :layer] = psi[:, x * layer : (x + 1) * layer]
        for i in range(wx):
            at = i * layer + y * wz
            hy[:, to_y + i * wz : to_y + (i + 1) * wz] = psi[:, at : at + wz]
        for k in range(3):
            for n, third in enumerate(thirds(coupling[x] * grad[k, x])):
                tmp[(3 * k + n) * wy : (3 * k + n + 1) * wy] = third
        hx[: tmp.shape[0], layer:] = tmp[...].astype(BF16)
        for k in range(3):
            for n, third in enumerate(thirds(coupling[:, y] * grad[k, :, y])):
                tmp[(3 * k + n) * wx : (3 * k + n + 1) * wx] = third
        hy[: tmp.shape[0], to_y + line : to_y + line + wz] = tmp[...].astype(BF16)


def operators(*refs, layers, shape):
    psi, *refs = refs
    outer = len(refs) == 13
    hx = refs[:2]
    hy, coupling, grad, u, w, half, back, ahead, tmp, ex, ey = refs[-11:]
    wx, wy, wz = shape
    layer, line = wy * wz, wx * wz
    states = psi.shape[0]
    half[...] = 0.5 * (coupling[...][None] * grad[...])

    def unpack(ref, at, to, count):
        tmp[...] = ref[: tmp.shape[0], at : at + wz].astype(F32)
        for k in range(3):
            third = [tmp[(3 * k + n) * count : (3 * k + n + 1) * count] for n in range(3)]
            to[k] = 0.5 * (third[0] + third[1] + third[2])

    for side in range(2):
        if outer:
            unpack(hx[side], layer, ex.at[side], wy)
        unpack(hy, side * (line + wz) + line, ey.at[side], wx)
    for k in range(3):
        for x in layers:
            back[k, x] = pltpu.roll(half[k, x], 1, 1)
            ahead[k, x] = pltpu.roll(half[k, x], wz - 1, 1)

    def coeff(k, x, y):
        if x < 0 or x >= wx:
            return ex[int(x >= wx), k, y : y + 1, :]
        if y < 0 or y >= wy:
            return ey[int(y >= wy), k, x : x + 1, :]
        return half[k, x, y : y + 1, :]

    def group(step, _):
        r = pl.ds(pl.multiple_of(step * CHUNK, CHUNK), CHUNK)

        def field(x, y):
            if x < 0 or x >= wx:
                return hx[int(x >= wx)][r, y * wz : (y + 1) * wz].astype(F32)
            if y < 0 or y >= wy:
                at = int(y >= wy) * (line + wz) + x * wz
                return hy[r, at : at + wz].astype(F32)
            at = x * layer + y * wz
            return psi[r, at : at + wz].astype(F32)

        for n, x in enumerate(layers):
            for y in range(wy):
                here = field(x, y)
                xb, xa = field(x - 1, y), field(x + 1, y)
                yb, ya = field(x, y - 1), field(x, y + 1)
                zb, za = pltpu.roll(here, 1, 1), pltpu.roll(here, wz - 1, 1)
                gx, gy, gz = xa - xb, ya - yb, za - zb
                c1, c2, c3 = [coeff(k, x, y) for k in range(3)]
                cols = slice(n * layer + y * wz, n * layer + (y + 1) * wz)

                def put(ref, k, value):
                    place = pl.ds(pl.multiple_of(k * states + step * CHUNK, CHUNK), CHUNK)
                    ref[place, cols] = value.astype(BF16)

                put(u, 0, c2 * gz - c3 * gy)
                put(u, 1, c3 * gx - c1 * gz)
                put(u, 2, c1 * gy - c2 * gx)

                def dx(k):
                    return coeff(k, x + 1, y) * xa - coeff(k, x - 1, y) * xb

                def dy(k):
                    return coeff(k, x, y + 1) * ya - coeff(k, x, y - 1) * yb

                def dz(k):
                    return ahead[k, x, y : y + 1, :] * za - back[k, x, y : y + 1, :] * zb

                put(w, 0, dy(2) - dz(1))
                put(w, 1, dz(0) - dx(2))
                put(w, 2, dx(1) - dy(0))
        return 0

    lax.fori_loop(0, states // CHUNK, group, 0)


def product(fields, panel, layer, flip=False):
    inner, outer = fields
    cells = inner.shape[1] + outer.shape[1]
    total = 0.0
    for a, start, stop in (
        (inner[...], layer, cells - layer),
        (outer[:, :layer], 0, layer),
        (outer[:, layer:], cells - layer, cells),
    ):
        b = panel(slice(start, stop))
        a, b = (b, a) if flip else (a, b)
        total = total + lax.dot_general(a, b, NT, preferred_element_type=F32)
    return total


def stacked(*panels):
    return lambda cols: jnp.concatenate([panel[:, cols] for panel in panels], axis=0)


def own_tiles(*refs, layer, scale):
    u, (psi, own) = refs[:2], refs[2:]
    own[...] = product(u, stacked(psi), layer) * scale


def cut(outs, slots, plane, states):
    rows = states // math.prod(plane)
    for ref, dest in zip(outs, destinations(*plane)):
        for n, slot in enumerate(slots):
            for k in range(3):
                ref[n, k] = slot(k, dest * rows, rows).astype(ref.dtype)


def tall_rows(tile):
    states = tile.shape[0] // 3

    def rows_of(k, start, rows):
        return tile[pl.ds(pl.multiple_of(k * states + start, rows), rows), :]

    return rows_of


def wide_rows(tile):
    states = tile.shape[0]

    def rows_of(k, start, rows):
        cols = slice(k * states, (k + 1) * states)
        return tile[pl.ds(pl.multiple_of(start, rows), rows), cols]

    return rows_of


def either(first, second):
    core = lax.rem(lax.axis_index("blk"), 2)
    return lambda *place: jnp.where(core == 0, first(*place), second(*place))


def there_tiles(*refs, layer, plane, scale):
    w, w_mate, (two, psi, own), refs = refs[:2], refs[2:4], refs[4:7], refs[7:]
    mate, outs, (there, there_mate) = refs[0], refs[1:-2], refs[-2:]
    states, cells = two.shape
    rows = stacked(two, psi)
    sums = [0.0, 0.0, 0.0]
    ends = [(1, 0, 0), (1, layer, cells - layer)]
    for part, at, start in [(0, n, n + layer) for n in range(0, cells - 2 * layer, layer)] + ends:
        stop = start + layer
        cols, both = slice(at, at + layer), rows(slice(start, stop))
        ours, theirs = w[part], w_mate[part]
        middle = jnp.concatenate([ours[2 * states :, cols], theirs[:states, cols]], axis=0)
        pairs = (
            (two[:, start:stop], ours[: 2 * states, cols]),
            (both, middle),
            (both, theirs[states:, cols]),
        )
        for n, (a, b) in enumerate(pairs):
            sums[n] = sums[n] + lax.dot_general(a, b, NT, preferred_element_type=F32)
    first, second, third = [total * scale for total in sums]
    there[:, : 2 * states], there[:, 2 * states :] = first, second[:states, :states]
    there_mate[:, :states], there_mate[:, states:] = second[:states, states:], third[:states]
    mate[:, :states], mate[:, states:] = second[states:, states:], third[states:]
    slots = (wide_rows(there), either(tall_rows(own), wide_rows(there_mate)))
    cut(outs, slots, plane, states)


def here_tiles(*refs, layer, plane, scale):
    u, (two, one, own, mate), refs = refs[:2], refs[2:6], refs[6:]
    outs, (here_two, here_one) = refs[:-2], refs[-2:]
    states = two.shape[0]
    both = product(u, stacked(two, one), layer) * scale
    here_two[...], here_one[...] = both[:, :states], both[:, states:]
    slots = (
        tall_rows(here_two), wide_rows(mate), either(tall_rows(here_one), tall_rows(own))
    )
    cut(outs, slots, plane, states)


def total_of(group, n, k):
    total = group[0][n, k]
    for part in group[1:]:
        total = total + part[n, k].astype(F32)
    return total


def add(*refs):
    group, (ours, back) = refs[:-2], refs[-2:]
    core = lax.rem(lax.axis_index("blk"), 2)
    for k in range(3):
        total, other = total_of(group, 0, k), total_of(group, 1, k)
        high = total.astype(BF16)
        ours[k], back[0, k] = other, high
        back[1, k] = jnp.where(core == 0, total - high.astype(F32), other).astype(BF16)


def assemble(*refs):
    group, (ours, back, out) = refs[:-3], refs[-3:]
    core = lax.rem(lax.axis_index("blk"), 2)
    for k in range(3):
        mate, third = total_of(group, 1, k), total_of(group, 2, k)
        first, second = back[0, k].astype(F32), back[1, k].astype(F32)
        out[k, 0] = total_of(group, 0, k)
        out[k, 1] = jnp.where(core == 0, third, mate)
        out[k, 2] = jnp.where(core == 0, ours[k], third)
        out[k, 3] = jnp.where(core == 0, mate, second)
        out[k, 4] = jnp.where(core == 0, first + second, first)


def on_device(orbitals, coupling, pot_grad):
    states, wx, wy, wz = orbitals.shape
    shape = (wx, wy, wz)
    plane = (lax.axis_size("dx"), lax.axis_size("dy"))
    places = math.prod(plane)
    rows = states // places
    layer, line = wy * wz, wx * wz
    cells = wx * layer
    scale = 1.0 / math.sqrt(cells * places)

    swap = [(i, i ^ 1) for i in range(lax.axis_size("blk"))]
    two = shift(orbitals, "blk", -2)
    psi = lax.optimization_barrier(orbitals.reshape(states, cells))

    tmp = pltpu.VMEM((-(-9 * max(wx, wy) // 16) * 16, wz), F32)
    tail, head, hy = call(
        functools.partial(edges, shape=shape),
        [shape_of((states, layer + wz), BF16)] * 2 + [shape_of((states, 2 * (line + wz)), BF16)],
        [psi, coupling, pot_grad],
        scratch=[tmp],
    )
    hx = [shift(tail, "dx", -1), shift(head, "dx", 1)]
    hy = both_sides(hy, "dy")

    coeffs = pltpu.VMEM((3, wx, wy, wz), F32)
    ends = [pltpu.VMEM((2, 3, wy, wz), F32), pltpu.VMEM((2, 3, wx, wz), F32)]
    u, w, w_mate = [], [], []
    for layers, sides in ((range(1, wx - 1), []), ((0, wx - 1), hx)):
        if sides:
            sides, u[0] = lax.optimization_barrier((sides, u[0]))
        field = shape_of((3 * states, len(layers) * layer), BF16)
        results = call(
            functools.partial(operators, layers=layers, shape=shape),
            [field, field],
            [psi, *sides, hy, coupling, pot_grad],
            scratch=[coeffs] * 3 + [tmp, *ends],
        )
        u.append(results[0])
        w.append(results[1])
        w_mate.append(lax.ppermute(w[-1], "blk", swap))
    tall, wide = shape_of((3 * states, states), F32), shape_of((states, 3 * states), F32)
    (own,) = call(
        functools.partial(own_tiles, layer=layer, scale=scale), [tall], [*u, psi]
    )

    def cut_shapes(slots):
        shape = (slots, 3, rows, states)
        return [shape_of(shape, F32)] + [shape_of(shape, BF16)] * (places - 1)

    given = dict(layer=layer, plane=plane, scale=scale)
    two, own = lax.optimization_barrier((two, own))
    two = lax.optimization_barrier(two.reshape(states, cells))
    one = lax.ppermute(two, "blk", swap)
    mate, kept_there, *sends = call(
        functools.partial(there_tiles, **given),
        [wide, *cut_shapes(2)],
        [*w, *w_mate, two, psi, own],
        scratch=[pltpu.VMEM(wide.shape, F32)] * 2,
        us=1,
    )
    first = exchange(sends)
    one, mate = lax.optimization_barrier((one, mate))
    kept, *sends = call(
        functools.partial(here_tiles, **given),
        cut_shapes(3),
        [*u, two, one, own, mate],
        scratch=[pltpu.VMEM(tall.shape, F32)] * 2,
        us=1,
    )
    second = exchange(sends)
    first, kept = lax.optimization_barrier((first, kept))
    small = (3, rows, states)
    ours, back = call(
        add, [shape_of(small, F32), shape_of((2, *small), BF16)], [kept_there, *first]
    )
    back = shift(back, "blk", 2)
    (out,) = call(
        assemble, [shape_of((3, 5, rows, states), F32)], [kept, *second, ours, back]
    )
    return out


def solution(mesh):
    in_specs = (P("blk", "dx", "dy", None), P("dx", "dy", None), P(None, "dx", "dy", None))
    out_specs = P(None, None, ("blk", "dx", "dy"), None)
    return jax.shard_map(
        on_device, mesh=mesh, in_specs=in_specs, out_specs=out_specs, check_vma=False
    )
```

```python
import functools
import math

import jax
import jax.numpy as jnp
from jax import lax
from jax.experimental import pallas as pl
from jax.experimental.pallas import tpu as pltpu
from jax.sharding import PartitionSpec as P

F32, BF16 = jnp.float32, jnp.bfloat16
VMEM = pl.BlockSpec(memory_space=pltpu.VMEM)
LIMIT = 12 * 1024 * 1024
NT = (((1,), (1,)), ((), ()))
CHUNK = 16


def shape_of(shape, dtype):
    return jax.ShapeDtypeStruct(shape, dtype)


def shift(block, axis, distance):
    count = lax.axis_size(axis)
    return lax.ppermute(block, axis, [((i + distance) % count, i) for i in range(count)])


def both_sides(pair, axis):
    if lax.axis_size(axis) == 2:
        return shift(pair, axis, 1)
    tail, head = jnp.split(pair, 2, axis=1)
    return jnp.concatenate([shift(tail, axis, -1), shift(head, axis, 1)], axis=1)


def exchange(sends):
    nx, ny = lax.axis_size("dx"), lax.axis_size("dy")
    got = []
    pieces = list(enumerate(sends, 1))
    for o, piece in pieces[-1:] + pieces[:-1]:
        ox, oy = o // ny, o % ny
        route = [
            (i * ny + j, ((i + ox) % nx) * ny + (j + oy) % ny) for i in range(nx) for j in range(ny)
        ]
        got.append(lax.ppermute(piece, ("dx", "dy"), route))
    return got


def call(body, outs, operands, scratch=(), specs=None, out_specs=None, us=0):
    run = pl.pallas_call(
        body,
        out_shape=outs,
        in_specs=specs or [VMEM] * len(operands),
        out_specs=out_specs or [VMEM] * len(outs),
        scratch_shapes=list(scratch),
        compiler_params=pltpu.CompilerParams(vmem_limit_bytes=LIMIT),
        cost_estimate=pl.CostEstimate(
            flops=0, bytes_accessed=int(us * 3e6), transcendentals=0
        ),
    )
    return list(run(*operands))


def destinations(nx, ny):
    x, y = lax.axis_index("dx"), lax.axis_index("dy")
    return [
        lax.rem(x + ox, nx) * ny + lax.rem(y + oy, ny) for ox in range(nx) for oy in range(ny)
    ]


def thirds(value):
    high = value.astype(BF16).astype(F32)
    middle = (value - high).astype(BF16).astype(F32)
    return high, middle, value - high - middle


def edges(psi, coupling, grad, tail, head, hy, tmp, *, shape):
    wx, wy, wz = shape
    layer, line = wy * wz, wx * wz
    for side, (x, y, hx) in enumerate(((wx - 1, wy - 1, tail), (0, 0, head))):
        to_y = side * (line + wz)
        hx[:, :layer] = psi[:, x * layer : (x + 1) * layer]
        for i in range(wx):
            at = i * layer + y * wz
            hy[:, to_y + i * wz : to_y + (i + 1) * wz] = psi[:, at : at + wz]
        for k in range(3):
            for n, third in enumerate(thirds(coupling[x] * grad[k, x])):
                tmp[(3 * k + n) * wy : (3 * k + n + 1) * wy] = third
        hx[: tmp.shape[0], layer:] = tmp[...].astype(BF16)
        for k in range(3):
            for n, third in enumerate(thirds(coupling[:, y] * grad[k, :, y])):
                tmp[(3 * k + n) * wx : (3 * k + n + 1) * wx] = third
        hy[: tmp.shape[0], to_y + line : to_y + line + wz] = tmp[...].astype(BF16)


def operators(*refs, layers, shape):
    psi, *refs = refs
    outer = len(refs) == 13
    hx = refs[:2]
    hy, coupling, grad, u, w, half, back, ahead, tmp, ex, ey = refs[-11:]
    wx, wy, wz = shape
    layer, line = wy * wz, wx * wz
    states = psi.shape[0]
    half[...] = 0.5 * (coupling[...][None] * grad[...])

    def unpack(ref, at, to, count):
        tmp[...] = ref[: tmp.shape[0], at : at + wz].astype(F32)
        for k in range(3):
            third = [tmp[(3 * k + n) * count : (3 * k + n + 1) * count] for n in range(3)]
            to[k] = 0.5 * (third[0] + third[1] + third[2])

    for side in range(2):
        if outer:
            unpack(hx[side], layer, ex.at[side], wy)
        unpack(hy, side * (line + wz) + line, ey.at[side], wx)
    for k in range(3):
        for x in layers:
            back[k, x] = pltpu.roll(half[k, x], 1, 1)
            ahead[k, x] = pltpu.roll(half[k, x], wz - 1, 1)

    def coeff(k, x, y):
        if x < 0 or x >= wx:
            return ex[int(x >= wx), k, y : y + 1, :]
        if y < 0 or y >= wy:
            return ey[int(y >= wy), k, x : x + 1, :]
        return half[k, x, y : y + 1, :]

    def group(step, _):
        r = pl.ds(pl.multiple_of(step * CHUNK, CHUNK), CHUNK)

        def field(x, y):
            if x < 0 or x >= wx:
                return hx[int(x >= wx)][r, y * wz : (y + 1) * wz].astype(F32)
            if y < 0 or y >= wy:
                at = int(y >= wy) * (line + wz) + x * wz
                return hy[r, at : at + wz].astype(F32)
            at = x * layer + y * wz
            return psi[r, at : at + wz].astype(F32)

        for n, x in enumerate(layers):
            for y in range(wy):
                here = field(x, y)
                xb, xa = field(x - 1, y), field(x + 1, y)
                yb, ya = field(x, y - 1), field(x, y + 1)
                zb, za = pltpu.roll(here, 1, 1), pltpu.roll(here, wz - 1, 1)
                gx, gy, gz = xa - xb, ya - yb, za - zb
                c1, c2, c3 = [coeff(k, x, y) for k in range(3)]
                cols = slice(n * layer + y * wz, n * layer + (y + 1) * wz)

                def put(ref, k, value):
                    place = pl.ds(pl.multiple_of(k * states + step * CHUNK, CHUNK), CHUNK)
                    ref[place, cols] = value.astype(BF16)

                put(u, 0, c2 * gz - c3 * gy)
                put(u, 1, c3 * gx - c1 * gz)
                put(u, 2, c1 * gy - c2 * gx)

                def dx(k):
                    return coeff(k, x + 1, y) * xa - coeff(k, x - 1, y) * xb

                def dy(k):
                    return coeff(k, x, y + 1) * ya - coeff(k, x, y - 1) * yb

                def dz(k):
                    return ahead[k, x, y : y + 1, :] * za - back[k, x, y : y + 1, :] * zb

                put(w, 0, dy(2) - dz(1))
                put(w, 1, dz(0) - dx(2))
                put(w, 2, dx(1) - dy(0))
        return 0

    lax.fori_loop(0, states // CHUNK, group, 0)


def product(fields, panel, layer, flip=False):
    inner, outer = fields
    cells = inner.shape[1] + outer.shape[1]
    total = 0.0
    for a, start, stop in (
        (inner[...], layer, cells - layer),
        (outer[:, :layer], 0, layer),
        (outer[:, layer:], cells - layer, cells),
    ):
        b = panel(slice(start, stop))
        a, b = (b, a) if flip else (a, b)
        total = total + lax.dot_general(a, b, NT, preferred_element_type=F32)
    return total


def stacked(*panels):
    return lambda cols: jnp.concatenate([panel[:, cols] for panel in panels], axis=0)


def own_tiles(*refs, layer, scale):
    u, (psi, own) = refs[:2], refs[2:]
    own[...] = product(u, stacked(psi), layer) * scale


def cut(outs, slots, plane, states):
    rows = states // math.prod(plane)
    for ref, dest in zip(outs, destinations(*plane)):
        for n, slot in enumerate(slots):
            for k in range(3):
                ref[n, k] = slot(k, dest * rows, rows).astype(ref.dtype)


def tall_rows(tile):
    states = tile.shape[0] // 3

    def rows_of(k, start, rows):
        return tile[pl.ds(pl.multiple_of(k * states + start, rows), rows), :]

    return rows_of


def wide_rows(tile):
    states = tile.shape[0]

    def rows_of(k, start, rows):
        cols = slice(k * states, (k + 1) * states)
        return tile[pl.ds(pl.multiple_of(start, rows), rows), cols]

    return rows_of


def either(first, second):
    core = lax.rem(lax.axis_index("blk"), 2)
    return lambda *place: jnp.where(core == 0, first(*place), second(*place))


def there_tiles(*refs, layer, plane, scale):
    w, w_mate, (two, psi, own), refs = refs[:2], refs[2:4], refs[4:7], refs[7:]
    mate, outs, (there, there_mate) = refs[0], refs[1:-2], refs[-2:]
    states, cells = two.shape
    rows = stacked(two, psi)
    sums = [0.0, 0.0, 0.0]
    ends = [(1, 0, 0), (1, layer, cells - layer)]
    for part, at, start in [(0, n, n + layer) for n in range(0, cells - 2 * layer, layer)] + ends:
        stop = start + layer
        cols, both = slice(at, at + layer), rows(slice(start, stop))
        ours, theirs = w[part], w_mate[part]
        middle = jnp.concatenate([ours[2 * states :, cols], theirs[:states, cols]], axis=0)
        pairs = (
            (two[:, start:stop], ours[: 2 * states, cols]),
            (both, middle),
            (both, theirs[states:, cols]),
        )
        for n, (a, b) in enumerate(pairs):
            sums[n] = sums[n] + lax.dot_general(a, b, NT, preferred_element_type=F32)
    first, second, third = [total * scale for total in sums]
    there[:, : 2 * states], there[:, 2 * states :] = first, second[:states, :states]
    there_mate[:, :states], there_mate[:, states:] = second[:states, states:], third[:states]
    mate[:, :states], mate[:, states:] = second[states:, states:], third[states:]
    slots = (wide_rows(there), either(tall_rows(own), wide_rows(there_mate)))
    cut(outs, slots, plane, states)


def here_tiles(*refs, layer, plane, scale):
    u, (two, one, own, mate), refs = refs[:2], refs[2:6], refs[6:]
    outs, (here_two, here_one) = refs[:-2], refs[-2:]
    states = two.shape[0]
    both = product(u, stacked(two, one), layer) * scale
    here_two[...], here_one[...] = both[:, :states], both[:, states:]
    slots = (
        tall_rows(here_two), wide_rows(mate), either(tall_rows(here_one), tall_rows(own))
    )
    cut(outs, slots, plane, states)


def total_of(group, n, k):
    total = group[0][n, k]
    for part in group[1:]:
        total = total + part[n, k].astype(F32)
    return total


def add(*refs):
    group, (ours, back) = refs[:-2], refs[-2:]
    core = lax.rem(lax.axis_index("blk"), 2)
    for k in range(3):
        total, other = total_of(group, 0, k), total_of(group, 1, k)
        high = total.astype(BF16)
        ours[k], back[0, k] = other, high
        back[1, k] = jnp.where(core == 0, total - high.astype(F32), other).astype(BF16)


def assemble(*refs):
    group, (ours, back, out) = refs[:-3], refs[-3:]
    core = lax.rem(lax.axis_index("blk"), 2)
    for k in range(3):
        mate, third = total_of(group, 1, k), total_of(group, 2, k)
        first, second = back[0, k].astype(F32), back[1, k].astype(F32)
        out[k, 0] = total_of(group, 0, k)
        out[k, 1] = jnp.where(core == 0, third, mate)
        out[k, 2] = jnp.where(core == 0, ours[k], third)
        out[k, 3] = jnp.where(core == 0, mate, second)
        out[k, 4] = jnp.where(core == 0, first + second, first)


def on_device(orbitals, coupling, pot_grad):
    states, wx, wy, wz = orbitals.shape
    shape = (wx, wy, wz)
    plane = (lax.axis_size("dx"), lax.axis_size("dy"))
    places = math.prod(plane)
    rows = states // places
    layer, line = wy * wz, wx * wz
    cells = wx * layer
    scale = 1.0 / math.sqrt(cells * places)

    swap = [(i, i ^ 1) for i in range(lax.axis_size("blk"))]
    two = shift(orbitals, "blk", -2)
    psi = lax.optimization_barrier(orbitals.reshape(states, cells))

    tmp = pltpu.VMEM((-(-9 * max(wx, wy) // 16) * 16, wz), F32)
    tail, head, hy = call(
        functools.partial(edges, shape=shape),
        [shape_of((states, layer + wz), BF16)] * 2 + [shape_of((states, 2 * (line + wz)), BF16)],
        [psi, coupling, pot_grad],
        scratch=[tmp],
    )
    hx = [shift(tail, "dx", -1), shift(head, "dx", 1)]
    hy = both_sides(hy, "dy")

    coeffs = pltpu.VMEM((3, wx, wy, wz), F32)
    ends = [pltpu.VMEM((2, 3, wy, wz), F32), pltpu.VMEM((2, 3, wx, wz), F32)]
    u, w, w_mate = [], [], []
    for layers, sides in ((range(1, wx - 1), []), ((0, wx - 1), hx)):
        if sides:
            sides, u[0] = lax.optimization_barrier((sides, u[0]))
        field = shape_of((3 * states, len(layers) * layer), BF16)
        results = call(
            functools.partial(operators, layers=layers, shape=shape),
            [field, field],
            [psi, *sides, hy, coupling, pot_grad],
            scratch=[coeffs] * 3 + [tmp, *ends],
        )
        u.append(results[0])
        w.append(results[1])
        w_mate.append(lax.ppermute(w[-1], "blk", swap))
    tall, wide = shape_of((3 * states, states), F32), shape_of((states, 3 * states), F32)
    (own,) = call(
        functools.partial(own_tiles, layer=layer, scale=scale), [tall], [*u, psi]
    )

    def cut_shapes(slots):
        shape = (slots, 3, rows, states)
        return [shape_of(shape, F32)] + [shape_of(shape, BF16)] * (places - 1)

    given = dict(layer=layer, plane=plane, scale=scale)
    two, own = lax.optimization_barrier((two, own))
    two = lax.optimization_barrier(two.reshape(states, cells))
    one = lax.ppermute(two, "blk", swap)
    mate, kept_there, *sends = call(
        functools.partial(there_tiles, **given),
        [wide, *cut_shapes(2)],
        [*w, *w_mate, two, psi, own],
        scratch=[pltpu.VMEM(wide.shape, F32)] * 2,
        us=1,
    )
    first = exchange(sends)
    one, mate = lax.optimization_barrier((one, mate))
    kept, *sends = call(
        functools.partial(here_tiles, **given),
        cut_shapes(3),
        [*u, two, one, own, mate],
        scratch=[pltpu.VMEM(tall.shape, F32)] * 2,
        us=1,
    )
    second = exchange(sends)
    first, kept = lax.optimization_barrier((first, kept))
    small = (3, rows, states)
    ours, back = call(
        add, [shape_of(small, F32), shape_of((2, *small), BF16)], [kept_there, *first]
    )
    back = shift(back, "blk", 2)
    (out,) = call(
        assemble, [shape_of((3, 5, rows, states), F32)], [kept, *second, ours, back]
    )
    return out


def solution(mesh):
    in_specs = (P("blk", "dx", "dy", None), P("dx", "dy", None), P(None, "dx", "dy", None))
    out_specs = P(None, None, ("blk", "dx", "dy"), None)
    return jax.shard_map(
        on_device, mesh=mesh, in_specs=in_specs, out_specs=out_specs, check_vma=False
    )
```

```python
import functools
import math

import jax
import jax.numpy as jnp
from jax import lax
from jax.experimental import pallas as pl
from jax.experimental.pallas import tpu as pltpu
from jax.sharding import PartitionSpec as P

F32, BF16 = jnp.float32, jnp.bfloat16
VMEM = pl.BlockSpec(memory_space=pltpu.VMEM)
LIMIT = 12 * 1024 * 1024
NT = (((1,), (1,)), ((), ()))
CHUNK = 16


def shape_of(shape, dtype):
    return jax.ShapeDtypeStruct(shape, dtype)


def shift(block, axis, distance):
    count = lax.axis_size(axis)
    return lax.ppermute(block, axis, [((i + distance) % count, i) for i in range(count)])


def both_sides(pair, axis):
    if lax.axis_size(axis) == 2:
        return shift(pair, axis, 1)
    tail, head = jnp.split(pair, 2, axis=1)
    return jnp.concatenate([shift(tail, axis, -1), shift(head, axis, 1)], axis=1)


def exchange(sends):
    nx, ny = lax.axis_size("dx"), lax.axis_size("dy")
    got = []
    for o, piece in reversed(list(enumerate(sends, 1))):
        ox, oy = o // ny, o % ny
        route = [
            (i * ny + j, ((i + ox) % nx) * ny + (j + oy) % ny) for i in range(nx) for j in range(ny)
        ]
        got.append(lax.ppermute(piece, ("dx", "dy"), route))
    return got


def call(body, outs, operands, scratch=(), specs=None, out_specs=None, us=0):
    run = pl.pallas_call(
        body,
        out_shape=outs,
        in_specs=specs or [VMEM] * len(operands),
        out_specs=out_specs or [VMEM] * len(outs),
        scratch_shapes=list(scratch),
        compiler_params=pltpu.CompilerParams(vmem_limit_bytes=LIMIT),
        cost_estimate=pl.CostEstimate(
            flops=0, bytes_accessed=int(us * 3e6), transcendentals=0
        ),
    )
    return list(run(*operands))


def destinations(nx, ny):
    x, y = lax.axis_index("dx"), lax.axis_index("dy")
    return [
        lax.rem(x + ox, nx) * ny + lax.rem(y + oy, ny) for ox in range(nx) for oy in range(ny)
    ]


def thirds(value):
    high = value.astype(BF16).astype(F32)
    middle = (value - high).astype(BF16).astype(F32)
    return high, middle, value - high - middle


def edges(psi, coupling, grad, tail, head, hy, tmp, *, shape):
    wx, wy, wz = shape
    layer, line = wy * wz, wx * wz
    for side, (x, y, hx) in enumerate(((wx - 1, wy - 1, tail), (0, 0, head))):
        to_y = side * (line + wz)
        hx[:, :layer] = psi[:, x * layer : (x + 1) * layer]
        for i in range(wx):
            at = i * layer + y * wz
            hy[:, to_y + i * wz : to_y + (i + 1) * wz] = psi[:, at : at + wz]
        for k in range(3):
            for n, third in enumerate(thirds(coupling[x] * grad[k, x])):
                tmp[(3 * k + n) * wy : (3 * k + n + 1) * wy] = third
        hx[: tmp.shape[0], layer:] = tmp[...].astype(BF16)
        for k in range(3):
            for n, third in enumerate(thirds(coupling[:, y] * grad[k, :, y])):
                tmp[(3 * k + n) * wx : (3 * k + n + 1) * wx] = third
        hy[: tmp.shape[0], to_y + line : to_y + line + wz] = tmp[...].astype(BF16)


def operators(*refs, layers, shape):
    psi, *refs = refs
    outer = len(refs) == 13
    hx = refs[:2]
    hy, coupling, grad, u, w, half, back, ahead, tmp, ex, ey = refs[-11:]
    wx, wy, wz = shape
    layer, line = wy * wz, wx * wz
    states = psi.shape[0]
    half[...] = 0.5 * (coupling[...][None] * grad[...])

    def unpack(ref, at, to, count):
        tmp[...] = ref[: tmp.shape[0], at : at + wz].astype(F32)
        for k in range(3):
            third = [tmp[(3 * k + n) * count : (3 * k + n + 1) * count] for n in range(3)]
            to[k] = 0.5 * (third[0] + third[1] + third[2])

    for side in range(2):
        if outer:
            unpack(hx[side], layer, ex.at[side], wy)
        unpack(hy, side * (line + wz) + line, ey.at[side], wx)
    for k in range(3):
        for x in layers:
            back[k, x] = pltpu.roll(half[k, x], 1, 1)
            ahead[k, x] = pltpu.roll(half[k, x], wz - 1, 1)

    def coeff(k, x, y):
        if x < 0 or x >= wx:
            return ex[int(x >= wx), k, y : y + 1, :]
        if y < 0 or y >= wy:
            return ey[int(y >= wy), k, x : x + 1, :]
        return half[k, x, y : y + 1, :]

    def group(step, _):
        r = pl.ds(pl.multiple_of(step * CHUNK, CHUNK), CHUNK)

        def field(x, y):
            if x < 0 or x >= wx:
                return hx[int(x >= wx)][r, y * wz : (y + 1) * wz].astype(F32)
            if y < 0 or y >= wy:
                at = int(y >= wy) * (line + wz) + x * wz
                return hy[r, at : at + wz].astype(F32)
            at = x * layer + y * wz
            return psi[r, at : at + wz].astype(F32)

        for n, x in enumerate(layers):
            for y in range(wy):
                here = field(x, y)
                xb, xa = field(x - 1, y), field(x + 1, y)
                yb, ya = field(x, y - 1), field(x, y + 1)
                zb, za = pltpu.roll(here, 1, 1), pltpu.roll(here, wz - 1, 1)
                gx, gy, gz = xa - xb, ya - yb, za - zb
                c1, c2, c3 = [coeff(k, x, y) for k in range(3)]
                cols = slice(n * layer + y * wz, n * layer + (y + 1) * wz)

                def put(ref, k, value):
                    place = pl.ds(pl.multiple_of(k * states + step * CHUNK, CHUNK), CHUNK)
                    ref[place, cols] = value.astype(BF16)

                put(u, 0, c2 * gz - c3 * gy)
                put(u, 1, c3 * gx - c1 * gz)
                put(u, 2, c1 * gy - c2 * gx)

                def dx(k):
                    return coeff(k, x + 1, y) * xa - coeff(k, x - 1, y) * xb

                def dy(k):
                    return coeff(k, x, y + 1) * ya - coeff(k, x, y - 1) * yb

                def dz(k):
                    return ahead[k, x, y : y + 1, :] * za - back[k, x, y : y + 1, :] * zb

                put(w, 0, dy(2) - dz(1))
                put(w, 1, dz(0) - dx(2))
                put(w, 2, dx(1) - dy(0))
        return 0

    lax.fori_loop(0, states // CHUNK, group, 0)


def product(fields, panel, layer):
    inner, outer = fields
    cells = inner.shape[1] + outer.shape[1]
    total = 0.0
    ends = [(outer, 0, 0), (outer, layer, cells - layer)]
    for a, at, start in [(inner, n, n + layer) for n in range(0, inner.shape[1], layer)] + ends:
        b = panel(slice(start, start + layer))
        total = total + lax.dot_general(a[:, at : at + layer], b, NT, preferred_element_type=F32)
    return total


def stacked(*panels):
    return lambda cols: jnp.concatenate([panel[:, cols] for panel in panels], axis=0)


def own_tiles(*refs, layer, scale):
    u, (psi, own) = refs[:2], refs[2:]
    own[...] = product(u, stacked(psi), layer) * scale


def cut(outs, slots, plane, states):
    rows = states // math.prod(plane)
    for ref, dest in zip(outs, destinations(*plane)):
        for n, slot in enumerate(slots):
            for k in range(3):
                ref[n, k] = slot(k, dest * rows, rows).astype(ref.dtype)


def tall_rows(tile):
    states = tile.shape[0] // 3

    def rows_of(k, start, rows):
        return tile[pl.ds(pl.multiple_of(k * states + start, rows), rows), :]

    return rows_of


def wide_rows(tile):
    states = tile.shape[0]

    def rows_of(k, start, rows):
        cols = slice(k * states, (k + 1) * states)
        return tile[pl.ds(pl.multiple_of(start, rows), rows), cols]

    return rows_of


def either(first, second):
    core = lax.rem(lax.axis_index("blk"), 2)
    return lambda *place: jnp.where(core == 0, first(*place), second(*place))


def there_tiles(*refs, layer, plane, scale):
    w, w_mate, (two, psi, own), refs = refs[:2], refs[2:4], refs[4:7], refs[7:]
    mate, outs, (there, there_mate) = refs[0], refs[1:-2], refs[-2:]
    states, cells = two.shape
    rows = stacked(two, psi)
    sums = [0.0, 0.0, 0.0]
    ends = [(1, 0, 0), (1, layer, cells - layer)]
    for part, at, start in [(0, n, n + layer) for n in range(0, cells - 2 * layer, layer)] + ends:
        stop = start + layer
        cols, both = slice(at, at + layer), rows(slice(start, stop))
        ours, theirs = w[part], w_mate[part]
        middle = jnp.concatenate([ours[2 * states :, cols], theirs[:states, cols]], axis=0)
        pairs = (
            (two[:, start:stop], ours[: 2 * states, cols]),
            (both, middle),
            (both, theirs[states:, cols]),
        )
        for n, (a, b) in enumerate(pairs):
            sums[n] = sums[n] + lax.dot_general(a, b, NT, preferred_element_type=F32)
    first, second, third = [total * scale for total in sums]
    there[:, : 2 * states], there[:, 2 * states :] = first, second[:states, :states]
    there_mate[:, :states], there_mate[:, states:] = second[:states, states:], third[:states]
    mate[:, :states], mate[:, states:] = second[states:, states:], third[states:]
    slots = (wide_rows(there), either(tall_rows(own), wide_rows(there_mate)))
    cut(outs, slots, plane, states)


def here_tiles(*refs, layer, plane, scale):
    u, (two, one, own, mate), refs = refs[:2], refs[2:6], refs[6:]
    outs, (here_two, here_one) = refs[:-2], refs[-2:]
    states = two.shape[0]
    both = product(u, stacked(two, one), layer) * scale
    here_two[...], here_one[...] = both[:, :states], both[:, states:]
    slots = (
        tall_rows(here_two), wide_rows(mate), either(tall_rows(here_one), tall_rows(own))
    )
    cut(outs, slots, plane, states)


def total_of(group, n, k):
    total = group[0][n, k]
    for part in group[1:]:
        total = total + part[n, k].astype(F32)
    return total


def add(*refs):
    group, (ours, back) = refs[:-2], refs[-2:]
    core = lax.rem(lax.axis_index("blk"), 2)
    for k in range(3):
        total, other = total_of(group, 0, k), total_of(group, 1, k)
        high = total.astype(BF16)
        ours[k], back[0, k] = other, high
        back[1, k] = jnp.where(core == 0, total - high.astype(F32), other).astype(BF16)


def assemble(*refs):
    group, (ours, back, out) = refs[:-3], refs[-3:]
    core = lax.rem(lax.axis_index("blk"), 2)
    for k in range(3):
        mate, third = total_of(group, 1, k), total_of(group, 2, k)
        first, second = back[0, k].astype(F32), back[1, k].astype(F32)
        out[k, 0] = total_of(group, 0, k)
        out[k, 1] = jnp.where(core == 0, third, mate)
        out[k, 2] = jnp.where(core == 0, ours[k], third)
        out[k, 3] = jnp.where(core == 0, mate, second)
        out[k, 4] = jnp.where(core == 0, first + second, first)


def on_device(orbitals, coupling, pot_grad):
    states, wx, wy, wz = orbitals.shape
    shape = (wx, wy, wz)
    plane = (lax.axis_size("dx"), lax.axis_size("dy"))
    places = math.prod(plane)
    rows = states // places
    layer, line = wy * wz, wx * wz
    cells = wx * layer
    scale = 1.0 / math.sqrt(cells * places)

    swap = [(i, i ^ 1) for i in range(lax.axis_size("blk"))]
    two = shift(orbitals, "blk", -2)
    psi = lax.optimization_barrier(orbitals.reshape(states, cells))

    tmp = pltpu.VMEM((-(-9 * max(wx, wy) // 16) * 16, wz), F32)
    tail, head, hy = call(
        functools.partial(edges, shape=shape),
        [shape_of((states, layer + wz), BF16)] * 2 + [shape_of((states, 2 * (line + wz)), BF16)],
        [psi, coupling, pot_grad],
        scratch=[tmp],
    )
    hx = [shift(tail, "dx", -1), shift(head, "dx", 1)]
    hy = both_sides(hy, "dy")

    coeffs = pltpu.VMEM((3, wx, wy, wz), F32)
    ends = [pltpu.VMEM((2, 3, wy, wz), F32), pltpu.VMEM((2, 3, wx, wz), F32)]
    u, w, w_mate = [], [], []
    for layers, sides in ((range(1, wx - 1), []), ((0, wx - 1), hx)):
        if sides:
            sides, u[0] = lax.optimization_barrier((sides, u[0]))
        field = shape_of((3 * states, len(layers) * layer), BF16)
        results = call(
            functools.partial(operators, layers=layers, shape=shape),
            [field, field],
            [psi, *sides, hy, coupling, pot_grad],
            scratch=[coeffs] * 3 + [tmp, *ends],
        )
        u.append(results[0])
        w.append(results[1])
        w_mate.append(lax.ppermute(w[-1], "blk", swap))
    tall, wide = shape_of((3 * states, states), F32), shape_of((states, 3 * states), F32)
    (own,) = call(
        functools.partial(own_tiles, layer=layer, scale=scale), [tall], [*u, psi]
    )

    def cut_shapes(slots):
        shape = (slots, 3, rows, states)
        return [shape_of(shape, F32)] + [shape_of(shape, BF16)] * (places - 1)

    given = dict(layer=layer, plane=plane, scale=scale)
    two, own = lax.optimization_barrier((two, own))
    two = lax.optimization_barrier(two.reshape(states, cells))
    one = lax.ppermute(two, "blk", swap)
    mate, kept_there, *sends = call(
        functools.partial(there_tiles, **given),
        [wide, *cut_shapes(2)],
        [*w, *w_mate, two, psi, own],
        scratch=[pltpu.VMEM(wide.shape, F32)] * 2,
        us=1,
    )
    first = exchange(sends)
    one, mate = lax.optimization_barrier((one, mate))
    kept, *sends = call(
        functools.partial(here_tiles, **given),
        cut_shapes(3),
        [*u, two, one, own, mate],
        scratch=[pltpu.VMEM(tall.shape, F32)] * 2,
        us=1,
    )
    second = exchange(sends)
    first, kept = lax.optimization_barrier((first, kept))
    small = (3, rows, states)
    ours, back = call(
        add, [shape_of(small, F32), shape_of((2, *small), BF16)], [kept_there, *first]
    )
    back = shift(back, "blk", 2)
    (out,) = call(
        assemble, [shape_of((3, 5, rows, states), F32)], [kept, *second, ours, back]
    )
    return out


def solution(mesh):
    in_specs = (P("blk", "dx", "dy", None), P("dx", "dy", None), P(None, "dx", "dy", None))
    out_specs = P(None, None, ("blk", "dx", "dy"), None)
    return jax.shard_map(
        on_device, mesh=mesh, in_specs=in_specs, out_specs=out_specs, check_vma=False
    )
```
